32 devices in a mesh: ba: 8 (over z, x), pb: 4 (over y, core).
Axes of the slice: x: 2, y: 2, z: 4, core: 2. Of those that a mesh axis runs over, the one named last changes fastest.
Arguments:
- decoder_input: bfloat16 [64, 100, 512], P('ba', 'pb'), may hold values from -6 to 6
- memory: bfloat16 [64, 1208, 512], P('ba'), may hold values from -6 to 6
- lengths: int32 [64], P('ba'), may hold values from 302 to 1208, as said below
- query_embed: bfloat16 [100, 512], P('pb'), may hold values from -6 to 6
- self_query: bfloat16 [512, 512], replicated, may hold values from -0.25 to 0.25
- self_query_bias: bfloat16 [512], replicated, may hold values from -2 to 2
- self_key: bfloat16 [512, 512], replicated, may hold values from -0.25 to 0.25
- self_value: bfloat16 [512, 512], replicated, may hold values from -0.25 to 0.25
- self_value_bias: bfloat16 [512], replicated, may hold values from -2 to 2
- self_out: bfloat16 [512, 512], replicated, may hold values from -0.75 to 0.75
- self_out_bias: bfloat16 [512], replicated, may hold values from -2 to 2
- norm_one_gain: bfloat16 [512], replicated, may hold values from 0.5 to 1.5
- norm_one_bias: bfloat16 [512], replicated, may hold values from -2 to 2
- cross_query: bfloat16 [512, 512], replicated, may hold values from -0.25 to 0.25
- cross_query_bias: bfloat16 [512], replicated, may hold values from -2 to 2
- cross_key: bfloat16 [512, 512], replicated, may hold values from -0.25 to 0.25
- cross_value: bfloat16 [512, 512], replicated, may hold values from -0.25 to 0.25
- cross_value_bias: bfloat16 [512], replicated, may hold values from -2 to 2
- cross_out: bfloat16 [512, 512], replicated, may hold values from -1 to 1
- cross_out_bias: bfloat16 [512], replicated, may hold values from -2 to 2
- norm_two_gain: bfloat16 [512], replicated, may hold values from 0.5 to 1.5
- norm_two_bias: bfloat16 [512], replicated, may hold values from -2 to 2
- expand_weight: bfloat16 [512, 3200], replicated, may hold values from -0.25 to 0.25
- expand_bias: bfloat16 [3200], replicated, may hold values from -3 to 3
- project_weight: bfloat16 [3200, 512], replicated, may hold values from -0.109375 to 0.109375
- project_bias: bfloat16 [512], replicated, may hold values from -2 to 2
- norm_three_gain: bfloat16 [512], replicated, may hold values from 0.5 to 1.5
- norm_three_bias: bfloat16 [512], replicated, may hold values from -2 to 2
- out_cotangent: bfloat16 [64, 100, 512], P('ba', 'pb'), may hold values from -6 to 6
Outputs:
- layer_output: bfloat16 [64, 100, 512], P('ba', 'pb')
- input_grad: bfloat16 [64, 100, 512], P('ba', 'pb')
- memory_grad: bfloat16 [64, 1208, 512], P('ba', 'pb')
- embed_grad: float32 [100, 512], P('pb', 'ba')
- self_query_grad: float32 [512, 512], P('ba', 'pb')
- self_query_bias_grad: float32 [512], replicated
- self_key_grad: float32 [512, 512], P('ba', 'pb')
- self_value_grad: float32 [512, 512], P('ba', 'pb')
- self_value_bias_grad: float32 [512], replicated
- self_out_grad: float32 [512, 512], P('ba', 'pb')
- self_out_bias_grad: float32 [512], replicated
- norm_one_gain_grad: float32 [512], replicated
- norm_one_bias_grad: float32 [512], replicated
- cross_query_grad: float32 [512, 512], P('ba', 'pb')
- cross_query_bias_grad: float32 [512], replicated
- cross_key_grad: float32 [512, 512], P('ba', 'pb')
- cross_value_grad: float32 [512, 512], P('ba', 'pb')
- cross_value_bias_grad: float32 [512], replicated
- cross_out_grad: float32 [512, 512], P('ba', 'pb')
- cross_out_bias_grad: float32 [512], replicated
- norm_two_gain_grad: float32 [512], replicated
- norm_two_bias_grad: float32 [512], replicated
- expand_weight_grad: float32 [512, 3200], P('ba', 'pb')
- expand_bias_grad: float32 [3200], replicated
- project_weight_grad: float32 [3200, 512], P('pb', 'ba')
- project_bias_grad: float32 [512], replicated
- norm_three_gain_grad: float32 [512], replicated
- norm_three_bias_grad: float32 [512], replicated
The draws below stay inside these ranges and needn't reach their ends.
Inputs may be any that keep to these rules, and one draw needn't show every extreme that they name: `lengths`: every length is 302 or 1208; among the 8 items of each index of ba at least one has 1208.
All inputs are finite; a program needn't handle non-finite values.
Results may differ from the reference program's by a relative error of at most 0.025.
The reference program's roundings to bfloat16 on the way count: a program that leaves them out, or rounds other values in their place, can miss the bound.
Values may be sent and summed in bfloat16 or wider, within the bound.
No kernel may reach another device: no remote copies, remote signals or barrier semaphores. Data moves between devices by JAX's collectives and lax.ppermute only.
A program may use at most 192 MiB of HBM per device.

```python
import math
import jax
import jax.numpy as jnp
from jax import lax

D = 512
HEADS = 8
FF = 3200
MEM = 1208
SHORT = 302
B_DEV = 8
NQ = 100
ITEMS = 64


def draw_lengths(key, part):
    key = jax.random.fold_in(key, 7)
    first_key, second_key = jax.random.split(key)
    longer = jax.random.randint(first_key, (ITEMS,), 0, 2)
    chosen = jax.random.randint(second_key, (ITEMS // B_DEV,), 0, B_DEV)
    forced = jnp.arange(ITEMS, dtype=jnp.int32) % B_DEV == jnp.repeat(chosen, B_DEV)
    longer = jnp.where(forced, 1, longer)
    return jnp.where(longer == 1, MEM, SHORT).astype(jnp.int32)


def block_levels(key, extent, cuts, least, high):
    def one(dim, parts):
        heights = jax.random.uniform(jax.random.fold_in(jax.random.fold_in(key, 6), dim), (parts,), jnp.float32, least / len(cuts), high / len(cuts))
        return jnp.repeat(jnp.exp(heights), extent[dim] // parts).reshape((-1,) + (1,) * (len(extent) - dim - 1))

    factor_of = one(*cuts[0])
    for cut in cuts[1:]:
        factor_of = factor_of * one(*cut)
    return factor_of


def gaussian(own_key, shape, scale, reach, cuts=(), kind=jnp.bfloat16):
    level = block_levels(own_key, shape, cuts, -0.22, 0.18) if cuts else 1.0
    values = jax.random.normal(own_key, shape, jnp.float32) * scale * level
    return jnp.minimum(jnp.maximum(values, -reach), reach).astype(kind)


def setup_inputs(seed: int = 0) -> dict:
    key_list = jax.random.split(jax.random.key(seed), 30)
    return {
        "decoder_input": gaussian(key_list[0], (ITEMS, NQ, D), 1.0, 6.0, ((0, 8), (1, 4))),
        "memory": gaussian(key_list[1], (ITEMS, MEM, D), 1.0, 6.0, ((0, 8),)),
        "lengths": draw_lengths(jax.random.fold_in(key_list[29], 71), 0),
        "query_embed": gaussian(key_list[3], (NQ, D), 1.0, 6.0, ((0, 4),)),
        "self_query": gaussian(key_list[4], (D, D), D ** -0.5, 0.25),
        "self_query_bias": gaussian(key_list[5], (D,), 0.3, 2.0),
        "self_key": gaussian(key_list[6], (D, D), D ** -0.5, 0.25),
        "self_value": gaussian(key_list[7], (D, D), D ** -0.5, 0.25),
        "self_value_bias": gaussian(key_list[8], (D,), 0.3, 2.0),
        "self_out": gaussian(key_list[9], (D, D), (D // 8) ** -0.5, 0.75),
        "self_out_bias": gaussian(key_list[10], (D,), 0.3, 2.0),
        "norm_one_gain": jnp.clip(1.0 + 0.1 * jax.random.normal(key_list[11], (D,), jnp.float32), 0.5, 1.5).astype(jnp.bfloat16),
        "norm_one_bias": gaussian(key_list[12], (D,), 0.3, 2.0),
        "cross_query": gaussian(key_list[13], (D, D), D ** -0.5, 0.25),
        "cross_query_bias": gaussian(key_list[14], (D,), 0.3, 2.0),
        "cross_key": gaussian(key_list[15], (D, D), D ** -0.5, 0.25),
        "cross_value": gaussian(key_list[16], (D, D), D ** -0.5, 0.25),
        "cross_value_bias": gaussian(key_list[17], (D,), 0.3, 2.0),
        "cross_out": gaussian(key_list[18], (D, D), (D // 16) ** -0.5, 1.0),
        "cross_out_bias": gaussian(key_list[19], (D,), 0.3, 2.0),
        "norm_two_gain": jnp.clip(1.0 + 0.1 * jax.random.normal(key_list[20], (D,), jnp.float32), 0.5, 1.5).astype(jnp.bfloat16),
        "norm_two_bias": gaussian(key_list[21], (D,), 0.3, 2.0),
        "expand_weight": gaussian(key_list[22], (D, FF), D ** -0.5, 0.25),
        "expand_bias": gaussian(key_list[23], (FF,), 0.5, 3.0),
        "project_weight": gaussian(key_list[24], (FF, D), FF ** -0.5, 0.109375),
        "project_bias": gaussian(key_list[25], (D,), 0.3, 2.0),
        "norm_three_gain": jnp.clip(1.0 + 0.1 * jax.random.normal(key_list[26], (D,), jnp.float32), 0.5, 1.5).astype(jnp.bfloat16),
        "norm_three_bias": gaussian(key_list[27], (D,), 0.3, 2.0),
        "out_cotangent": gaussian(key_list[28], (ITEMS, NQ, D), 1.0, 6.0, ((0, 8), (1, 4))),
    }


@jax.custom_vjp
def low(v):
    return lax.optimization_barrier(v.astype(jnp.bfloat16)).astype(jnp.float32)

@jax.custom_vjp
def low_back(v):
    return v

def low_keep(v):
    return (low(v), None)

def low_pass(kept, grad):
    return (grad,)

def back_keep(v):
    return (v, None)

def back_low(kept, grad):
    return (low(grad),)
low.defvjp(low_keep, low_pass)
low_back.defvjp(back_keep, back_low)

def sinusoid(first, count, model_width):
    position = (first + jnp.arange(count, dtype=jnp.int32)).astype(jnp.float32)
    column = jnp.arange(model_width // 2, dtype=jnp.int32).astype(jnp.float32)
    frequency = jnp.exp(column * (-2.0 * math.log(10000.0) / model_width))
    angles = position[:, None] * frequency[None, :]
    return jnp.stack([jnp.sin(angles), jnp.cos(angles)], axis=-1).reshape(count, model_width)

def layer_norm(values, norm_gain, norm_shift):
    average = lax.optimization_barrier(jnp.mean(values, axis=-1, keepdims=True))
    centred = values - average
    spread = lax.optimization_barrier(jnp.mean(centred * centred, axis=-1, keepdims=True))
    return centred * lax.rsqrt(spread + 1e-05) * norm_gain + norm_shift

def matmul(left, right):
    return jnp.dot(left, right, precision=lax.Precision.HIGHEST)

def rounded(values):
    return low_back(low(values))

def attention(queries, key_rows, value_rows, visible):
    head_dim = queries.shape[1] // HEADS
    query_heads = queries.reshape(queries.shape[0], HEADS, head_dim)
    key_heads = key_rows.reshape(key_rows.shape[0], HEADS, head_dim)
    value_heads = value_rows.reshape(value_rows.shape[0], HEADS, head_dim)
    logits = jnp.einsum('qhd,khd->hqk', query_heads, key_heads, precision=lax.Precision.HIGHEST) * head_dim ** (-0.5)
    logits = low_back(jnp.where(visible[None, None, :], logits, -1e+30))
    weights = low(jax.nn.softmax(logits, axis=-1))
    result = jnp.einsum('hqk,khd->qhd', weights, value_heads, precision=lax.Precision.HIGHEST)
    return rounded(result.reshape(queries.shape))

def layer(params, inputs, memory_rows, visible, positions):
    self_query, self_query_bias, self_key, self_value, self_value_bias, self_out, self_out_bias, norm_one_gain, norm_one_bias, cross_query, cross_query_bias, cross_key, cross_value, cross_value_bias, cross_out, cross_out_bias, norm_two_gain, norm_two_bias, expand_weight, expand_bias, project_weight, project_bias, norm_three_gain, norm_three_bias, query_embed = params
    attn_input = low(inputs + query_embed)
    self_queries = rounded(matmul(attn_input, self_query) + self_query_bias)
    self_keys = rounded(matmul(attn_input, self_key))
    self_values = rounded(matmul(inputs, self_value) + self_value_bias)
    everyone = jnp.ones((inputs.shape[0],), dtype=jnp.bool_)
    self_result = attention(self_queries, self_keys, self_values, everyone)
    first_sum = inputs + low_back(matmul(self_result, self_out) + self_out_bias)
    first_normed = layer_norm(first_sum, norm_one_gain, norm_one_bias)
    cross_input = low(first_normed + query_embed)
    cross_queries = rounded(matmul(cross_input, cross_query) + cross_query_bias)
    memory_keys = rounded(matmul(low(memory_rows + positions), cross_key))
    memory_values = rounded(matmul(memory_rows, cross_value) + cross_value_bias)
    cross_result = attention(cross_queries, memory_keys, memory_values, visible)
    second_sum = first_normed + low_back(matmul(cross_result, cross_out) + cross_out_bias)
    second_normed = layer_norm(second_sum, norm_two_gain, norm_two_bias)
    hidden_pre = low_back(matmul(low(second_normed), expand_weight) + expand_bias)
    hidden_act = low(jax.nn.gelu(hidden_pre, approximate=False))
    third_sum = second_normed + low_back(matmul(hidden_act, project_weight) + project_bias)
    return layer_norm(third_sum, norm_three_gain, norm_three_bias)

def reference(decoder_input, memory, lengths, query_embed, self_query, self_query_bias, self_key, self_value, self_value_bias, self_out, self_out_bias, norm_one_gain, norm_one_bias, cross_query, cross_query_bias, cross_key, cross_value, cross_value_bias, cross_out, cross_out_bias, norm_two_gain, norm_two_bias, expand_weight, expand_bias, project_weight, project_bias, norm_three_gain, norm_three_bias, out_cotangent):
    params = tuple((p.astype(jnp.float32) for p in (self_query, self_query_bias, self_key, self_value, self_value_bias, self_out, self_out_bias, norm_one_gain, norm_one_bias, cross_query, cross_query_bias, cross_key, cross_value, cross_value_bias, cross_out, cross_out_bias, norm_two_gain, norm_two_bias, expand_weight, expand_bias, project_weight, project_bias, norm_three_gain, norm_three_bias, query_embed)))
    positions = sinusoid(0, MEM, D)

    def one_item(totals, item):
        inputs, memory_rows, length, grad_out = item
        visible = jnp.arange(MEM, dtype=jnp.int32) < length

        def forward(weights, layer_in, memory_in):
            return layer(weights, layer_in, memory_in, visible, positions)
        result, backward = jax.vjp(forward, params, inputs.astype(jnp.float32), memory_rows.astype(jnp.float32))
        grad_params, grad_in, grad_memory = backward(grad_out.astype(jnp.float32))
        totals = jax.tree.map(jnp.add, totals, grad_params)
        return (totals, (result.astype(jnp.bfloat16), grad_in.astype(jnp.bfloat16), grad_memory.astype(jnp.bfloat16)))
    zeros = tuple((jnp.zeros_like(p) for p in params))
    totals, (outputs, input_grads, memory_grads) = lax.scan(one_item, zeros, (decoder_input, memory, lengths, out_cotangent))
    return (outputs, input_grads, memory_grads, totals[24], totals[0], totals[1], totals[2], totals[3], totals[4], totals[5], totals[6], totals[7], totals[8], totals[9], totals[10], totals[11], totals[12], totals[13], totals[14], totals[15], totals[16], totals[17], totals[18], totals[19], totals[20], totals[21], totals[22], totals[23])
```

```python
import math

import jax
import jax.numpy as jnp
import numpy as np
from jax import lax
from jax.sharding import PartitionSpec as P

HEADS = 8


def sinusoid(count, model_width):
    position = np.arange(count, dtype=np.float32)
    column = np.arange(model_width // 2, dtype=np.float32)
    frequency = np.exp(column * np.float32(-2.0 * math.log(10000.0) / model_width)).astype(np.float32)
    angles = (position[:, None] * frequency[None, :]).astype(np.float32)
    table = np.stack([np.sin(angles), np.cos(angles)], axis=-1)
    return table.reshape(count, model_width).astype(np.float32)


def layer_norm(values, norm_gain, norm_shift):
    average = jnp.mean(values, axis=-1, keepdims=True)
    centred = values - average
    spread = jnp.mean(centred * centred, axis=-1, keepdims=True)
    return centred * lax.rsqrt(spread + 1e-05) * norm_gain + norm_shift


def linear(left, right):
    return jnp.dot(left, right, preferred_element_type=jnp.float32)


def back_linear(grad_rows, weight):
    return jnp.einsum("bne,de->bnd", grad_rows, weight, preferred_element_type=jnp.float32)


def outer_sum(left, grad_rows):
    return jnp.einsum("bnd,bne->de", left, grad_rows, preferred_element_type=jnp.float32)


def column_sum(grad_rows):
    return jnp.sum(grad_rows.astype(jnp.float32), axis=(0, 1))


def split_heads(values):
    return values.reshape(values.shape[0], values.shape[1], HEADS, values.shape[2] // HEADS)


def join_heads(values):
    return values.reshape(values.shape[0], values.shape[1], values.shape[2] * values.shape[3])


def attend(queries, key_rows, value_rows, score_scale, visible):
    logits = (
        jnp.einsum("bqhd,bkhd->bhqk", queries, key_rows, preferred_element_type=jnp.float32)
        * score_scale
    )
    if visible is not None:
        logits = jnp.where(visible[:, None, None, :], logits, -1e30)
    highest = jnp.max(logits, axis=-1, keepdims=True)
    raised = jnp.exp(logits - highest)
    weights = raised / jnp.sum(raised, axis=-1, keepdims=True)
    low = weights.astype(jnp.bfloat16)
    result = jnp.einsum("bhqk,bkhd->bqhd", low, value_rows, preferred_element_type=jnp.float32)
    return join_heads(result).astype(jnp.bfloat16), weights


def attend_back(queries, key_rows, value_rows, score_scale, weights, grad_out):
    grad_weights = jnp.einsum(
        "bqhd,bkhd->bhqk", grad_out, value_rows, preferred_element_type=jnp.float32
    )
    inner = jnp.sum(weights * grad_weights, axis=-1, keepdims=True)
    grad_logits = (weights * (grad_weights - inner)).astype(jnp.bfloat16)
    grad_queries = (
        jnp.einsum("bhqk,bkhd->bqhd", grad_logits, key_rows, preferred_element_type=jnp.float32)
        * score_scale
    )
    grad_keys = (
        jnp.einsum("bhqk,bqhd->bkhd", grad_logits, queries, preferred_element_type=jnp.float32)
        * score_scale
    )
    grad_values = jnp.einsum(
        "bhqk,bqhd->bkhd",
        weights.astype(jnp.bfloat16),
        grad_out,
        preferred_element_type=jnp.float32,
    )
    return (
        join_heads(grad_queries).astype(jnp.bfloat16),
        join_heads(grad_keys).astype(jnp.bfloat16),
        join_heads(grad_values).astype(jnp.bfloat16),
    )


def swap(values, axis, bit):
    size = lax.axis_size(axis)
    return lax.ppermute(values, axis, [(i, i ^ bit) for i in range(size)])


def pick(values, index, axis):
    return lax.dynamic_index_in_dim(values, index, axis, keepdims=False)


def halve(values, axis, bit, dim):
    mine = (lax.axis_index(axis) // bit) % 2
    sent = pick(values, 1 - mine, dim)
    kept = pick(values, mine, dim)
    got = swap(sent, axis, bit)
    total = kept.astype(jnp.float32) + got.astype(jnp.float32)
    return total


def reduce_blocks(blocks, order):
    total = blocks.astype(jnp.bfloat16)
    for step, (axis, bit) in enumerate(order):
        total = halve(total, axis, bit, 0)
        if step < len(order) - 1:
            total = total.astype(jnp.bfloat16)
    return total


def bits_of(size):
    return [1 << b for b in range(size.bit_length() - 1)]


def regroup(values, axis_dims, order):
    return values


def to_blocks(grad, row_axis, col_axis, order):
    sizes = {axis: lax.axis_size(axis) for axis in ("ba", "pb")}
    dims = []
    shape = []
    for axis, extent in ((row_axis, grad.shape[0]), (col_axis, grad.shape[1])):
        for bit in reversed(bits_of(sizes[axis])):
            dims.append((axis, bit))
            shape.append(2)
        dims.append((axis, 0))
        shape.append(extent // sizes[axis])
    grad = grad.reshape(shape)
    places = [dims.index(step) for step in order]
    rest = [i for i, d in enumerate(dims) if d[1] == 0]
    return grad.transpose(places + rest)


def exchange(values, axis):
    size = lax.axis_size(axis)
    return [values[0]] + [swap(values[k], axis, k) for k in range(1, size)]


def local(
    decoder_input,
    memory,
    lengths,
    query_embed,
    self_query,
    self_query_bias,
    self_key,
    self_value,
    self_value_bias,
    self_out,
    self_out_bias,
    norm_one_gain,
    norm_one_bias,
    cross_query,
    cross_query_bias,
    cross_key,
    cross_value,
    cross_value_bias,
    cross_out,
    cross_out_bias,
    norm_two_gain,
    norm_two_bias,
    expand_weight,
    expand_bias,
    project_weight,
    project_bias,
    norm_three_gain,
    norm_three_bias,
    out_cotangent,
):
    f32 = jnp.float32
    bf16 = jnp.bfloat16
    items, chunk, model_width = decoder_input.shape
    memory_length = memory.shape[1]
    group = lax.axis_size("pb")
    place = lax.axis_index("pb")
    own = items // group
    quarter = memory_length // group
    score_scale = (model_width // HEADS) ** (-0.5)

    def gather_rows(values):
        parts = [lax.dynamic_slice_in_dim(values, (place ^ k) * own, own, 0) for k in range(group)]
        return jnp.concatenate(exchange(parts, "pb"), axis=1)

    def return_rows(values):
        parts = exchange([values[:, k * chunk : (k + 1) * chunk] for k in range(group)], "pb")
        whole = jnp.zeros((items, chunk, model_width), values.dtype)
        for k in range(group):
            whole = lax.dynamic_update_slice_in_dim(whole, parts[k], (place ^ k) * own, 0)
        return whole

    decoder_rows = gather_rows(decoder_input)
    embed = jnp.concatenate(exchange([query_embed] * group, "pb"), axis=0).astype(f32)
    cotangent_rows = gather_rows(out_cotangent)
    own_memory = lax.dynamic_slice_in_dim(memory, place * own, own, 0)
    own_lengths = lax.dynamic_slice_in_dim(lengths, place * own, own, 0)

    table = jnp.asarray(sinusoid(memory_length, model_width))
    keyed = (own_memory.astype(f32) + table[None]).astype(bf16)
    memory_keys = linear(keyed, cross_key).astype(bf16)
    memory_values = (linear(own_memory, cross_value) + cross_value_bias.astype(f32)).astype(bf16)
    visible = jnp.arange(memory_length, dtype=jnp.int32)[None, :] < own_lengths[:, None]

    inputs = decoder_rows.astype(f32)
    attn_input = (inputs + embed[None]).astype(bf16)
    self_queries = (linear(attn_input, self_query) + self_query_bias.astype(f32)).astype(bf16)
    self_keys = linear(attn_input, self_key).astype(bf16)
    self_values = (linear(decoder_rows, self_value) + self_value_bias.astype(f32)).astype(bf16)
    self_result, self_weights = attend(
        split_heads(self_queries), split_heads(self_keys), split_heads(self_values), score_scale, None
    )
    first_sum = inputs + linear(self_result, self_out) + self_out_bias.astype(f32)
    first_normed, norm_one_back = jax.vjp(
        layer_norm, first_sum, norm_one_gain.astype(f32), norm_one_bias.astype(f32)
    )
    cross_input = (first_normed + embed[None]).astype(bf16)
    cross_queries = (linear(cross_input, cross_query) + cross_query_bias.astype(f32)).astype(bf16)
    cross_result, cross_weights = attend(
        split_heads(cross_queries),
        split_heads(memory_keys),
        split_heads(memory_values),
        score_scale,
        visible,
    )
    second_sum = first_normed + linear(cross_result, cross_out) + cross_out_bias.astype(f32)
    second_normed, norm_two_back = jax.vjp(
        layer_norm, second_sum, norm_two_gain.astype(f32), norm_two_bias.astype(f32)
    )
    second_low = second_normed.astype(bf16)
    hidden_pre = linear(second_low, expand_weight) + expand_bias.astype(f32)
    hidden_act, gelu_back = jax.vjp(lambda v: jax.nn.gelu(v, approximate=False), hidden_pre)
    hidden_low = hidden_act.astype(bf16)
    third_sum = second_normed + linear(hidden_low, project_weight) + project_bias.astype(f32)
    final_normed, norm_three_back = jax.vjp(
        layer_norm, third_sum, norm_three_gain.astype(f32), norm_three_bias.astype(f32)
    )
    layer_output = return_rows(final_normed.astype(bf16))

    third_grad, grad_gain_three, grad_bias_three = norm_three_back(cotangent_rows.astype(f32))
    branch_grad = third_grad.astype(bf16)
    grad_project_bias = column_sum(branch_grad)
    grad_project = outer_sum(hidden_low, branch_grad)
    (hidden_grad,) = gelu_back(back_linear(branch_grad, project_weight))
    hidden_grad = hidden_grad.astype(bf16)
    grad_expand_bias = column_sum(hidden_grad)
    grad_expand = outer_sum(second_low, hidden_grad)

    ba_bits = bits_of(lax.axis_size("ba"))
    pb_bits = bits_of(lax.axis_size("pb"))
    x_first = [("pb", 1), ("ba", 1)] + [("pb", b) for b in pb_bits[1:]] + [("ba", b) for b in ba_bits[1:]]
    y_first = [("pb", b) for b in pb_bits] + [("ba", b) for b in ba_bits]

    project_out = reduce_blocks(to_blocks(grad_project, "pb", "ba", x_first), x_first)
    expand_out = reduce_blocks(to_blocks(grad_expand, "ba", "pb", y_first), y_first)

    second_grad = third_grad + back_linear(hidden_grad, expand_weight)
    cross_sum_grad, grad_gain_two, grad_bias_two = norm_two_back(second_grad)
    cross_branch = cross_sum_grad.astype(bf16)
    grad_cross_out_bias = column_sum(cross_branch)
    grad_cross_out = outer_sum(cross_result, cross_branch)
    cross_result_grad = back_linear(cross_branch, cross_out).astype(bf16)
    cross_query_grad, memory_key_grad, memory_value_grad = attend_back(
        split_heads(cross_queries),
        split_heads(memory_keys),
        split_heads(memory_values),
        score_scale,
        cross_weights,
        split_heads(cross_result_grad),
    )
    grad_cross_key = outer_sum(keyed, memory_key_grad)
    grad_cross_value = outer_sum(own_memory, memory_value_grad)
    grad_cross_value_bias = column_sum(memory_value_grad)
    own_memory_grad = (
        back_linear(memory_key_grad, cross_key) + back_linear(memory_value_grad, cross_value)
    ).astype(bf16)
    parts = exchange(
        [
            lax.dynamic_slice_in_dim(own_memory_grad, (place ^ k) * quarter, quarter, 1)
            for k in range(group)
        ],
        "pb",
    )
    memory_grad = jnp.zeros((items, quarter, model_width), bf16)
    for k in range(group):
        memory_grad = lax.dynamic_update_slice_in_dim(memory_grad, parts[k], (place ^ k) * own, 0)

    grad_cross_query_bias = column_sum(cross_query_grad)
    grad_cross_query = outer_sum(cross_input, cross_query_grad)
    cross_input_grad = back_linear(cross_query_grad, cross_query)
    cross_grads = jnp.stack(
        [
            to_blocks(g, "ba", "pb", x_first)
            for g in (grad_cross_query, grad_cross_key, grad_cross_value, grad_cross_out)
        ],
        axis=len(x_first),
    )
    cross_outs = reduce_blocks(cross_grads, x_first)

    first_grad = cross_sum_grad + cross_input_grad
    self_sum_grad, grad_gain_one, grad_bias_one = norm_one_back(first_grad)
    self_branch = self_sum_grad.astype(bf16)
    grad_self_out_bias = column_sum(self_branch)
    grad_self_out = outer_sum(self_result, self_branch)
    self_result_grad = back_linear(self_branch, self_out).astype(bf16)
    self_query_grad, self_key_grad, self_value_grad = attend_back(
        split_heads(self_queries),
        split_heads(self_keys),
        split_heads(self_values),
        score_scale,
        self_weights,
        split_heads(self_result_grad),
    )
    grad_self_query = outer_sum(attn_input, self_query_grad)
    grad_self_query_bias = column_sum(self_query_grad)
    grad_self_key = outer_sum(attn_input, self_key_grad)
    grad_self_value = outer_sum(decoder_rows, self_value_grad)
    grad_self_value_bias = column_sum(self_value_grad)
    self_grads = jnp.stack(
        [
            to_blocks(g, "ba", "pb", x_first)
            for g in (grad_self_query, grad_self_key, grad_self_value, grad_self_out)
        ],
        axis=len(x_first),
    )
    self_outs = reduce_blocks(self_grads, x_first)

    attn_input_grad = back_linear(self_query_grad, self_query) + back_linear(self_key_grad, self_key)
    input_grad = return_rows(
        (self_sum_grad + attn_input_grad + back_linear(self_value_grad, self_value)).astype(bf16)
    )
    embed_local = jnp.sum(attn_input_grad + cross_input_grad, axis=0)
    embed_local = embed_local.reshape(group, chunk, model_width)
    for bit in pb_bits:
        spread = embed_local.reshape(group // (2 * bit), 2, bit, chunk, model_width)
        embed_local = jnp.where((place // bit) % 2 == 1, spread[:, ::-1], spread).reshape(
            group, chunk, model_width
        )
    embed_local = embed_local.reshape(group * chunk, model_width)
    embed_grad = reduce_blocks(to_blocks(embed_local, "pb", "ba", x_first), x_first)

    vectors = (
        grad_self_query_bias,
        grad_self_value_bias,
        grad_self_out_bias,
        grad_gain_one,
        grad_bias_one,
        grad_cross_query_bias,
        grad_cross_value_bias,
        grad_cross_out_bias,
        grad_gain_two,
        grad_bias_two,
        grad_expand_bias,
        grad_project_bias,
        grad_gain_three,
        grad_bias_three,
    )
    total = jnp.concatenate(vectors).reshape(-1, 128)
    for axis, bit in x_first:
        total = total + swap(total, axis, bit)
    total = total.reshape(-1)
    summed = []
    start = 0
    for v in vectors:
        summed.append(total[start : start + v.shape[0]])
        start += v.shape[0]
    (
        query_bias_out,
        value_bias_out,
        out_bias_out,
        gain_one_out,
        bias_one_out,
        cross_query_bias_out,
        cross_value_bias_out,
        cross_out_bias_out,
        gain_two_out,
        bias_two_out,
        expand_bias_out,
        project_bias_out,
        gain_three_out,
        bias_three_out,
    ) = summed
    return (
        layer_output,
        input_grad,
        memory_grad,
        embed_grad,
        self_outs[0],
        query_bias_out,
        self_outs[1],
        self_outs[2],
        value_bias_out,
        self_outs[3],
        out_bias_out,
        gain_one_out,
        bias_one_out,
        cross_outs[0],
        cross_query_bias_out,
        cross_outs[1],
        cross_outs[2],
        cross_value_bias_out,
        cross_outs[3],
        cross_out_bias_out,
        gain_two_out,
        bias_two_out,
        expand_out,
        expand_bias_out,
        project_out,
        project_bias_out,
        gain_three_out,
        bias_three_out,
    )


def solution(mesh):
    rows = P("ba", "pb", None)
    copied = P()
    placed = (rows, P("ba", None, None), P("ba"), P("pb", None)) + (copied,) * 24 + (rows,)
    square = P("ba", "pb")
    return jax.shard_map(
        local,
        mesh=mesh,
        in_specs=placed,
        out_specs=(
            rows,
            rows,
            rows,
            P("pb", "ba"),
            square,
            copied,
            square,
            square,
            copied,
            square,
            copied,
            copied,
            copied,
            square,
            copied,
            square,
            square,
            copied,
            square,
            copied,
            copied,
            copied,
            square,
            copied,
            P("pb", "ba"),
            copied,
            copied,
            copied,
        ),
        check_vma=False,
    )
```

```python
import math

import jax
import jax.numpy as jnp
import numpy as np
from jax import lax
from jax.experimental import pallas as pl
from jax.experimental.pallas import tpu as pltpu
from jax.sharding import PartitionSpec as P

HEADS = 8
GROUP_HEADS = 4
F32 = jnp.float32
BF16 = jnp.bfloat16
HIDDEN_CHUNKS = 5
VMEM_BYTES = 58 * 2**20


def sinusoid(count, model_width):
    position = np.arange(count, dtype=np.float32)
    column = np.arange(model_width // 2, dtype=np.float32)
    frequency = np.exp(column * np.float32(-2.0 * math.log(10000.0) / model_width)).astype(np.float32)
    angles = (position[:, None] * frequency[None, :]).astype(np.float32)
    table = np.stack([np.sin(angles), np.cos(angles)], axis=-1)
    return table.reshape(count, model_width).astype(np.float32)


def padded_to(extent, multiple):
    return -(-extent // multiple) * multiple


def nn(left, right):
    return lax.dot_general(left, right, (((1,), (0,)), ((), ())), preferred_element_type=F32)


def nt(left, right):
    return lax.dot_general(left, right, (((1,), (1,)), ((), ())), preferred_element_type=F32)


def tn(left, right):
    return lax.dot_general(left, right, (((0,), (0,)), ((), ())), preferred_element_type=F32)


VM, SM, DMA, OWN = range(4)


class Named:
    def __init__(self, find):
        self.find = find

    def __getattr__(self, key):
        return self.find(key)


class Numbered:
    def __init__(self, find, key):
        self.find, self.key = find, key

    def __getitem__(self, place):
        return self.find((self.key, place))


def flat(entries):
    result = {}
    for key, (value, *rest) in entries.items():
        if isinstance(value, list):
            for place, member in enumerate(value):
                result[(key, place)] = (member, *rest)
        else:
            result[key] = (value, *rest)
    return result


def run(body, ins, outs, scratch=None, after=(), microseconds=5.0):
    listed = {key for entries in (ins, outs) for key, entry in entries.items() if isinstance(entry[0], list)}
    ins, outs, scratch = flat(ins), flat(outs), scratch or {}
    in_dma = [key for key, entry in ins.items() if entry[1] in (DMA, OWN)]
    out_dma = [key for key, entry in outs.items() if entry[2] == DMA]

    def kernel(*refs):
        refs = list(refs)
        held = {key: refs.pop(0) for key in ins}
        del refs[: len(after)]
        results = {key: refs.pop(0) for key in outs}
        arrived = {key: refs.pop(0) for key in in_dma}
        leaving = {key: refs.pop(0) for key in out_dma}
        held.update(results)
        sources = {key: held[key] for key in in_dma}
        held.update(arrived)
        held.update(leaving)
        held.update({key: refs.pop(0) for key in scratch})
        in_sem, out_sem, part_sem = refs
        pending = {}
        for place, key in enumerate(in_dma):
            source = sources[key]
            if ins[key][1] == OWN:
                count = arrived[key].shape[0]
                source = source.at[pl.ds(lax.axis_index("pb") * count, count)]
            pending[key] = pltpu.make_async_copy(source, arrived[key], in_sem.at[place])
            pending[key].start()
        started = {}

        def find(key):
            if key in listed:
                return Numbered(find, key)
            if key in pending:
                pending.pop(key).wait()
            return held[key]

        def put(**values):
            for key, value in values.items():
                if key in listed:
                    key = (key, value)
                elif value is not None:
                    held[key][...] = value
                if key in leaving:
                    place = out_dma.index(key)
                    started[key] = pltpu.make_async_copy(leaving[key], results[key], out_sem.at[place])
                    started[key].start()

        def put_part(part, **values):
            for key in values:
                place = out_dma.index(key)
                copy = pltpu.make_async_copy(leaving[key].at[part], results[key].at[part], part_sem.at[place, part])
                copy.start()
                started[(key, part)] = copy
                started[key] = copy

        bag = Named(find)
        bag.put = put
        bag.put_part = put_part
        body(bag)
        for key in list(pending):
            pending.pop(key).wait()
        for key in out_dma:
            assert key in started, key
        for copy in {id(copy): copy for copy in started.values()}.values():
            copy.wait()

    spaces = [pltpu.VMEM, pltpu.SMEM, pl.ANY, pl.ANY]
    arrays = [entry[0] for entry in ins.values()]
    nbytes = sum(int(np.prod(array.shape)) * array.dtype.itemsize for array in arrays)
    made = pl.pallas_call(
        kernel,
        out_shape=[jax.ShapeDtypeStruct(entry[0], entry[1]) for entry in outs.values()],
        in_specs=[pl.BlockSpec(memory_space=spaces[entry[1]]) for entry in ins.values()]
        + [pl.BlockSpec(memory_space=pl.ANY)] * len(after),
        out_specs=[pl.BlockSpec(memory_space=spaces[entry[2]]) for entry in outs.values()],
        scratch_shapes=[
            pltpu.VMEM(
                (ins[key][0].shape[0] // lax.axis_size("pb"), *ins[key][0].shape[1:])
                if ins[key][1] == OWN
                else ins[key][0].shape,
                ins[key][0].dtype,
            )
            for key in in_dma
        ]
        + [pltpu.VMEM(outs[key][0], outs[key][1]) for key in out_dma]
        + [pltpu.VMEM(shape, dtype) for shape, dtype in scratch.values()]
        + [pltpu.SemaphoreType.DMA((max(1, len(in_dma)),)), pltpu.SemaphoreType.DMA((max(1, len(out_dma)),)), pltpu.SemaphoreType.DMA((max(1, len(out_dma)), 2))],
        compiler_params=pltpu.CompilerParams(vmem_limit_bytes=VMEM_BYTES),
        cost_estimate=pl.CostEstimate(
            flops=int(microseconds * 1.1e9), bytes_accessed=nbytes, transcendentals=0
        ),
        name=body.__name__,
    )(*arrays, *after)
    by_key = dict(zip(outs, made))

    def result(key):
        if key in listed:
            return [value for name, value in by_key.items() if isinstance(name, tuple) and name[0] == key]
        return by_key[key]

    return Named(result)


def norm_forward(values, gain, shift):
    average = jnp.mean(values, axis=-1, keepdims=True)
    centred = values - average
    spread = jnp.mean(centred * centred, axis=-1, keepdims=True)
    scale = lax.rsqrt(spread + 1e-05)
    unit = centred * scale
    return unit, scale, unit * gain + shift


def norm_backward(grad, unit, scale, gain):
    lifted = grad * gain
    first = jnp.mean(lifted, axis=-1, keepdims=True)
    second = jnp.mean(lifted * unit, axis=-1, keepdims=True)
    return scale * (lifted - first - unit * second)


def column_sum(values):
    return jnp.sum(values.astype(F32), axis=0, keepdims=True)


def spread_heads(rows, width):
    count, columns = rows.shape
    lane = lax.broadcasted_iota(jnp.int32, (1, columns), 1) // width
    return jnp.concatenate(
        [rows * (lane == h).astype(F32).astype(BF16) for h in range(columns // width)], axis=0
    )


def diagonal(blocks, width, count):
    heads = blocks.shape[0] // width
    return jnp.concatenate(
        [blocks[h * width : (h + 1) * width, h * count : (h + 1) * count] for h in range(heads)], axis=0
    )


def swap(values, axis, bit):
    size = lax.axis_size(axis)
    return lax.ppermute(values, axis, [(i, i ^ bit) for i in range(size)])


def bits_of(size):
    return [1 << b for b in range(size.bit_length() - 1)]


def exchange(values, axis):
    size = lax.axis_size(axis)
    return [values[0]] + [swap(values[k], axis, k) for k in range(1, size)]


def pair_sum(kept, got):
    return kept.astype(F32) + got.astype(F32)


def meet(*arrays):
    return lax.optimization_barrier(arrays)


def tie(values, *before):
    return lax.optimization_barrier((values, *before))[0]


def halves(values, dim):
    dim = dim % values.ndim
    if values.shape[dim] == 2:
        parts = [lax.index_in_dim(values, j, dim, keepdims=False) for j in range(2)]
    else:
        half = values.shape[dim] // 2
        parts = [lax.slice_in_dim(values, j * half, (j + 1) * half, axis=dim) for j in range(2)]
    return parts[0].astype(BF16), parts[1].astype(BF16)


def row_halves(total, extra):
    body = total.shape[0] - extra
    parts = [total[: body // 2], total[body // 2 : body]]
    if extra:
        parts = [jnp.concatenate([part, total[body:]]) for part in parts]
    return parts[0].astype(BF16), parts[1].astype(BF16)


def finish(total, bits, split):
    for bit in bits:
        kept, sent = split(total)
        total = pair_sum(kept, swap(sent, "ba", bit))
    return total


def interleave(first, second, first_size, second_size, extra):
    count = second.shape[0] // second_size
    tail = [first[count * first_size :]] if extra else []
    body = jnp.concatenate(
        [
            first[: count * first_size].reshape(count, first_size, -1),
            second.reshape(count, second_size, -1),
        ],
        axis=1,
    )
    return jnp.concatenate([body.reshape(count * (first_size + second_size), -1)] + tail)


def permutation(order, model_width, ba_size, mine):
    width = model_width // ba_size
    column = lax.broadcasted_iota(jnp.int32, (1, model_width), 1)
    position = column // width
    relative = jnp.zeros_like(column)
    for step, bit in enumerate(order):
        digit = (position >> (len(order) - 1 - step)) & 1
        relative = relative + digit * bit
    source = (relative ^ mine) * width + column % width
    row = lax.broadcasted_iota(jnp.int32, (model_width, model_width), 0)
    return (row == source).astype(BF16)


def local(
    decoder_input,
    memory,
    lengths,
    query_embed,
    self_query,
    self_query_bias,
    self_key,
    self_value,
    self_value_bias,
    self_out,
    self_out_bias,
    norm_one_gain,
    norm_one_bias,
    cross_query,
    cross_query_bias,
    cross_key,
    cross_value,
    cross_value_bias,
    cross_out,
    cross_out_bias,
    norm_two_gain,
    norm_two_bias,
    expand_weight,
    expand_bias,
    project_weight,
    project_bias,
    norm_three_gain,
    norm_three_bias,
    out_cotangent,
):
    items, chunk, width = decoder_input.shape
    tokens = memory.shape[1]
    hidden = expand_weight.shape[1]
    group = lax.axis_size("pb")
    ba_size = lax.axis_size("ba")
    place = lax.axis_index("pb")
    mine = lax.axis_index("ba")
    own = items // group
    quarter = tokens // group
    slot = padded_to(chunk, 32)
    rows = group * slot
    all_rows = own * rows
    part = padded_to(quarter, 16)
    span = group * part
    head = width // HEADS
    scale = head ** (-0.5)
    share = hidden // group
    step = hidden // HIDDEN_CHUNKS
    wide = GROUP_HEADS * head
    many = GROUP_HEADS * rows
    groups = HEADS // GROUP_HEADS
    ba_bits = bits_of(ba_size)
    block = width // ba_size
    lanes = width // group


    def prepare(r):
        index = lax.axis_index("pb")
        r.wide_x[...] = r.x[...].astype(F32)
        r.wide_g[...] = r.g[...].astype(F32)
        for k in range(group):
            source = (index ^ k) * own
            piece = r.rows[k]
            piece[...] = jnp.zeros(piece.shape, BF16)
            for i in range(own):
                piece[i, 0:chunk, :] = r.wide_x[:, source + i, :].astype(BF16)
                piece[own + 1 + i, 0:chunk, :] = r.wide_g[:, source + i, :].astype(BF16)
            piece[own, 0:chunk, :] = r.e[...]

    prepared = run(
        prepare,
        dict(
            x=(decoder_input.transpose(1, 0, 2), VM),
            e=(query_embed, VM),
            g=(out_cotangent.transpose(1, 0, 2), VM),
        ),
        dict(rows=([(2 * own + 1, slot, width)] * group, BF16, VM)),
        dict(wide_x=((chunk, items, width), F32), wide_g=((chunk, items, width), F32)),
        microseconds=1.0,
    )
    row_parts = exchange(prepared.rows, "pb")

    table = np.zeros((group, part, width), np.float32)
    table[:, :quarter] = sinusoid(tokens, width).reshape(group, quarter, width)
    table = jnp.asarray(table.reshape(span, width))

    def project_memory(r):
        for i in range(own):
            source = r.memory[i]
            for q in range(group):
                r.plain[i, q * part : q * part + quarter, :] = source[q * quarter : (q + 1) * quarter, :]
                if part > quarter:
                    r.plain[i, q * part + quarter : (q + 1) * part, :] = jnp.zeros((part - quarter, width), BF16)
            r.keyed[i] = (r.plain[i].astype(F32) + r.table[...]).astype(BF16)
            r.keys[i] = nn(r.keyed[i], r.wk[...]).astype(BF16)
            r.put_part(i, keys=None, keyed=None)
            r.values[i] = (nn(r.plain[i], r.wv[...]) + r.bv[...].astype(F32).reshape(1, width)).astype(BF16)
            r.put_part(i, values=None, plain=None)

    memory_block = ((own, span, width), BF16, DMA)
    prj = run(
        project_memory,
        dict(
            memory=(memory, OWN),
            table=(table, DMA),
            wk=(cross_key, DMA),
            wv=(cross_value, DMA),
            bv=(cross_value_bias, VM),
        ),
        dict(keys=memory_block, values=memory_block, keyed=memory_block, plain=memory_block),
        after=prepared.rows[:1],
        microseconds=7.0,
    )
    memory_keys, memory_values, keyed, plain = prj.keys, prj.values, prj.keyed, prj.plain

    vectors = [
        self_query_bias,
        self_value_bias,
        self_out_bias,
        norm_one_gain,
        norm_one_bias,
        cross_query_bias,
        cross_out_bias,
        norm_two_gain,
        norm_two_bias,
        project_bias,
        norm_three_gain,
        norm_three_bias,
    ]
    BQ, BV, BO, G1, B1, BCQ, BCO, G2, B2, BP, G3, B3 = range(12)

    def vector(r, place):
        return r.vectors[place][...].astype(F32).reshape(1, width)

    def attend(r, queries, keys, values, kept, inverse, where_scores, item, mask):
        results = []
        count = where_scores.shape[0]
        for g in range(groups):
            cols = slice(g * wide, (g + 1) * wide)
            where_scores[...] = nt(keys(cols), spread_heads(queries[:, cols], head))
            mask(where_scores)
            scores = where_scores[...]
            highest = jnp.max(scores, axis=0, keepdims=True)
            raised = jnp.exp(scores - highest)
            total = jnp.sum(raised, axis=0, keepdims=True)
            kept[item, :, g * many : (g + 1) * many] = raised.astype(BF16)
            back = 1.0 / total
            inverse[item, :, g * many : (g + 1) * many] = jnp.broadcast_to(back, (8, many))
            mixed = tn(values(cols), kept[item, :, g * many : (g + 1) * many]) * back
            results.append(diagonal(mixed, head, rows))
        return jnp.concatenate(results, axis=0).T

    def forward(r):
        x_buf, e_buf = r.x0, r.embed
        for k in range(group):
            piece = r.rows[k]
            for i in range(own):
                x_buf[i * rows + k * slot : i * rows + (k + 1) * slot, :] = piece[i]
                e_buf[i * rows + k * slot : i * rows + (k + 1) * slot, :] = piece[own].astype(F32)
        r.put(x0=None)
        a_in = (x_buf[...].astype(F32) + e_buf[...]).astype(BF16)
        r.put(a_in=a_in)
        queries = (nn(a_in, r.wq[...]) + vector(r, BQ)).astype(BF16)
        r.put(q1=(queries.astype(F32) * scale).astype(BF16))
        r.put(k1=nn(a_in, r.wk[...]).astype(BF16))
        r.put(v1=(nn(x_buf[...], r.wv[...]) + vector(r, BV)).astype(BF16))

        def self_mask(scores):
            row = lax.broadcasted_iota(jnp.int32, (rows, 1), 0) % slot
            scores[...] = jnp.where(row < chunk, scores[...], -1e30)

        for i in range(own):
            span_rows = slice(i * rows, (i + 1) * rows)
            result = attend(
                r,
                r.q1[span_rows, :],
                lambda cols: r.k1[span_rows, cols],
                lambda cols: r.v1[span_rows, cols],
                r.e1,
                r.inv1,
                r.self_scores,
                i,
                self_mask,
            )
            r.o1[span_rows, :] = result.astype(BF16)
        r.put(e1=None)
        r.put(inv1=None)
        r.put(o1=None)
        summed = x_buf[...].astype(F32) + nn(r.o1[...], r.wo[...]) + vector(r, BO)
        unit, spread, normed = norm_forward(summed, vector(r, G1), vector(r, B1))
        r.put(unit1=unit)
        r.put(spread1=spread)
        r.normed[...] = normed
        r.put(c_in=(normed + e_buf[...]).astype(BF16))
        queries = (nn(r.c_in[...], r.wcq[...]) + vector(r, BCQ)).astype(BF16)
        r.put(q2=(queries.astype(F32) * scale).astype(BF16))
        for i in range(own):
            span_rows = slice(i * rows, (i + 1) * rows)
            length = r.lengths[lax.axis_index("pb") * own + i]

            def cross_mask(scores):
                if part > quarter:
                    low = quarter // 8 * 8
                    row = lax.broadcasted_iota(jnp.int32, (part - low, 1), 0) + low
                    for q in range(group):
                        edge = slice(q * part + low, (q + 1) * part)
                        scores[edge, :] = jnp.where(row < quarter, scores[edge, :], -1e30)

                @pl.when(length < tokens)
                def _():
                    for q in range(group):
                        row = lax.broadcasted_iota(jnp.int32, (part, 1), 0)
                        edge = slice(q * part, (q + 1) * part)
                        seen = (row + q * quarter < length) & (row < quarter)
                        scores[edge, :] = jnp.where(seen, scores[edge, :], -1e30)

            result = attend(
                r,
                r.q2[span_rows, :],
                lambda cols: r.keys[i, :, cols],
                lambda cols: r.values[i, :, cols],
                r.e2,
                r.inv2,
                r.cross_scores,
                i,
                cross_mask,
            )
            r.o2[span_rows, :] = result.astype(BF16)
        r.put(e2=None)
        r.put(inv2=None)
        r.put(o2=None)
        summed = r.normed[...] + nn(r.o2[...], r.wco[...]) + vector(r, BCO)
        unit, spread, normed = norm_forward(summed, vector(r, G2), vector(r, B2))
        r.put(unit2=unit)
        r.put(spread2=spread)
        r.normed[...] = normed
        r.put(x2b=normed.astype(BF16))
        r.third[...] = normed + vector(r, BP)
        for j in range(HIDDEN_CHUNKS):
            cols = slice(j * step, (j + 1) * step)
            before = nn(r.x2b[...], r.we[:, cols]) + r.be[cols].astype(F32).reshape(1, step)
            share_below = 0.5 + 0.5 * lax.erf(before * (0.5**0.5))
            density = jnp.exp(-0.5 * before * before) * ((2.0 * math.pi) ** (-0.5))
            r.slope[:, cols] = share_below + before * density
            active = (before * share_below).astype(BF16)
            r.third[...] += nn(active, r.wp[cols, :])
            r.active_t[cols, :] = active.T
        index = lax.axis_index("pb")

        def ship(source, kept, sent):
            for y in range(group // 2):
                for c, target in ((0, kept), (1, sent)):
                    first = pl.multiple_of((index ^ (2 * y + c)) * share, 16)
                    target[y] = source[pl.ds(first, share), :]

        ship(r.active_t, r.act_keep, r.act_send)
        r.put(act_send=None, act_keep=None)
        unit, spread, normed = norm_forward(r.third[...], vector(r, G3), vector(r, B3))
        low = normed.astype(BF16)
        cot = r.cot
        for k in range(group):
            piece = r.rows[k]
            for i in range(own):
                here = slice(i * rows + k * slot, i * rows + (k + 1) * slot)
                (r.near[k] if k < 2 else r.far.at[k - 2])[i] = low[here, :]
                cot[here, :] = piece[own + 1 + i].astype(F32)
        r.put(near=0)
        r.put(near=1)
        r.put(far=None)
        sums = r.sums
        sums[...] = jnp.zeros(sums.shape, F32)
        sums[0:1, :] = column_sum(cot[...] * unit)
        sums[1:2, :] = column_sum(cot[...])
        third = norm_backward(cot[...], unit, spread, vector(r, G3))
        r.put(dr3=third)
        branch = third.astype(BF16)
        r.put(df=branch)
        sums[2:3, :] = column_sum(branch)
        r.put(sums=None)
        for j in range(HIDDEN_CHUNKS):
            cols = slice(j * step, (j + 1) * step)
            grad = (nt(r.df[...], r.wp[cols, :]) * r.slope[:, cols]).astype(BF16)
            r.dh[:, cols] = grad
            r.hidden_sum[:, cols] = column_sum(grad)
            r.active_t[cols, :] = grad.T
        ship(r.active_t, r.dh_keep, r.dh_send)
        r.put(dh_send=None, dh_keep=None, dh=None, hidden_sum=None)

    two = group // 2
    fw = run(
        forward,
        dict(
            lengths=(lengths, SM),
            rows=(row_parts, VM),
            vectors=(vectors, VM),
            be=(expand_bias, VM),
            wq=(self_query, DMA),
            wk=(self_key, DMA),
            wv=(self_value, DMA),
            wo=(self_out, DMA),
            wcq=(cross_query, DMA),
            keys=(memory_keys, DMA),
            values=(memory_values, DMA),
            wco=(cross_out, DMA),
            we=(expand_weight, DMA),
            wp=(project_weight, DMA),
        ),
        dict(

            x0=((all_rows, width), BF16, DMA),
            a_in=((all_rows, width), BF16, DMA),
            q1=((all_rows, width), BF16, DMA),
            k1=((all_rows, width), BF16, DMA),
            v1=((all_rows, width), BF16, DMA),
            e1=((own, rows, groups * many), BF16, DMA),
            inv1=((own, 8, groups * many), F32, DMA),
            o1=((all_rows, width), BF16, DMA),
            unit1=((all_rows, width), F32, DMA),
            spread1=((all_rows, 1), F32, DMA),
            c_in=((all_rows, width), BF16, DMA),
            q2=((all_rows, width), BF16, DMA),
            e2=((own, span, groups * many), BF16, DMA),
            inv2=((own, 8, groups * many), F32, DMA),
            o2=((all_rows, width), BF16, DMA),
            unit2=((all_rows, width), F32, DMA),
            spread2=((all_rows, 1), F32, DMA),
            x2b=((all_rows, width), BF16, DMA),
            act_keep=((two, share, all_rows), BF16, DMA),
            act_send=((two, share, all_rows), BF16, DMA),
            dr3=((all_rows, width), F32, DMA),
            df=((all_rows, width), BF16, DMA),
            dh=((all_rows, hidden), BF16, DMA),
            dh_keep=((two, share, all_rows), BF16, DMA),
            dh_send=((two, share, all_rows), BF16, DMA),
            sums=((8, width), F32, DMA),
            hidden_sum=((1, hidden), F32, DMA),
        near=([(own, slot, width)] * 2, BF16, DMA),
            far=((2, own, slot, width), BF16, DMA),
        ),
        dict(
            embed=((all_rows, width), F32),
            self_scores=((rows, many), F32),
            cross_scores=((span, many), F32),
            normed=((all_rows, width), F32),
            third=((all_rows, width), F32),
            cot=((all_rows, width), F32),
            slope=((all_rows, hidden), F32),
            active_t=((hidden, all_rows), BF16),
        ),
        microseconds=18.0,
    )

    act_got = swap(fw.act_send, "pb", 1)
    x2b_got = swap(fw.x2b, "pb", 1)
    df_got = swap(fw.df, "pb", 1)
    dh_got = swap(fw.dh_send, "pb", 1)
    project_order = list(ba_bits)
    expand_order = [ba_bits[1], ba_bits[0]] + list(ba_bits[2:])
    project_perm = permutation(project_order, width, ba_size, mine)
    expand_perm = permutation(expand_order, width, ba_size, mine)
    half = width // 2

    def hidden_grads(r):
        def one(perm, keep, got, rows_own, rows_got, kept, sent):
            own_cols = nn(rows_own(), perm()).astype(BF16)
            got_cols = nn(rows_got(), perm()).astype(BF16)
            for y in range(two):
                total = nn(keep()[y], own_cols) + nn(got()[y], got_cols)
                kept[y] = total[:, :half].astype(BF16)
                sent[y] = total[:, half:].astype(BF16)

        one(
            lambda: r.pperm[...],
            lambda: r.act_keep,
            lambda: r.act_got,
            lambda: r.df[...],
            lambda: r.df_got[...],
            r.p_keep,
            r.p_send,
        )
        r.put(p_send=None, p_keep=None)
        one(
            lambda: r.eperm[...],
            lambda: r.dh_keep,
            lambda: r.dh_got,
            lambda: r.x2b[...],
            lambda: r.x2b_got[...],
            r.e_keep,
            r.e_send,
        )
        r.put(e_send=None, e_keep=None)

    piece = ((two, share, half), BF16, DMA)
    hid = run(
        hidden_grads,
        dict(
            df=(fw.df, DMA),
            pperm=(project_perm, DMA),
            df_got=(df_got, DMA),
            act_keep=(fw.act_keep, DMA),
            act_got=(act_got, DMA),
            x2b=(fw.x2b, DMA),
            eperm=(expand_perm, DMA),
            x2b_got=(x2b_got, DMA),
            dh_keep=(fw.dh_keep, DMA),
            dh_got=(dh_got, DMA),
        ),
        dict(p_keep=piece, p_send=piece, e_keep=piece, e_send=piece),
        microseconds=4.0,
    )

    def row_place(steps, relative, y):
        place_of = 0
        for axis, bit in steps:
            place_of = 2 * place_of + (y if axis == "pb" else relative // bit % 2)
        return place_of

    def pack(r, grad, region, offset):
        base, steps, size = region
        index, here = lax.axis_index("pb"), lax.axis_index("ba")
        for relative in range(ba_size):
            for y in range(two):
                first = base + row_place(steps, relative, y) * size + offset
                for c, target in ((0, r.keep), (1, r.send)):
                    source = pl.multiple_of((here ^ relative) * block, 8)
                    column = pl.multiple_of((index ^ (2 * y + c)) * lanes, 128)
                    target[first : first + block, :] = grad[pl.ds(source, block), pl.ds(column, lanes)].astype(BF16)

    later = [("pb", 2)] + [("ba", bit) for bit in ba_bits[2:]]
    x_first = [("ba", ba_bits[0]), ("ba", ba_bits[1])] + later
    z_first = [("ba", ba_bits[1]), ("ba", ba_bits[0])] + later
    copies = ba_size * two
    pair_size = 2 * block
    embed_size = pair_size + slot
    cross_regions = ((0, x_first, pair_size), (copies * pair_size, z_first, pair_size))
    self_regions = ((0, x_first, embed_size), (copies * embed_size, z_first, pair_size))
    vector_count = 13 * width + hidden
    extra = padded_to(vector_count // 128, 16)
    cross_packed = (copies * 2 * pair_size, lanes)
    self_packed = (copies * (embed_size + pair_size) + extra, lanes)

    def attend_back(r, queries, grads, keys, values, kept, inverse, scores, logit, item, grad_keys, grad_values):
        results = []
        for g in range(groups):
            cols = slice(g * wide, (g + 1) * wide)
            big = slice(g * many, (g + 1) * many)
            back = inverse[item, 0:1, big]
            upright = jnp.broadcast_to(back, (128, many)).T
            scaled = jnp.concatenate(
                [
                    (
                        grads[:, cols].astype(F32)
                        * upright[h * rows : (h + 1) * rows, 0:1]
                    ).astype(BF16)
                    for h in range(GROUP_HEADS)
                ],
                axis=0,
            )
            lane = lax.broadcasted_iota(jnp.int32, (1, wide), 1) // head
            spread = jnp.concatenate(
                [
                    scaled[h * rows : (h + 1) * rows] * (lane == h).astype(F32).astype(BF16)
                    for h in range(GROUP_HEADS)
                ],
                axis=0,
            )
            scores[...] = nt(values(cols), spread)
            inner = jnp.sum(kept[item, :, big].astype(F32) * scores[...], axis=0, keepdims=True)
            logit[...] = (kept[item, :, big].astype(F32) * (scores[...] - inner * back)).astype(BF16)
            grad_values(cols, nn(kept[item, :, big], spread))
            grad_keys(cols, nn(logit[...], spread_heads(queries[:, cols], head)))
            results.append(diagonal(tn(keys(cols), logit[...]), head, rows))
        return jnp.concatenate(results, axis=0).T * scale

    def cross_back(r):
        grad = r.dr3[...] + nt(r.dh[...], r.we[...])
        sums = r.sums
        sums[...] = jnp.zeros(sums.shape, F32)
        unit = r.unit2[...]
        sums[0:1, :] = column_sum(grad * unit)
        sums[1:2, :] = column_sum(grad)
        dr2 = norm_backward(grad, unit, r.spread2[...], vector(r, G2))
        r.put(dr2=dr2)
        branch = dr2.astype(BF16)
        sums[2:3, :] = column_sum(branch)
        r.put(ds2=branch)
        r.do2[...] = nt(branch, r.wco[...]).astype(BF16)
        for i in range(own):
            span_rows = slice(i * rows, (i + 1) * rows)

            def grad_keys(cols, value):
                r.dk[i, :, cols] = value.astype(BF16)

            def grad_values(cols, value):
                r.dv[i, :, cols] = value.astype(BF16)

            result = attend_back(
                r,
                r.q2[span_rows, :],
                r.do2[span_rows, :],
                lambda cols: r.keys[i, :, cols],
                lambda cols: r.values[i, :, cols],
                r.e2,
                r.inv2,
                r.scores,
                r.logit,
                i,
                grad_keys,
                grad_values,
            )
            r.dq[span_rows, :] = result.astype(BF16)
        r.put(dk=None, dv=None, dq=None)
        sums[3:4, :] = column_sum(r.dq[...])
        total = jnp.zeros((1, width), F32)
        for i in range(own):
            total = total + column_sum(r.dv[i])
        sums[4:5, :] = total
        r.put(sums=None)
        r.put(dc=nt(r.dq[...], r.wcq[...]))

    p_got = swap(hid.p_send, "ba", ba_bits[0])
    e_got = swap(hid.e_send, "ba", ba_bits[1])
    out_across = swap(fw.far, "pb", 2)
    back = run(
        cross_back,
        dict(
            vectors=(vectors, VM),
            dh=(fw.dh, DMA),
            we=(expand_weight, DMA),
            dr3=(tie(fw.dr3, hid.p_send, hid.e_send), DMA),
            unit2=(fw.unit2, DMA),
            spread2=(fw.spread2, DMA),
            wco=(cross_out, DMA),
            values=(memory_values, DMA),
            inv2=(fw.inv2, DMA),
            e2=(fw.e2, DMA),
            q2=(fw.q2, DMA),
            keys=(memory_keys, DMA),
            wcq=(cross_query, DMA),
        ),
        dict(
            dq=((all_rows, width), BF16, DMA),
            dc=((all_rows, width), F32, DMA),
            dk=((own, span, width), BF16, DMA),
            dv=((own, span, width), BF16, DMA),
            dr2=((all_rows, width), F32, DMA),
            ds2=((all_rows, width), BF16, DMA),
            sums=((8, width), F32, DMA),
        ),
        dict(do2=((all_rows, width), BF16), scores=((span, many), F32), logit=((span, many), BF16)),
        microseconds=14.0,
    )


    def self_back(r):
        grad = r.dr2[...] + r.dc[...]
        sums = r.sums
        sums[...] = jnp.zeros(sums.shape, F32)
        unit = r.unit1[...]
        sums[0:1, :] = column_sum(grad * unit)
        sums[1:2, :] = column_sum(grad)
        first = r.first
        first[...] = norm_backward(grad, unit, r.spread1[...], vector(r, G1))
        branch = first[...].astype(BF16)
        sums[2:3, :] = column_sum(branch)
        whole = r.grad
        whole[...] = tn(r.o1[...], branch)
        pack(r, whole, self_regions[1], block)
        r.do1[...] = nt(branch, r.wo[...]).astype(BF16)
        for i in range(own):
            span_rows = slice(i * rows, (i + 1) * rows)

            def grad_keys(cols, value):
                r.dk[span_rows, cols] = value.astype(BF16)

            def grad_values(cols, value):
                r.dv[span_rows, cols] = value.astype(BF16)

            result = attend_back(
                r,
                r.q1[span_rows, :],
                r.do1[span_rows, :],
                lambda cols: r.k1[span_rows, cols],
                lambda cols: r.v1[span_rows, cols],
                r.e1,
                r.inv1,
                r.scores,
                r.logit,
                i,
                grad_keys,
                grad_values,
            )
            r.dq[span_rows, :] = result.astype(BF16)
        dq, dk, dv = r.dq[...], r.dk[...], r.dv[...]
        sums[3:4, :] = column_sum(dq)
        sums[4:5, :] = column_sum(dv)
        both = nt(dq, r.wq[...]) + nt(dk, r.wk[...])
        low = (first[...] + both + nt(dv, r.wv[...])).astype(BF16)
        for k in range(group):
            for i in range(own):
                (r.near[k] if k < 2 else r.far.at[k - 2])[i] = low[i * rows + k * slot : i * rows + (k + 1) * slot, :]
        r.put(near=0)
        r.put(near=1)
        r.put(far=None)
        both = both + r.dc[...]
        embed = both[0:rows]
        for i in range(1, own):
            embed = embed + both[i * rows : (i + 1) * rows]
        embed = nn(embed.astype(BF16), r.perm[...]).astype(BF16)
        order_bits = project_order
        for position in range(ba_size):
            relative = sum(((position >> (len(order_bits) - 1 - b)) & 1) * bit for b, bit in enumerate(order_bits))
            for y in range(two):
                first = row_place(x_first, relative, y) * embed_size + pair_size
                for c, target in ((0, r.keep), (1, r.send)):
                    k = 2 * y + c
                    piece = embed[k * slot : (k + 1) * slot, position * block : (position + 1) * block]
                    filled = jnp.concatenate([piece, jnp.zeros((slot, lanes - block), BF16)], axis=1)
                    target[first : first + slot, :] = filled
        table_rows = r.rows
        table_rows[...] = jnp.zeros(table_rows.shape, F32)
        sources = [
            (sums, 3),
            (sums, 4),
            (sums, 2),
            (sums, 0),
            (sums, 1),
            (r.sums_s, 3),
            (r.sums_s, 4),
            (r.sums_s, 2),
            (r.sums_s, 0),
            (r.sums_s, 1),
            (r.sums_f, 2),
            (r.sums_f, 0),
            (r.sums_f, 1),
        ] + [(r.hidden_sum, None)]
        filled_rows = 0
        for source, place_of in sources:
            place_of = place_of or 0
            for j in range(source.shape[1] // 128):
                table_rows[filled_rows : filled_rows + 1, :] = source[place_of : place_of + 1, j * 128 : (j + 1) * 128]
                filled_rows += 1
        low_rows = table_rows[...].astype(BF16)
        r.keep[self_packed[0] - extra :, :] = low_rows
        r.send[self_packed[0] - extra :, :] = low_rows
        for matrix, left, right in ((0, r.a_in, dq), (1, r.a_in, dk), (2, r.x0, dv)):
            whole[...] = tn(left[...], right)
            pack(r, whole, self_regions[matrix // 2], matrix % 2 * block)
        r.put(send=None, keep=None)

    p_got, e_got, out_across, dr2, near = meet(p_got, e_got, out_across, back.dr2, fw.near[1])

    p_keep, p_send = halves(pair_sum(hid.p_keep, p_got), 0)
    e_keep, e_send = halves(pair_sum(hid.e_keep, e_got), -1)
    p_got = swap(p_send, "pb", 2)
    e_got = swap(e_send, "ba", ba_bits[0])
    out_other = swap(near, "pb", 1)
    out_last = swap(out_across[1], "pb", 1)
    slf = run(
        self_back,
        dict(
            vectors=(vectors, VM),
            dr2=(tie(dr2, p_send, e_send), DMA),
            dc=(back.dc, DMA),
            unit1=(fw.unit1, DMA),
            spread1=(fw.spread1, DMA),
            o1=(fw.o1, DMA),
            wo=(self_out, DMA),
            inv1=(fw.inv1, DMA),
            e1=(fw.e1, DMA),
            q1=(fw.q1, DMA),
            k1=(fw.k1, DMA),
            v1=(fw.v1, DMA),
            wq=(self_query, DMA),
            wk=(self_key, DMA),
            wv=(self_value, DMA),
            a_in=(fw.a_in, DMA),
            x0=(fw.x0, DMA),
            perm=(project_perm, DMA),
            sums_s=(back.sums, DMA),
            sums_f=(fw.sums, DMA),
            hidden_sum=(fw.hidden_sum, DMA),
        ),
        dict(
            keep=(self_packed, BF16, DMA),
            send=(self_packed, BF16, DMA),
            near=([(own, slot, width)] * 2, BF16, DMA),
            far=((2, own, slot, width), BF16, DMA),
        ),
        dict(
            sums=((8, width), F32),
            rows=((extra, 128), F32),
            first=((all_rows, width), F32),
            grad=((width, width), F32),
            do1=((all_rows, width), BF16),
            dq=((all_rows, width), BF16),
            dk=((all_rows, width), BF16),
            dv=((all_rows, width), BF16),
            scores=((rows, many), F32),
            logit=((rows, many), BF16),
        ),
        microseconds=7.0,
    )
    p_got, e_got, out_other, out_last, far = meet(p_got, e_got, out_other, out_last, slf.far)

    p_keep, p_send = halves(pair_sum(p_keep, p_got), -1)
    e_keep, e_send = halves(pair_sum(e_keep, e_got), 0)
    p_got = swap(p_send, "ba", ba_bits[1])
    e_got = swap(e_send, "pb", 2)
    s_got = swap(slf.send, "pb", 1)
    grad_across = swap(far, "pb", 2)

    def cross_memory(r):
        index = lax.axis_index("pb")
        for k in (3, 2, 1, 0):
            first = pl.multiple_of((index ^ k) * part, 16)
            for i in range(own):
                edge = pl.ds(first, part)
                value = nt(r.dk[i, edge, :], r.wck[...]) + nt(r.dv[i, edge, :], r.wcv[...])
                if k < 2:
                    r.near[k][i] = value.astype(BF16)
                else:
                    r.far[(k - 2) * own + i][...] = value.astype(BF16)
                    r.put(far=(k - 2) * own + i)
            if k < 2:
                r.put(near=k)

    mem = run(
        cross_memory,
        dict(
            wck=(cross_key, DMA),
            wcv=(cross_value, DMA),
            dk=(tie(back.dk, p_send, e_send), DMA),
            dv=(back.dv, DMA),
        ),
        dict(near=([(own, part, width)] * 2, BF16, DMA), far=([(part, width)] * (2 * own), BF16, DMA)),
        microseconds=5.0,
    )
    p_got, e_got, s_got, grad_across, mem_first = meet(p_got, e_got, s_got, grad_across, mem.far[2])

    whole = pair_sum(slf.keep, s_got)
    first_rows, second_rows = copies * embed_size, copies * pair_size
    a_keep, a_send = row_halves(
        jnp.concatenate([whole[:first_rows], whole[first_rows + second_rows :]]), extra
    )
    b_keep, b_send = row_halves(whole[first_rows : first_rows + second_rows], 0)
    p_keep, p_send = halves(pair_sum(p_keep, p_got), -1)
    e_keep, e_send = halves(pair_sum(e_keep, e_got), -1)
    a_got = swap(a_send, "ba", ba_bits[0])
    b_got = swap(b_send, "ba", ba_bits[1])
    p_got = swap(p_send, "ba", ba_bits[2])
    e_got = swap(e_send, "ba", ba_bits[2])
    mem_got = [swap(mem_first, "pb", 2)]

    def cross_weights(r):
        grad = r.grad
        grad[...] = tn(r.o2[...], r.ds2[...])
        pack(r, grad, cross_regions[1], 1 * block)
        grad[...] = tn(r.c_in[...], r.dq[...])
        pack(r, grad, cross_regions[0], 0 * block)
        grad[...] = tn(r.plain[0], r.dv[0])
        for i in range(1, own):
            grad[...] += tn(r.plain[i], r.dv[i])
        pack(r, grad, cross_regions[1], 0 * block)
        grad[...] = tn(r.keyed[0], r.dk[0])
        for i in range(1, own):
            grad[...] += tn(r.keyed[i], r.dk[i])
        pack(r, grad, cross_regions[0], 1 * block)
        r.put(send=None, keep=None)

    crs = run(
        cross_weights,
        dict(
            o2=(fw.o2, DMA),
            ds2=(back.ds2, DMA),
            c_in=(fw.c_in, DMA),
            dq=(tie(back.dq, p_send, e_send, a_send, b_send), DMA),
            dv=(back.dv, DMA),
            plain=(plain, DMA),
            dk=(back.dk, DMA),
            keyed=(keyed, DMA),
        ),
        dict(keep=(cross_packed, BF16, DMA), send=(cross_packed, BF16, DMA)),
        dict(grad=((width, width), F32)),
        microseconds=8.0,
    )
    a_got, b_got, p_got, e_got, mem_got[0], mem_first, grad_last, c_send = meet(
        a_got, b_got, p_got, e_got, mem_got[0], mem.far[3], grad_across[1], crs.send
    )

    lane_halves = lambda total: halves(total, -1)
    project_out = finish(pair_sum(p_keep, p_got), ba_bits[3:], lane_halves)
    expand_out = finish(pair_sum(e_keep, e_got), ba_bits[3:], lane_halves)
    a_keep, a_send = row_halves(pair_sum(a_keep, a_got), extra)
    b_keep, b_send = row_halves(pair_sum(b_keep, b_got), 0)
    c_got = swap(c_send, "pb", 1)
    a_got = swap(a_send, "ba", ba_bits[1])
    b_got = swap(b_send, "ba", ba_bits[0])
    mem_got.append(swap(mem_first, "pb", 2))
    grad_last = swap(grad_last, "pb", 1)
    c_got, a_got, b_got, mem_got[1], grad_last, mem_first, near = meet(
        c_got, a_got, b_got, mem_got[1], grad_last, mem.far[0], slf.near[1]
    )

    whole = pair_sum(crs.keep, c_got)
    ca_keep, ca_send = row_halves(whole[:second_rows], 0)
    cb_keep, cb_send = row_halves(whole[second_rows:], 0)
    s_keep, s_send = row_halves(
        interleave(pair_sum(a_keep, a_got), pair_sum(b_keep, b_got), embed_size, pair_size, extra), extra
    )
    ca_got = swap(ca_send, "ba", ba_bits[0])
    cb_got = swap(cb_send, "ba", ba_bits[1])
    s_got = swap(s_send, "pb", 2)
    mem_got.append(swap(mem_first, "pb", 2))
    grad_other = swap(near, "pb", 1)
    ca_got, cb_got, s_got, mem_got[2], grad_other, mem_first, near = meet(
        ca_got, cb_got, s_got, mem_got[2], grad_other, mem.far[1], mem.near[1]
    )

    ca_keep, ca_send = row_halves(pair_sum(ca_keep, ca_got), 0)
    cb_keep, cb_send = row_halves(pair_sum(cb_keep, cb_got), 0)
    s_keep, s_send = row_halves(pair_sum(s_keep, s_got), extra)
    ca_got = swap(ca_send, "ba", ba_bits[1])
    cb_got = swap(cb_send, "ba", ba_bits[0])
    s_got = swap(s_send, "ba", ba_bits[2])
    mem_got.append(swap(mem_first, "pb", 2))
    mem_other = swap(near, "pb", 1)
    def placed(parts, across, count, *before):
        def place_rows(r):
            index = lax.axis_index("pb")
            for k in range(group):
                for i in range(own):
                    source = (r.mine, r.other, r.across, r.last)[k]
                    piece = source[i][0:count, :] if isinstance(source, Numbered) else source[i, 0:count, :]
                    r.wide[:, (index ^ k) * own + i, :] = piece.astype(F32)
            r.put(whole=r.wide[...].astype(BF16))

        made = run(
            place_rows,
            dict(
                mine=(tie(parts[0], *before), DMA),
                other=(parts[1], DMA),
                across=(list(across), DMA) if isinstance(across, list) else (across, DMA),
                last=(list(parts[2]), DMA) if isinstance(parts[2], list) else (parts[2], DMA),
            ),
            dict(whole=((count, items, width), BF16, DMA)),
            dict(wide=((count, items, width), F32)),
            microseconds=2.0,
        )
        return made.whole.transpose(1, 0, 2)

    input_grad = placed(
        (slf.near[0], grad_other, grad_last), grad_across[0], chunk, ca_send, cb_send, s_send, mem_first, near
    )
    ca_got, cb_got, s_got, mem_got[3], mem_other, mem_got[0], mem_got[1], input_grad = meet(
        ca_got, cb_got, s_got, mem_got[3], mem_other, mem_got[0], mem_got[1], input_grad
    )

    row_cut = lambda total: row_halves(total, extra)
    self_outs = finish(pair_sum(s_keep, s_got), ba_bits[3:], row_cut)
    c_keep, c_send = row_halves(
        interleave(pair_sum(ca_keep, ca_got), pair_sum(cb_keep, cb_got), pair_size, pair_size, 0), 0
    )
    c_got = swap(c_send, "pb", 2)
    mem_last = [swap(piece, "pb", 1) for piece in mem_got[:2]]
    layer_output = placed((fw.near[0], out_other, out_last), out_across[0], chunk, c_send, mem_got[0], mem_got[1])
    c_got, mem_last[0], mem_last[1], layer_output = meet(c_got, mem_last[0], mem_last[1], layer_output)

    c_keep, c_send = row_halves(pair_sum(c_keep, c_got), 0)
    c_got = swap(c_send, "ba", ba_bits[2])
    memory_grad = placed((mem.near[0], mem_other, mem_last), mem_got[2:], quarter, c_send)
    cross_outs = finish(pair_sum(c_keep, c_got), ba_bits[3:], lambda total: row_halves(total, 0))

    summands = self_outs[self_outs.shape[0] - extra :].reshape(-1)[:vector_count]
    vecs = [summands[j * width : (j + 1) * width] for j in range(13)]
    expand_bias_out = summands[13 * width :]

    def square(outs, matrix):
        return outs[matrix * block : (matrix + 1) * block]

    return (
        layer_output,
        input_grad,
        memory_grad,
        self_outs[pair_size : pair_size + chunk, :block],
        square(self_outs, 0),
        vecs[0],
        square(self_outs, 1),
        self_outs[embed_size : embed_size + block],
        vecs[1],
        self_outs[embed_size + block : embed_size + 2 * block],
        vecs[2],
        vecs[3],
        vecs[4],
        square(cross_outs, 0),
        vecs[5],
        square(cross_outs, 1),
        square(cross_outs, 2),
        vecs[6],
        square(cross_outs, 3),
        vecs[7],
        vecs[8],
        vecs[9],
        expand_out.T,
        expand_bias_out,
        project_out,
        vecs[10],
        vecs[11],
        vecs[12],
    )


def solution(mesh):
    rows = P("ba", "pb", None)
    copied = P()
    placed = (rows, P("ba", None, None), P("ba"), P("pb", None)) + (copied,) * 24 + (rows,)
    square = P("ba", "pb")
    return jax.shard_map(
        local,
        mesh=mesh,
        in_specs=placed,
        out_specs=(
            rows,
            rows,
            rows,
            P("pb", "ba"),
            square,
            copied,
            square,
            square,
            copied,
            square,
            copied,
            copied,
            copied,
            square,
            copied,
            square,
            square,
            copied,
            square,
            copied,
            copied,
            copied,
            square,
            copied,
            P("pb", "ba"),
            copied,
            copied,
            copied,
        ),
        check_vma=False,
    )
```

```python
import math

import jax
import jax.numpy as jnp
import numpy as np
from jax import lax
from jax.experimental import pallas as pl
from jax.experimental.pallas import tpu as pltpu
from jax.sharding import PartitionSpec as P

HEADS = 8
GROUP_HEADS = 4
F32 = jnp.float32
BF16 = jnp.bfloat16
HIDDEN_CHUNKS = 5
VMEM_BYTES = 58 * 2**20


def sinusoid(count, model_width):
    position = np.arange(count, dtype=np.float32)
    column = np.arange(model_width // 2, dtype=np.float32)
    frequency = np.exp(column * np.float32(-2.0 * math.log(10000.0) / model_width)).astype(np.float32)
    angles = (position[:, None] * frequency[None, :]).astype(np.float32)
    table = np.stack([np.sin(angles), np.cos(angles)], axis=-1)
    return table.reshape(count, model_width).astype(np.float32)


def padded_to(extent, multiple):
    return -(-extent // multiple) * multiple


def nn(left, right):
    return lax.dot_general(left, right, (((1,), (0,)), ((), ())), preferred_element_type=F32)


def nt(left, right):
    return lax.dot_general(left, right, (((1,), (1,)), ((), ())), preferred_element_type=F32)


def tn(left, right):
    return lax.dot_general(left, right, (((0,), (0,)), ((), ())), preferred_element_type=F32)


VM, SM, DMA, OWN = range(4)


class Named:
    def __init__(self, find):
        self.find = find

    def __getattr__(self, key):
        return self.find(key)


class Numbered:
    def __init__(self, find, key):
        self.find, self.key = find, key

    def __getitem__(self, place):
        return self.find((self.key, place))


def flat(entries):
    result = {}
    for key, (value, *rest) in entries.items():
        if isinstance(value, list):
            for place, member in enumerate(value):
                result[(key, place)] = (member, *rest)
        else:
            result[key] = (value, *rest)
    return result


def run(body, ins, outs, scratch=None, after=(), microseconds=5.0, spare=64):
    listed = {key for entries in (ins, outs) for key, entry in entries.items() if isinstance(entry[0], list)}
    ins, outs, scratch = flat(ins), flat(outs), scratch or {}
    in_dma = [key for key, entry in ins.items() if entry[1] in (DMA, OWN)]
    out_dma = [key for key, entry in outs.items() if entry[2] == DMA]

    def kernel(*refs):
        refs = list(refs)
        held = {key: refs.pop(0) for key in ins}
        del refs[: len(after)]
        results = {key: refs.pop(0) for key in outs}
        arrived = {key: refs.pop(0) for key in in_dma}
        leaving = {key: refs.pop(0) for key in out_dma}
        held.update(results)
        sources = {key: held[key] for key in in_dma}
        held.update(arrived)
        held.update(leaving)
        held.update({key: refs.pop(0) for key in scratch})
        in_sem, out_sem, part_sem = refs
        pending = {}
        for place, key in enumerate(in_dma):
            source = sources[key]
            if ins[key][1] == OWN:
                count = arrived[key].shape[0]
                source = source.at[pl.ds(lax.axis_index("pb") * count, count)]
            pending[key] = pltpu.make_async_copy(source, arrived[key], in_sem.at[place])
            pending[key].start()
        started = {}

        def find(key):
            if key in listed:
                return Numbered(find, key)
            if key in pending:
                pending.pop(key).wait()
            return held[key]

        def put(**values):
            for key, value in values.items():
                if key in listed:
                    key = (key, value)
                elif value is not None:
                    held[key][...] = value
                if key in leaving:
                    place = out_dma.index(key)
                    started[key] = pltpu.make_async_copy(leaving[key], results[key], out_sem.at[place])
                    started[key].start()

        def put_part(part, **values):
            for key in values:
                place = out_dma.index(key)
                copy = pltpu.make_async_copy(leaving[key].at[part], results[key].at[part], part_sem.at[place, part])
                copy.start()
                started[(key, part)] = copy
                started[key] = copy

        bag = Named(find)
        bag.put = put
        bag.put_part = put_part
        body(bag)
        for key in list(pending):
            pending.pop(key).wait()
        for key in out_dma:
            assert key in started, key
        for copy in {id(copy): copy for copy in started.values()}.values():
            copy.wait()

    spaces = [pltpu.VMEM, pltpu.SMEM, pl.ANY, pl.ANY]
    arrays = [entry[0] for entry in ins.values()]
    nbytes = sum(int(np.prod(array.shape)) * array.dtype.itemsize for array in arrays)
    held_bytes = sum(
        int(np.prod(shape)) * (4 if dtype == F32 else 2)
        for shape, dtype in [(entry[0].shape, entry[0].dtype) for entry in ins.values()]
        + [(entry[0], entry[1]) for entry in outs.values()]
        + list(scratch.values())
    )
    made = pl.pallas_call(
        kernel,
        out_shape=[jax.ShapeDtypeStruct(entry[0], entry[1]) for entry in outs.values()],
        in_specs=[pl.BlockSpec(memory_space=spaces[entry[1]]) for entry in ins.values()]
        + [pl.BlockSpec(memory_space=pl.ANY)] * len(after),
        out_specs=[pl.BlockSpec(memory_space=spaces[entry[2]]) for entry in outs.values()],
        scratch_shapes=[
            pltpu.VMEM(
                (ins[key][0].shape[0] // lax.axis_size("pb"), *ins[key][0].shape[1:])
                if ins[key][1] == OWN
                else ins[key][0].shape,
                ins[key][0].dtype,
            )
            for key in in_dma
        ]
        + [pltpu.VMEM(outs[key][0], outs[key][1]) for key in out_dma]
        + [pltpu.VMEM(shape, dtype) for shape, dtype in scratch.values()]
        + [pltpu.SemaphoreType.DMA((max(1, len(in_dma)),)), pltpu.SemaphoreType.DMA((max(1, len(out_dma)),)), pltpu.SemaphoreType.DMA((max(1, len(out_dma)), 2))],
        compiler_params=pltpu.CompilerParams(vmem_limit_bytes=min(VMEM_BYTES, held_bytes + spare * 2**20)),
        cost_estimate=pl.CostEstimate(
            flops=int(microseconds * 1e3), bytes_accessed=1024, transcendentals=0
        ),
        name=body.__name__,
    )(*arrays, *after)
    by_key = dict(zip(outs, made))

    def result(key):
        if key in listed:
            return [value for name, value in by_key.items() if isinstance(name, tuple) and name[0] == key]
        return by_key[key]

    return Named(result)


def norm_forward(values, gain, shift):
    average = jnp.mean(values, axis=-1, keepdims=True)
    centred = values - average
    spread = jnp.mean(centred * centred, axis=-1, keepdims=True)
    scale = lax.rsqrt(spread + 1e-05)
    unit = centred * scale
    return unit, scale, unit * gain + shift


def norm_backward(grad, unit, scale, gain):
    lifted = grad * gain
    first = jnp.mean(lifted, axis=-1, keepdims=True)
    second = jnp.mean(lifted * unit, axis=-1, keepdims=True)
    return scale * (lifted - first - unit * second)


def column_sum(values):
    return jnp.sum(values.astype(F32), axis=0, keepdims=True)


def spread_heads(rows, width):
    count, columns = rows.shape
    lane = lax.broadcasted_iota(jnp.int32, (1, columns), 1) // width
    return jnp.concatenate(
        [rows * (lane == h).astype(F32).astype(BF16) for h in range(columns // width)], axis=0
    )


def diagonal(blocks, width, count):
    heads = blocks.shape[0] // width
    return jnp.concatenate(
        [blocks[h * width : (h + 1) * width, h * count : (h + 1) * count] for h in range(heads)], axis=0
    )


def swap(values, axis, bit):
    size = lax.axis_size(axis)
    return lax.ppermute(values, axis, [(i, i ^ bit) for i in range(size)])


def bits_of(size):
    return [1 << b for b in range(size.bit_length() - 1)]


def exchange(values, axis):
    size = lax.axis_size(axis)
    return [values[0]] + [swap(values[k], axis, k) for k in range(1, size)]


def pair_sum(kept, got):
    return kept.astype(F32) + got.astype(F32)


def meet(*arrays):
    return lax.optimization_barrier(arrays)


def tie(values, *before):
    return lax.optimization_barrier((values, *before))[0]


def halves(values, dim):
    dim = dim % values.ndim
    if values.shape[dim] == 2:
        parts = [lax.index_in_dim(values, j, dim, keepdims=False) for j in range(2)]
    else:
        half = values.shape[dim] // 2
        parts = [lax.slice_in_dim(values, j * half, (j + 1) * half, axis=dim) for j in range(2)]
    return parts[0].astype(BF16), parts[1].astype(BF16)


def row_halves(total, extra):
    body = total.shape[0] - extra
    parts = [total[: body // 2], total[body // 2 : body]]
    if extra:
        parts = [jnp.concatenate([part, total[body:]]) for part in parts]
    return parts[0].astype(BF16), parts[1].astype(BF16)


def finish(total, bits, split):
    for bit in bits:
        kept, sent = split(total)
        total = pair_sum(kept, swap(sent, "ba", bit))
    return total


def interleave(first, second, first_size, second_size, extra):
    count = second.shape[0] // second_size
    body = jnp.concatenate(
        [
            first[: count * first_size].reshape(count, first_size, -1),
            second.reshape(count, second_size, -1),
        ],
        axis=1,
    )
    return jnp.concatenate([body.reshape(count * (first_size + second_size), -1), first[count * first_size :]])


def permutation(order, model_width, ba_size, mine):
    width = model_width // ba_size
    column = lax.broadcasted_iota(jnp.int32, (1, model_width), 1)
    position = column // width
    relative = jnp.zeros_like(column)
    for step, bit in enumerate(order):
        digit = (position >> (len(order) - 1 - step)) & 1
        relative = relative + digit * bit
    source = (relative ^ mine) * width + column % width
    row = lax.broadcasted_iota(jnp.int32, (model_width, model_width), 0)
    return (row == source).astype(BF16)


def local(
    decoder_input,
    memory,
    lengths,
    query_embed,
    self_query,
    self_query_bias,
    self_key,
    self_value,
    self_value_bias,
    self_out,
    self_out_bias,
    norm_one_gain,
    norm_one_bias,
    cross_query,
    cross_query_bias,
    cross_key,
    cross_value,
    cross_value_bias,
    cross_out,
    cross_out_bias,
    norm_two_gain,
    norm_two_bias,
    expand_weight,
    expand_bias,
    project_weight,
    project_bias,
    norm_three_gain,
    norm_three_bias,
    out_cotangent,
):
    items, chunk, width = decoder_input.shape
    tokens = memory.shape[1]
    hidden = expand_weight.shape[1]
    group = lax.axis_size("pb")
    ba_size = lax.axis_size("ba")
    place = lax.axis_index("pb")
    mine = lax.axis_index("ba")
    own = items // group
    quarter = tokens // group
    slot = padded_to(chunk, 32)
    rows = group * slot
    all_rows = own * rows
    part = padded_to(quarter, 16)
    span = group * part
    head = width // HEADS
    scale = head ** (-0.5)
    share = hidden // group
    step = hidden // HIDDEN_CHUNKS
    wide = GROUP_HEADS * head
    many = GROUP_HEADS * rows
    groups = HEADS // GROUP_HEADS
    ba_bits = bits_of(ba_size)
    block = width // ba_size
    lanes = width // group


    def prepare(r):
        index = lax.axis_index("pb")
        r.wide_x[...] = r.x[...].astype(F32)
        r.wide_g[...] = r.g[...].astype(F32)
        for k in range(group):
            source = (index ^ k) * own
            piece = r.rows[k]
            piece[...] = jnp.zeros(piece.shape, BF16)
            for i in range(own):
                piece[i, 0:chunk, :] = r.wide_x[:, source + i, :].astype(BF16)
                piece[own + 1 + i, 0:chunk, :] = r.wide_g[:, source + i, :].astype(BF16)
            piece[own, 0:chunk, :] = r.e[...]

    prepared = run(
        prepare,
        dict(
            x=(decoder_input.transpose(1, 0, 2), VM),
            e=(query_embed, VM),
            g=(out_cotangent.transpose(1, 0, 2), VM),
        ),
        dict(rows=([(2 * own + 1, slot, width)] * group, BF16, VM)),
        dict(wide_x=((chunk, items, width), F32), wide_g=((chunk, items, width), F32)),
        microseconds=1.0,
    )
    row_parts = exchange(prepared.rows, "pb")

    table = np.zeros((group, part, width), np.float32)
    table[:, :quarter] = sinusoid(tokens, width).reshape(group, quarter, width)
    table = jnp.asarray(table.reshape(span, width))

    def project_memory(r):
        for i in range(own):
            source = r.memory[i]
            for q in range(group):
                r.plain[i, q * part : q * part + quarter, :] = source[q * quarter : (q + 1) * quarter, :]
                if part > quarter:
                    r.plain[i, q * part + quarter : (q + 1) * part, :] = jnp.zeros((part - quarter, width), BF16)
            r.keyed[i] = (r.plain[i].astype(F32) + r.table[...]).astype(BF16)
            r.keys[i] = nn(r.keyed[i], r.wk[...]).astype(BF16)
            r.put_part(i, keys=None, keyed=None)
            r.values[i] = (nn(r.plain[i], r.wv[...]) + r.bv[...].astype(F32).reshape(1, width)).astype(BF16)
            r.put_part(i, values=None, plain=None)

    memory_block = ((own, span, width), BF16, DMA)
    prj = run(
        project_memory,
        dict(
            memory=(memory, OWN),
            table=(table, DMA),
            wk=(cross_key, DMA),
            wv=(cross_value, DMA),
            bv=(cross_value_bias, VM),
        ),
        dict(keys=memory_block, values=memory_block, keyed=memory_block, plain=memory_block),
        after=prepared.rows[:1],
        microseconds=7.0,
    )
    memory_keys, memory_values, keyed, plain = prj.keys, prj.values, prj.keyed, prj.plain

    vectors = [
        self_query_bias,
        self_value_bias,
        self_out_bias,
        norm_one_gain,
        norm_one_bias,
        cross_query_bias,
        cross_out_bias,
        norm_two_gain,
        norm_two_bias,
        project_bias,
        norm_three_gain,
        norm_three_bias,
    ]
    BQ, BV, BO, G1, B1, BCQ, BCO, G2, B2, BP, G3, B3 = range(12)

    def vector(r, place):
        return r.vectors[place][...].astype(F32).reshape(1, width)

    def attend(r, queries, keys, values, kept, inverse, where_scores, item, mask):
        results = []
        count = where_scores.shape[0]
        for g in range(groups):
            cols = slice(g * wide, (g + 1) * wide)
            where_scores[...] = nt(keys(cols), spread_heads(queries[:, cols], head))
            mask(where_scores)
            scores = where_scores[...]
            highest = jnp.max(scores, axis=0, keepdims=True)
            raised = jnp.exp(scores - highest)
            total = jnp.sum(raised, axis=0, keepdims=True)
            kept[item, :, g * many : (g + 1) * many] = raised.astype(BF16)
            back = 1.0 / total
            inverse[item, :, g * many : (g + 1) * many] = jnp.broadcast_to(back, (8, many))
            mixed = tn(values(cols), kept[item, :, g * many : (g + 1) * many]) * back
            results.append(diagonal(mixed, head, rows))
        return jnp.concatenate(results, axis=0).T

    def forward(r):
        x_buf, e_buf = r.x0, r.embed
        for k in range(group):
            piece = r.rows[k]
            for i in range(own):
                x_buf[i * rows + k * slot : i * rows + (k + 1) * slot, :] = piece[i]
                e_buf[i * rows + k * slot : i * rows + (k + 1) * slot, :] = piece[own].astype(F32)
        r.put(x0=None)
        a_in = (x_buf[...].astype(F32) + e_buf[...]).astype(BF16)
        r.put(a_in=a_in)
        queries = (nn(a_in, r.wq[...]) + vector(r, BQ)).astype(BF16)
        r.put(q1=(queries.astype(F32) * scale).astype(BF16))
        r.put(k1=nn(a_in, r.wk[...]).astype(BF16))
        r.put(v1=(nn(x_buf[...], r.wv[...]) + vector(r, BV)).astype(BF16))

        def self_mask(scores):
            row = lax.broadcasted_iota(jnp.int32, (rows, 1), 0) % slot
            scores[...] = jnp.where(row < chunk, scores[...], -1e30)

        for i in range(own):
            span_rows = slice(i * rows, (i + 1) * rows)
            result = attend(
                r,
                r.q1[span_rows, :],
                lambda cols: r.k1[span_rows, cols],
                lambda cols: r.v1[span_rows, cols],
                r.e1,
                r.inv1,
                r.self_scores,
                i,
                self_mask,
            )
            r.o1[span_rows, :] = result.astype(BF16)
        r.put(e1=None)
        r.put(inv1=None)
        r.put(o1=None)
        summed = x_buf[...].astype(F32) + nn(r.o1[...], r.wo[...]) + vector(r, BO)
        unit, spread, normed = norm_forward(summed, vector(r, G1), vector(r, B1))
        r.put(unit1=unit)
        r.put(spread1=spread)
        r.normed[...] = normed
        r.put(c_in=(normed + e_buf[...]).astype(BF16))
        queries = (nn(r.c_in[...], r.wcq[...]) + vector(r, BCQ)).astype(BF16)
        r.put(q2=(queries.astype(F32) * scale).astype(BF16))
        for i in range(own):
            span_rows = slice(i * rows, (i + 1) * rows)
            length = r.lengths[lax.axis_index("pb") * own + i]

            def cross_mask(scores):
                if part > quarter:
                    low = quarter // 8 * 8
                    row = lax.broadcasted_iota(jnp.int32, (part - low, 1), 0) + low
                    for q in range(group):
                        edge = slice(q * part + low, (q + 1) * part)
                        scores[edge, :] = jnp.where(row < quarter, scores[edge, :], -1e30)

                @pl.when(length < tokens)
                def _():
                    for q in range(group):
                        row = lax.broadcasted_iota(jnp.int32, (part, 1), 0)
                        edge = slice(q * part, (q + 1) * part)
                        seen = (row + q * quarter < length) & (row < quarter)
                        scores[edge, :] = jnp.where(seen, scores[edge, :], -1e30)

            result = attend(
                r,
                r.q2[span_rows, :],
                lambda cols: r.keys[i, :, cols],
                lambda cols: r.values[i, :, cols],
                r.e2,
                r.inv2,
                r.cross_scores,
                i,
                cross_mask,
            )
            r.o2[span_rows, :] = result.astype(BF16)
        r.put(e2=None)
        r.put(inv2=None)
        r.put(o2=None)
        summed = r.normed[...] + nn(r.o2[...], r.wco[...]) + vector(r, BCO)
        unit, spread, normed = norm_forward(summed, vector(r, G2), vector(r, B2))
        r.put(unit2=unit)
        r.put(spread2=spread)
        r.normed[...] = normed
        r.put(x2b=normed.astype(BF16))
        r.third[...] = normed + vector(r, BP)
        for j in range(HIDDEN_CHUNKS):
            cols = slice(j * step, (j + 1) * step)
            before = nn(r.x2b[...], r.we[:, cols]) + r.be[cols].astype(F32).reshape(1, step)
            share_below = 0.5 + 0.5 * lax.erf(before * (0.5**0.5))
            density = jnp.exp(-0.5 * before * before) * ((2.0 * math.pi) ** (-0.5))
            r.slope[:, cols] = share_below + before * density
            active = (before * share_below).astype(BF16)
            r.third[...] += nn(active, r.wp[cols, :])
            r.active_t[cols, :] = active.T
        index = lax.axis_index("pb")

        def ship(source, kept, sent):
            for y in range(group // 2):
                for c, target in ((0, kept), (1, sent)):
                    first = pl.multiple_of((index ^ (2 * y + c)) * share, 16)
                    target[y] = source[pl.ds(first, share), :]

        ship(r.active_t, r.act_keep, r.act_send)
        r.put(act_send=None, act_keep=None)
        unit, spread, normed = norm_forward(r.third[...], vector(r, G3), vector(r, B3))
        low = normed.astype(BF16)
        cot = r.cot
        for k in range(group):
            piece = r.rows[k]
            for i in range(own):
                here = slice(i * rows + k * slot, i * rows + (k + 1) * slot)
                (r.near[k] if k < 2 else r.far.at[k - 2])[i] = low[here, :]
                cot[here, :] = piece[own + 1 + i].astype(F32)
        r.put(near=0)
        r.put(near=1)
        r.put(far=None)
        sums = r.sums
        sums[...] = jnp.zeros(sums.shape, F32)
        sums[0:1, :] = column_sum(cot[...] * unit)
        sums[1:2, :] = column_sum(cot[...])
        third = norm_backward(cot[...], unit, spread, vector(r, G3))
        r.put(dr3=third)
        branch = third.astype(BF16)
        r.put(df=branch)
        sums[2:3, :] = column_sum(branch)
        r.put(sums=None)
        for j in range(HIDDEN_CHUNKS):
            cols = slice(j * step, (j + 1) * step)
            grad = (nt(r.df[...], r.wp[cols, :]) * r.slope[:, cols]).astype(BF16)
            r.dh[:, cols] = grad
            r.hidden_sum[:, cols] = column_sum(grad)
            r.active_t[cols, :] = grad.T
        ship(r.active_t, r.dh_keep, r.dh_send)
        r.put(dh_send=None, dh_keep=None, dh=None, hidden_sum=None)

    two = group // 2
    fw = run(
        forward,
        dict(
            lengths=(lengths, SM),
            rows=(row_parts, VM),
            vectors=(vectors, VM),
            be=(expand_bias, VM),
            wq=(self_query, DMA),
            wk=(self_key, DMA),
            wv=(self_value, DMA),
            wo=(self_out, DMA),
            wcq=(cross_query, DMA),
            keys=(memory_keys, DMA),
            values=(memory_values, DMA),
            wco=(cross_out, DMA),
            we=(expand_weight, DMA),
            wp=(project_weight, DMA),
        ),
        dict(

            x0=((all_rows, width), BF16, DMA),
            a_in=((all_rows, width), BF16, DMA),
            q1=((all_rows, width), BF16, DMA),
            k1=((all_rows, width), BF16, DMA),
            v1=((all_rows, width), BF16, DMA),
            e1=((own, rows, groups * many), BF16, DMA),
            inv1=((own, 8, groups * many), F32, DMA),
            o1=((all_rows, width), BF16, DMA),
            unit1=((all_rows, width), F32, DMA),
            spread1=((all_rows, 1), F32, DMA),
            c_in=((all_rows, width), BF16, DMA),
            q2=((all_rows, width), BF16, DMA),
            e2=((own, span, groups * many), BF16, DMA),
            inv2=((own, 8, groups * many), F32, DMA),
            o2=((all_rows, width), BF16, DMA),
            unit2=((all_rows, width), F32, DMA),
            spread2=((all_rows, 1), F32, DMA),
            x2b=((all_rows, width), BF16, DMA),
            act_keep=((two, share, all_rows), BF16, DMA),
            act_send=((two, share, all_rows), BF16, DMA),
            dr3=((all_rows, width), F32, DMA),
            df=((all_rows, width), BF16, DMA),
            dh=((all_rows, hidden), BF16, DMA),
            dh_keep=((two, share, all_rows), BF16, DMA),
            dh_send=((two, share, all_rows), BF16, DMA),
            sums=((8, width), F32, DMA),
            hidden_sum=((1, hidden), F32, DMA),
        near=([(own, slot, width)] * 2, BF16, DMA),
            far=((2, own, slot, width), BF16, DMA),
        ),
        dict(
            embed=((all_rows, width), F32),
            self_scores=((rows, many), F32),
            cross_scores=((span, many), F32),
            normed=((all_rows, width), F32),
            third=((all_rows, width), F32),
            cot=((all_rows, width), F32),
            slope=((all_rows, hidden), F32),
            active_t=((hidden, all_rows), BF16),
        ),
        microseconds=18.0,
    )

    project_order = list(ba_bits)
    expand_order = [ba_bits[1], ba_bits[0]] + list(ba_bits[2:])
    project_perm = permutation(project_order, width, ba_size, mine)
    expand_perm = permutation(expand_order, width, ba_size, mine)
    half = width // 2

    def row_place(steps, relative, y):
        place_of = 0
        for axis, bit in steps:
            place_of = 2 * place_of + (y if axis == "pb" else relative // bit % 2)
        return place_of

    def pack(r, grad, region, offset):
        base, steps, size = region
        index, here = lax.axis_index("pb"), lax.axis_index("ba")
        for relative in range(ba_size):
            for y in range(two):
                first = base + row_place(steps, relative, y) * size + offset
                for c, target in ((0, r.keep), (1, r.send)):
                    source = pl.multiple_of((here ^ relative) * block, 8)
                    column = pl.multiple_of((index ^ (2 * y + c)) * lanes, 128)
                    target[first : first + block, :] = grad[pl.ds(source, block), pl.ds(column, lanes)].astype(BF16)

    later = [("pb", 2)] + [("ba", bit) for bit in ba_bits[2:]]
    copies = ba_size * two
    cross_size = 4 * block
    self_size = 4 * block + slot
    self_region = (0, [("ba", ba_bits[0]), ("ba", ba_bits[1])] + later, self_size)
    cross_region = (copies * self_size, [("ba", ba_bits[1]), ("ba", ba_bits[0])] + later, cross_size)
    vector_count = 13 * width + hidden
    extra = padded_to(vector_count // 128, 16)
    packed = (copies * (self_size + cross_size) + extra, lanes)

    def attend_back(r, queries, grads, keys, values, kept, inverse, scores, logit, item, grad_keys, grad_values):
        results = []
        for g in range(groups):
            cols = slice(g * wide, (g + 1) * wide)
            big = slice(g * many, (g + 1) * many)
            back = inverse[item, 0:1, big]
            upright = jnp.broadcast_to(back, (128, many)).T
            scaled = jnp.concatenate(
                [
                    (
                        grads[:, cols].astype(F32)
                        * upright[h * rows : (h + 1) * rows, 0:1]
                    ).astype(BF16)
                    for h in range(GROUP_HEADS)
                ],
                axis=0,
            )
            lane = lax.broadcasted_iota(jnp.int32, (1, wide), 1) // head
            spread = jnp.concatenate(
                [
                    scaled[h * rows : (h + 1) * rows] * (lane == h).astype(F32).astype(BF16)
                    for h in range(GROUP_HEADS)
                ],
                axis=0,
            )
            scores[...] = nt(values(cols), spread)
            inner = jnp.sum(kept[item, :, big].astype(F32) * scores[...], axis=0, keepdims=True)
            logit[...] = (kept[item, :, big].astype(F32) * (scores[...] - inner * back)).astype(BF16)
            grad_values(cols, nn(kept[item, :, big], spread))
            grad_keys(cols, nn(logit[...], spread_heads(queries[:, cols], head)))
            results.append(diagonal(tn(keys(cols), logit[...]), head, rows))
        return jnp.concatenate(results, axis=0).T * scale

    def cross_back(r):
        grad = r.dr3[...] + nt(r.dh[...], r.we[...])
        sums = r.sums
        sums[...] = jnp.zeros(sums.shape, F32)
        unit = r.unit2[...]
        sums[0:1, :] = column_sum(grad * unit)
        sums[1:2, :] = column_sum(grad)
        dr2 = norm_backward(grad, unit, r.spread2[...], vector(r, G2))
        r.put(dr2=dr2)
        branch = dr2.astype(BF16)
        sums[2:3, :] = column_sum(branch)
        r.put(ds2=branch)
        r.do2[...] = nt(branch, r.wco[...]).astype(BF16)
        for i in range(own):
            span_rows = slice(i * rows, (i + 1) * rows)

            def grad_keys(cols, value):
                r.dk[i, :, cols] = value.astype(BF16)

            def grad_values(cols, value):
                r.dv[i, :, cols] = value.astype(BF16)

            result = attend_back(
                r,
                r.q2[span_rows, :],
                r.do2[span_rows, :],
                lambda cols: r.keys[i, :, cols],
                lambda cols: r.values[i, :, cols],
                r.e2,
                r.inv2,
                r.scores,
                r.logit,
                i,
                grad_keys,
                grad_values,
            )
            r.dq[span_rows, :] = result.astype(BF16)
            r.put_part(i, dk=None, dv=None)
            index = lax.axis_index("pb")
            for k in range(group - 1, -1, -1):
                edge = pl.ds(pl.multiple_of((index ^ k) * part, 16), part)
                value = nt(r.dk[i, edge, :], r.wck[...]) + nt(r.dv[i, edge, :], r.wcv[...])
                if k < 2:
                    r.near[k][i] = value.astype(BF16)
                elif k == 2:
                    r.far[i] = value.astype(BF16)
                else:
                    r.pass_on[i][...] = value.astype(BF16)
                    r.put(pass_on=i)
        r.put(far=None)
        r.put(near=0)
        r.put(near=1)
        r.put(dq=None)
        sums[3:4, :] = column_sum(r.dq[...])
        total = jnp.zeros((1, width), F32)
        for i in range(own):
            total = total + column_sum(r.dv[i])
        sums[4:5, :] = total
        r.put(sums=None)
        r.put(dc=nt(r.dq[...], r.wcq[...]))

    act_got = swap(fw.act_send, "pb", 1)
    x2b_got = swap(fw.x2b, "pb", 1)
    df_got = swap(fw.df, "pb", 1)
    dh_got = swap(fw.dh_send, "pb", 1)
    back = run(
        cross_back,
        dict(
            vectors=(vectors, VM),
            dh=(fw.dh, DMA),
            we=(expand_weight, DMA),
            dr3=(fw.dr3, DMA),
            unit2=(fw.unit2, DMA),
            spread2=(fw.spread2, DMA),
            wco=(cross_out, DMA),
            values=(memory_values, DMA),
            inv2=(fw.inv2, DMA),
            e2=(fw.e2, DMA),
            q2=(fw.q2, DMA),
            keys=(memory_keys, DMA),
            wck=(cross_key, DMA),
            wcv=(cross_value, DMA),
            wcq=(cross_query, DMA),
        ),
        dict(
            near=([(own, part, width)] * 2, BF16, DMA),
            far=((own, part, width), BF16, DMA),
            pass_on=([(part, width)] * own, BF16, DMA),
            dq=((all_rows, width), BF16, DMA),
            dc=((all_rows, width), F32, DMA),
            dk=((own, span, width), BF16, DMA),
            dv=((own, span, width), BF16, DMA),
            dr2=((all_rows, width), F32, DMA),
            ds2=((all_rows, width), BF16, DMA),
            sums=((8, width), F32, DMA),
        ),
        dict(do2=((all_rows, width), BF16), scores=((span, many), F32), logit=((span, many), BF16)),
        microseconds=20.0,
    )


    def cross_weights(r):
        grad = r.grad
        grad[...] = tn(r.o2[...], r.ds2[...])
        pack(r, grad, cross_region, 3 * block)
        grad[...] = tn(r.c_in[...], r.cross_dq[...])
        pack(r, grad, cross_region, 0 * block)
        grad[...] = tn(r.plain[0], r.cross_dv[0])
        for i in range(1, own):
            grad[...] += tn(r.plain[i], r.cross_dv[i])
        pack(r, grad, cross_region, 2 * block)
        grad[...] = tn(r.keyed[0], r.cross_dk[0])
        for i in range(1, own):
            grad[...] += tn(r.keyed[i], r.cross_dk[i])
        pack(r, grad, cross_region, 1 * block)

    def rest_back(r):
        grad = r.dr2[...] + r.dc[...]
        sums = r.sums
        sums[...] = jnp.zeros(sums.shape, F32)
        unit = r.unit1[...]
        sums[0:1, :] = column_sum(grad * unit)
        sums[1:2, :] = column_sum(grad)
        first = r.first
        first[...] = norm_backward(grad, unit, r.spread1[...], vector(r, G1))
        branch = first[...].astype(BF16)
        sums[2:3, :] = column_sum(branch)
        whole = r.grad
        whole[...] = tn(r.o1[...], branch)
        pack(r, whole, self_region, 3 * block)
        r.do1[...] = nt(branch, r.wo[...]).astype(BF16)
        for i in range(own):
            span_rows = slice(i * rows, (i + 1) * rows)

            def grad_keys(cols, value):
                r.dk[span_rows, cols] = value.astype(BF16)

            def grad_values(cols, value):
                r.dv[span_rows, cols] = value.astype(BF16)

            result = attend_back(
                r,
                r.q1[span_rows, :],
                r.do1[span_rows, :],
                lambda cols: r.k1[span_rows, cols],
                lambda cols: r.v1[span_rows, cols],
                r.e1,
                r.inv1,
                r.scores,
                r.logit,
                i,
                grad_keys,
                grad_values,
            )
            r.dq[span_rows, :] = result.astype(BF16)
        dq, dk, dv = r.dq[...], r.dk[...], r.dv[...]
        sums[3:4, :] = column_sum(dq)
        sums[4:5, :] = column_sum(dv)
        both = nt(dq, r.wq[...]) + nt(dk, r.wk[...])
        low = (first[...] + both + nt(dv, r.wv[...])).astype(BF16)
        for k in range(group):
            for i in range(own):
                (r.near[k] if k < 2 else r.far.at[k - 2])[i] = low[i * rows + k * slot : i * rows + (k + 1) * slot, :]
        for j in range(2):
            r.near[j][own:] = r.out_near[j][...]
            r.far[j, own:] = r.out_far[j]
        r.put(near=0)
        r.put(near=1)
        r.put(far=None)
        both = both + r.dc[...]
        embed = both[0:rows]
        for i in range(1, own):
            embed = embed + both[i * rows : (i + 1) * rows]
        embed = nn(embed.astype(BF16), r.perm[...]).astype(BF16)
        order_bits = project_order
        for position in range(ba_size):
            relative = sum(((position >> (len(order_bits) - 1 - b)) & 1) * bit for b, bit in enumerate(order_bits))
            for y in range(two):
                first = row_place(self_region[1], relative, y) * self_size + 4 * block
                for c, target in ((0, r.keep), (1, r.send)):
                    k = 2 * y + c
                    piece = embed[k * slot : (k + 1) * slot, position * block : (position + 1) * block]
                    filled = jnp.concatenate([piece, jnp.zeros((slot, lanes - block), BF16)], axis=1)
                    target[first : first + slot, :] = filled
        table_rows = r.rows
        table_rows[...] = jnp.zeros(table_rows.shape, F32)
        sources = [
            (sums, 3),
            (sums, 4),
            (sums, 2),
            (sums, 0),
            (sums, 1),
            (r.sums_s, 3),
            (r.sums_s, 4),
            (r.sums_s, 2),
            (r.sums_s, 0),
            (r.sums_s, 1),
            (r.sums_f, 2),
            (r.sums_f, 0),
            (r.sums_f, 1),
        ] + [(r.hidden_sum, None)]
        filled_rows = 0
        for source, place_of in sources:
            place_of = place_of or 0
            for j in range(source.shape[1] // 128):
                table_rows[filled_rows : filled_rows + 1, :] = source[place_of : place_of + 1, j * 128 : (j + 1) * 128]
                filled_rows += 1
        low_rows = table_rows[...].astype(BF16)
        r.keep[packed[0] - extra :, :] = low_rows
        r.send[packed[0] - extra :, :] = low_rows
        for matrix, left, right in ((0, r.a_in, dq), (1, r.a_in, dk), (2, r.x0, dv)):
            whole[...] = tn(left[...], right)
            pack(r, whole, self_region, matrix * block)
        cross_weights(r)
        r.put(send=None, keep=None)

    act_got, x2b_got, df_got, dh_got, pass_first = meet(act_got, x2b_got, df_got, dh_got, back.pass_on[0])
    pass_first_got = swap(pass_first, "pb", 2)

    def hidden_grads(r):
        def one(perm, keep, got, rows_own, rows_got, kept, sent):
            own_cols = nn(rows_own(), perm()).astype(BF16)
            got_cols = nn(rows_got(), perm()).astype(BF16)
            for y in range(two):
                total = nn(keep()[y], own_cols) + nn(got()[y], got_cols)
                kept[y] = total[:, :half].astype(BF16)
                sent[y] = total[:, half:].astype(BF16)

        one(
            lambda: r.pperm[...],
            lambda: r.act_keep,
            lambda: r.act_got,
            lambda: r.df[...],
            lambda: r.df_got[...],
            r.p_keep,
            r.p_send,
        )
        r.put(p_send=None, p_keep=None)
        one(
            lambda: r.eperm[...],
            lambda: r.dh_keep,
            lambda: r.dh_got,
            lambda: r.x2b[...],
            lambda: r.x2b_got[...],
            r.e_keep,
            r.e_send,
        )
        r.put(e_send=None, e_keep=None)

    piece = ((two, share, half), BF16, DMA)
    hid = run(
        hidden_grads,
        dict(
            df=(tie(fw.df, pass_first), DMA),
            pperm=(project_perm, DMA),
            df_got=(df_got, DMA),
            act_keep=(fw.act_keep, DMA),
            act_got=(act_got, DMA),
            x2b=(fw.x2b, DMA),
            eperm=(expand_perm, DMA),
            x2b_got=(x2b_got, DMA),
            dh_keep=(fw.dh_keep, DMA),
            dh_got=(dh_got, DMA),
        ),
        dict(p_keep=piece, p_send=piece, e_keep=piece, e_send=piece),
        microseconds=4.0,
    )

    pass_first_got, p_send, e_send, pass_second, far = meet(
        pass_first_got, hid.p_send, hid.e_send, back.pass_on[1], back.far
    )

    p_got = swap(p_send, "ba", ba_bits[0])
    e_got = swap(e_send, "ba", ba_bits[1])
    pass_second_got = swap(pass_second, "pb", 2)
    far_got = swap(far, "pb", 2)
    slf = run(
        rest_back,
        dict(
            vectors=(vectors, VM),
            dr2=(tie(back.dr2, p_send, e_send), DMA),
            dc=(back.dc, DMA),
            unit1=(fw.unit1, DMA),
            spread1=(fw.spread1, DMA),
            o1=(fw.o1, DMA),
            wo=(self_out, DMA),
            inv1=(fw.inv1, DMA),
            e1=(fw.e1, DMA),
            q1=(fw.q1, DMA),
            k1=(fw.k1, DMA),
            v1=(fw.v1, DMA),
            wq=(self_query, DMA),
            wk=(self_key, DMA),
            wv=(self_value, DMA),
            a_in=(fw.a_in, DMA),
            x0=(fw.x0, DMA),
            perm=(project_perm, DMA),
            out_near=(fw.near, DMA),
            out_far=(fw.far, DMA),
            o2=(fw.o2, DMA),
            ds2=(back.ds2, DMA),
            c_in=(fw.c_in, DMA),
            cross_dq=(back.dq, DMA),
            cross_dv=(back.dv, DMA),
            plain=(plain, DMA),
            cross_dk=(back.dk, DMA),
            keyed=(keyed, DMA),
            sums_s=(back.sums, DMA),
            sums_f=(fw.sums, DMA),
            hidden_sum=(fw.hidden_sum, DMA),
        ),
        dict(
            keep=(packed, BF16, DMA),
            send=(packed, BF16, DMA),
            near=([(2 * own, slot, width)] * 2, BF16, DMA),
            far=((2, 2 * own, slot, width), BF16, DMA),
        ),
        dict(
            sums=((8, width), F32),
            rows=((extra, 128), F32),
            first=((all_rows, width), F32),
            grad=((width, width), F32),
            do1=((all_rows, width), BF16),
            dq=((all_rows, width), BF16),
            dk=((all_rows, width), BF16),
            dv=((all_rows, width), BF16),
            scores=((rows, many), F32),
            logit=((rows, many), BF16),
        ),
        microseconds=7.0,
    )
    p_got, e_got, pass_first_got, pass_second_got, far_got, send, home_far = meet(
        p_got, e_got, pass_first_got, pass_second_got, far_got, slf.send, slf.far
    )

    p_keep, p_send = halves(pair_sum(hid.p_keep, p_got), -1)
    e_keep, e_send = halves(pair_sum(hid.e_keep, e_got), -1)
    p_got = swap(p_send, "ba", ba_bits[1])
    e_got = swap(e_send, "ba", ba_bits[0])
    got = swap(send, "pb", 1)
    home_across = swap(home_far, "pb", 2)
    last_first = swap(pass_first_got, "pb", 1)
    p_got, e_got, got, home_across, last_first, pass_second_got, mem_near = meet(
        p_got, e_got, got, home_across, last_first, pass_second_got, back.near[1]
    )

    whole = pair_sum(slf.keep, got)
    edge = copies * self_size
    a_keep, a_send = row_halves(jnp.concatenate([whole[:edge], whole[packed[0] - extra :]]), extra)
    b_keep, b_send = row_halves(whole[edge : packed[0] - extra], 0)
    p_total, e_total = pair_sum(p_keep, p_got), pair_sum(e_keep, e_got)
    f_keep, f_send = (jnp.stack([p_total[y], e_total[y]]).astype(BF16) for y in range(two))
    a_got = swap(a_send, "ba", ba_bits[0])
    b_got = swap(b_send, "ba", ba_bits[1])
    f_got = swap(f_send, "pb", 2)
    last_second = swap(pass_second_got, "pb", 1)
    mem_other = swap(mem_near, "pb", 1)
    a_got, b_got, f_got, last_second, mem_other, home_near, home_passed = meet(
        a_got, b_got, f_got, last_second, mem_other, slf.near[1], home_across[1]
    )

    f_total = pair_sum(f_keep, f_got)
    f_half = f_total.shape[-1] // 2
    f_keep, f_send = (
        jnp.concatenate(
            [f_total[0, :, j * f_half : (j + 1) * f_half], f_total[1, :, j * f_half : (j + 1) * f_half]], axis=-1
        ).astype(BF16)
        for j in range(2)
    )
    a_keep, a_send = row_halves(pair_sum(a_keep, a_got), extra)
    b_keep, b_send = row_halves(pair_sum(b_keep, b_got), 0)
    f_got = swap(f_send, "ba", ba_bits[2])
    a_got = swap(a_send, "ba", ba_bits[1])
    b_got = swap(b_send, "ba", ba_bits[0])
    home_other = swap(home_near, "pb", 1)
    home_last = swap(home_passed, "pb", 1)

    def place_memory(r):
        index = lax.axis_index("pb")
        for i in range(own):
            for k, piece in enumerate((r.mine.at[i], r.other.at[i], r.across.at[i], r.last[i])):
                r.wide[:, (index ^ k) * own + i, :] = piece[0:quarter, :].astype(F32)
        r.put(whole=r.wide[...].astype(BF16))

    memory_grad = run(
        place_memory,
        dict(
            mine=(tie(back.near[0], f_send, a_send, b_send), DMA),
            other=(mem_other, DMA),
            across=(far_got, DMA),
            last=([last_first, last_second], DMA),
        ),
        dict(whole=((quarter, items, width), BF16, DMA)),
        dict(wide=((quarter, items, width), F32)),
        microseconds=4.0,
    ).whole
    f_got, a_got, b_got, home_other, home_last, memory_grad = meet(
        f_got, a_got, b_got, home_other, home_last, memory_grad
    )

    keep, send = row_halves(
        interleave(pair_sum(a_keep, a_got), pair_sum(b_keep, b_got), self_size, cross_size, extra), extra
    )
    got = swap(send, "pb", 2)
    hidden_out = pair_sum(f_keep, f_got)
    project_out, expand_out = (
        finish(part_out, ba_bits[3:], lambda total: halves(total, -1))
        for part_out in (hidden_out[:, :f_half], hidden_out[:, f_half:])
    )
    expand_out = expand_out.T

    def place_rows(r):
        index = lax.axis_index("pb")
        for i in range(own):
            for k in range(group):
                source = (r.mine, r.other, r.across.at[0], r.last)[k]
                r.wide[:, (index ^ k) * own + i, :] = source[i, 0:chunk, :].astype(F32)
                r.wide_out[:, (index ^ k) * own + i, :] = source[own + i, 0:chunk, :].astype(F32)
        r.put(grad=r.wide[...].astype(BF16))
        r.put(out=r.wide_out[...].astype(BF16))

    wide_rows = (chunk, items, width)
    rows_home = run(
        place_rows,
        dict(
            mine=(tie(slf.near[0], send), DMA),
            other=(home_other, DMA),
            across=(home_across, DMA),
            last=(home_last, DMA),
        ),
        dict(grad=(wide_rows, BF16, DMA), out=(wide_rows, BF16, DMA)),
        dict(wide=(wide_rows, F32), wide_out=(wide_rows, F32)),
        microseconds=2.0,
    )
    got, input_grad, layer_output = meet(got, rows_home.grad, rows_home.out)

    keep, send = row_halves(pair_sum(keep, got), extra)
    square_outs = finish(
        pair_sum(keep, swap(send, "ba", ba_bits[2])), ba_bits[3:], lambda total: row_halves(total, extra)
    )
    input_grad, layer_output = input_grad.transpose(1, 0, 2), layer_output.transpose(1, 0, 2)
    memory_grad = memory_grad.transpose(1, 0, 2)
    self_outs = jnp.concatenate([square_outs[:self_size], square_outs[self_size + cross_size :]])
    cross_outs = square_outs[self_size : self_size + cross_size]

    summands = self_outs[self_outs.shape[0] - extra :].reshape(-1)[:vector_count]
    vecs = [summands[j * width : (j + 1) * width] for j in range(13)]
    expand_bias_out = summands[13 * width :]

    def square(outs, matrix):
        return outs[matrix * block : (matrix + 1) * block]

    return (
        layer_output,
        input_grad,
        memory_grad,
        self_outs[4 * block : 4 * block + chunk, :block],
        square(self_outs, 0),
        vecs[0],
        square(self_outs, 1),
        square(self_outs, 2),
        vecs[1],
        square(self_outs, 3),
        vecs[2],
        vecs[3],
        vecs[4],
        square(cross_outs, 0),
        vecs[5],
        square(cross_outs, 1),
        square(cross_outs, 2),
        vecs[6],
        square(cross_outs, 3),
        vecs[7],
        vecs[8],
        vecs[9],
        expand_out,
        expand_bias_out,
        project_out,
        vecs[10],
        vecs[11],
        vecs[12],
    )


def solution(mesh):
    rows = P("ba", "pb", None)
    copied = P()
    placed = (rows, P("ba", None, None), P("ba"), P("pb", None)) + (copied,) * 24 + (rows,)
    square = P("ba", "pb")
    return jax.shard_map(
        local,
        mesh=mesh,
        in_specs=placed,
        out_specs=(
            rows,
            rows,
            rows,
            P("pb", "ba"),
            square,
            copied,
            square,
            square,
            copied,
            square,
            copied,
            copied,
            copied,
            square,
            copied,
            square,
            square,
            copied,
            square,
            copied,
            copied,
            copied,
            square,
            copied,
            P("pb", "ba"),
            copied,
            copied,
            copied,
        ),
        check_vma=False,
    )
```

```python
import math

import jax
import jax.numpy as jnp
import numpy as np
from jax import lax
from jax.experimental import pallas as pl
from jax.experimental.pallas import tpu as pltpu
from jax.sharding import PartitionSpec as P

HEADS = 8
GROUP_HEADS = 4
F32 = jnp.float32
BF16 = jnp.bfloat16
HIDDEN_CHUNKS = 5
VMEM_BYTES = 58 * 2**20


def sinusoid(count, model_width):
    position = np.arange(count, dtype=np.float32)
    column = np.arange(model_width // 2, dtype=np.float32)
    frequency = np.exp(column * np.float32(-2.0 * math.log(10000.0) / model_width)).astype(np.float32)
    angles = (position[:, None] * frequency[None, :]).astype(np.float32)
    table = np.stack([np.sin(angles), np.cos(angles)], axis=-1)
    return table.reshape(count, model_width).astype(np.float32)


def padded_to(extent, multiple):
    return -(-extent // multiple) * multiple


def nn(left, right):
    return lax.dot_general(left, right, (((1,), (0,)), ((), ())), preferred_element_type=F32)


def nt(left, right):
    return lax.dot_general(left, right, (((1,), (1,)), ((), ())), preferred_element_type=F32)


def tn(left, right):
    return lax.dot_general(left, right, (((0,), (0,)), ((), ())), preferred_element_type=F32)


VM, SM, DMA, OWN = range(4)


class Named:
    def __init__(self, find):
        self.find = find

    def __getattr__(self, key):
        return self.find(key)


class Numbered:
    def __init__(self, find, key):
        self.find, self.key = find, key

    def __getitem__(self, place):
        return self.find((self.key, place))


def flat(entries):
    result = {}
    for key, (value, *rest) in entries.items():
        if isinstance(value, list):
            for place, member in enumerate(value):
                result[(key, place)] = (member, *rest)
        else:
            result[key] = (value, *rest)
    return result


def run(body, ins, outs, scratch=None, after=(), microseconds=5.0, spare=64):
    listed = {key for entries in (ins, outs) for key, entry in entries.items() if isinstance(entry[0], list)}
    ins, outs, scratch = flat(ins), flat(outs), scratch or {}
    in_dma = [key for key, entry in ins.items() if entry[1] in (DMA, OWN)]
    out_dma = [key for key, entry in outs.items() if entry[2] == DMA]

    def kernel(*refs):
        refs = list(refs)
        held = {key: refs.pop(0) for key in ins}
        del refs[: len(after)]
        results = {key: refs.pop(0) for key in outs}
        arrived = {key: refs.pop(0) for key in in_dma}
        leaving = {key: refs.pop(0) for key in out_dma}
        held.update(results)
        sources = {key: held[key] for key in in_dma}
        held.update(arrived)
        held.update(leaving)
        held.update({key: refs.pop(0) for key in scratch})
        in_sem, out_sem, part_sem = refs
        pending = {}
        for place, key in enumerate(in_dma):
            source = sources[key]
            if ins[key][1] == OWN:
                count = arrived[key].shape[0]
                source = source.at[pl.ds(lax.axis_index("pb") * count, count)]
            pending[key] = pltpu.make_async_copy(source, arrived[key], in_sem.at[place])
            pending[key].start()
        started = {}

        def find(key):
            if key in listed:
                return Numbered(find, key)
            if key in pending:
                pending.pop(key).wait()
            return held[key]

        def put(**values):
            for key, value in values.items():
                if key in listed:
                    key = (key, value)
                elif value is not None:
                    held[key][...] = value
                if key in leaving:
                    place = out_dma.index(key)
                    started[key] = pltpu.make_async_copy(leaving[key], results[key], out_sem.at[place])
                    started[key].start()

        def put_part(part, **values):
            for key in values:
                place = out_dma.index(key)
                copy = pltpu.make_async_copy(leaving[key].at[part], results[key].at[part], part_sem.at[place, part])
                copy.start()
                started[(key, part)] = copy
                started[key] = copy

        bag = Named(find)
        bag.put = put
        bag.put_part = put_part
        body(bag)
        for key in list(pending):
            pending.pop(key).wait()
        for key in out_dma:
            assert key in started, key
        for copy in {id(copy): copy for copy in started.values()}.values():
            copy.wait()

    spaces = [pltpu.VMEM, pltpu.SMEM, pl.ANY, pl.ANY]
    arrays = [entry[0] for entry in ins.values()]
    nbytes = sum(int(np.prod(array.shape)) * array.dtype.itemsize for array in arrays)
    held_bytes = sum(
        int(np.prod(shape)) * (4 if dtype == F32 else 2)
        for shape, dtype in [(entry[0].shape, entry[0].dtype) for entry in ins.values()]
        + [(entry[0], entry[1]) for entry in outs.values()]
        + list(scratch.values())
    )
    made = pl.pallas_call(
        kernel,
        out_shape=[jax.ShapeDtypeStruct(entry[0], entry[1]) for entry in outs.values()],
        in_specs=[pl.BlockSpec(memory_space=spaces[entry[1]]) for entry in ins.values()]
        + [pl.BlockSpec(memory_space=pl.ANY)] * len(after),
        out_specs=[pl.BlockSpec(memory_space=spaces[entry[2]]) for entry in outs.values()],
        scratch_shapes=[
            pltpu.VMEM(
                (ins[key][0].shape[0] // lax.axis_size("pb"), *ins[key][0].shape[1:])
                if ins[key][1] == OWN
                else ins[key][0].shape,
                ins[key][0].dtype,
            )
            for key in in_dma
        ]
        + [pltpu.VMEM(outs[key][0], outs[key][1]) for key in out_dma]
        + [pltpu.VMEM(shape, dtype) for shape, dtype in scratch.values()]
        + [pltpu.SemaphoreType.DMA((max(1, len(in_dma)),)), pltpu.SemaphoreType.DMA((max(1, len(out_dma)),)), pltpu.SemaphoreType.DMA((max(1, len(out_dma)), 2))],
        compiler_params=pltpu.CompilerParams(vmem_limit_bytes=min(VMEM_BYTES, held_bytes + spare * 2**20)),
        cost_estimate=pl.CostEstimate(
            flops=int(microseconds * 1e3), bytes_accessed=1024, transcendentals=0
        ),
        name=body.__name__,
    )(*arrays, *after)
    by_key = dict(zip(outs, made))

    def result(key):
        if key in listed:
            return [value for name, value in by_key.items() if isinstance(name, tuple) and name[0] == key]
        return by_key[key]

    return Named(result)


def norm_forward(values, gain, shift):
    average = jnp.mean(values, axis=-1, keepdims=True)
    centred = values - average
    spread = jnp.mean(centred * centred, axis=-1, keepdims=True)
    scale = lax.rsqrt(spread + 1e-05)
    unit = centred * scale
    return unit, scale, unit * gain + shift


def norm_backward(grad, unit, scale, gain):
    lifted = grad * gain
    first = jnp.mean(lifted, axis=-1, keepdims=True)
    second = jnp.mean(lifted * unit, axis=-1, keepdims=True)
    return scale * (lifted - first - unit * second)


def column_sum(values):
    return jnp.sum(values.astype(F32), axis=0, keepdims=True)


def spread_heads(rows, width):
    count, columns = rows.shape
    lane = lax.broadcasted_iota(jnp.int32, (1, columns), 1) // width
    return jnp.concatenate(
        [rows * (lane == h).astype(F32).astype(BF16) for h in range(columns // width)], axis=0
    )


def diagonal(blocks, width, count):
    heads = blocks.shape[0] // width
    return jnp.concatenate(
        [blocks[h * width : (h + 1) * width, h * count : (h + 1) * count] for h in range(heads)], axis=0
    )


def swap(values, axis, bit):
    size = lax.axis_size(axis)
    return lax.ppermute(values, axis, [(i, i ^ bit) for i in range(size)])


def bits_of(size):
    return [1 << b for b in range(size.bit_length() - 1)]


def exchange(values, axis):
    size = lax.axis_size(axis)
    return [values[0]] + [swap(values[k], axis, k) for k in range(1, size)]


def pair_sum(kept, got):
    return kept.astype(F32) + got.astype(F32)


def meet(*arrays):
    return lax.optimization_barrier(arrays)


def tie(values, *before):
    return lax.optimization_barrier((values, *before))[0]


def halves(values, dim):
    dim = dim % values.ndim
    if values.shape[dim] == 2:
        parts = [lax.index_in_dim(values, j, dim, keepdims=False) for j in range(2)]
    else:
        half = values.shape[dim] // 2
        parts = [lax.slice_in_dim(values, j * half, (j + 1) * half, axis=dim) for j in range(2)]
    return parts[0].astype(BF16), parts[1].astype(BF16)


def row_halves(total, extra):
    body = total.shape[0] - extra
    parts = [total[: body // 2], total[body // 2 : body]]
    if extra:
        parts = [jnp.concatenate([part, total[body:]]) for part in parts]
    return parts[0].astype(BF16), parts[1].astype(BF16)


def sum_halves(kept, got, low, high, extra):
    def piece(first, last):
        return pair_sum(kept[first:last], got[first:last]).astype(BF16)

    middle = (low + high) // 2
    tail = [piece(kept.shape[0] - extra, kept.shape[0])] if extra else []
    return tuple(
        jnp.concatenate([piece(*edge)] + tail) if tail else piece(*edge) for edge in ((low, middle), (middle, high))
    )


def finish(total, bits, split):
    for bit in bits:
        kept, sent = split(total)
        total = pair_sum(kept, swap(sent, "ba", bit))
    return total


def interleave(first, second, first_size, second_size, extra):
    count = second.shape[0] // second_size
    body = jnp.concatenate(
        [
            first[: count * first_size].reshape(count, first_size, -1),
            second.reshape(count, second_size, -1),
        ],
        axis=1,
    )
    return jnp.concatenate([body.reshape(count * (first_size + second_size), -1), first[count * first_size :]])


def permutation(order, model_width, ba_size):
    mine = lax.axis_index("ba")
    width = model_width // ba_size
    column = lax.broadcasted_iota(jnp.int32, (1, model_width), 1)
    position = column // width
    relative = jnp.zeros_like(column)
    for step, bit in enumerate(order):
        digit = (position >> (len(order) - 1 - step)) & 1
        relative = relative + digit * bit
    source = (relative ^ mine) * width + column % width
    row = lax.broadcasted_iota(jnp.int32, (model_width, model_width), 0)
    return (row == source).astype(BF16)


def local(
    decoder_input,
    memory,
    lengths,
    query_embed,
    self_query,
    self_query_bias,
    self_key,
    self_value,
    self_value_bias,
    self_out,
    self_out_bias,
    norm_one_gain,
    norm_one_bias,
    cross_query,
    cross_query_bias,
    cross_key,
    cross_value,
    cross_value_bias,
    cross_out,
    cross_out_bias,
    norm_two_gain,
    norm_two_bias,
    expand_weight,
    expand_bias,
    project_weight,
    project_bias,
    norm_three_gain,
    norm_three_bias,
    out_cotangent,
):
    items, chunk, width = decoder_input.shape
    tokens = memory.shape[1]
    hidden = expand_weight.shape[1]
    group = lax.axis_size("pb")
    ba_size = lax.axis_size("ba")
    place = lax.axis_index("pb")
    mine = lax.axis_index("ba")
    own = items // group
    quarter = tokens // group
    slot = padded_to(chunk, 32)
    rows = group * slot
    all_rows = own * rows
    part = padded_to(quarter, 16)
    span = group * part
    head = width // HEADS
    scale = head ** (-0.5)
    share = hidden // group
    step = hidden // HIDDEN_CHUNKS
    wide = GROUP_HEADS * head
    many = GROUP_HEADS * rows
    groups = HEADS // GROUP_HEADS
    ba_bits = bits_of(ba_size)
    block = width // ba_size
    lanes = width // group


    def prepare(r):
        index = lax.axis_index("pb")
        r.wide_x[...] = r.x[...].astype(F32)
        r.wide_g[...] = r.g[...].astype(F32)
        for k in range(group):
            source = (index ^ k) * own
            piece = r.rows[k]
            piece[...] = jnp.zeros(piece.shape, BF16)
            for i in range(own):
                piece[i, 0:chunk, :] = r.wide_x[:, source + i, :].astype(BF16)
                piece[own + 1 + i, 0:chunk, :] = r.wide_g[:, source + i, :].astype(BF16)
            piece[own, 0:chunk, :] = r.e[...]

    prepared = run(
        prepare,
        dict(
            x=(decoder_input.transpose(1, 0, 2), VM),
            e=(query_embed, VM),
            g=(out_cotangent.transpose(1, 0, 2), VM),
        ),
        dict(rows=([(2 * own + 1, slot, width)] * group, BF16, VM)),
        dict(wide_x=((chunk, items, width), F32), wide_g=((chunk, items, width), F32)),
        microseconds=1.0,
    )
    row_parts = exchange(prepared.rows, "pb")

    table = np.zeros((group, part, width), np.float32)
    table[:, :quarter] = sinusoid(tokens, width).reshape(group, quarter, width)
    table = jnp.asarray(table.reshape(span, width))

    def project_memory(r):
        for i in range(own):
            source = r.memory[i]
            for q in range(group):
                r.plain[i, q * part : q * part + quarter, :] = source[q * quarter : (q + 1) * quarter, :]
                if part > quarter:
                    r.plain[i, q * part + quarter : (q + 1) * part, :] = jnp.zeros((part - quarter, width), BF16)
            r.keyed[i] = (r.plain[i].astype(F32) + r.table[...]).astype(BF16)
            r.keys[i] = nn(r.keyed[i], r.wk[...]).astype(BF16)
            r.put_part(i, keys=None, keyed=None)
            r.values[i] = (nn(r.plain[i], r.wv[...]) + r.bv[...].astype(F32).reshape(1, width)).astype(BF16)
            r.put_part(i, values=None, plain=None)

    memory_block = ((own, span, width), BF16, DMA)
    prj = run(
        project_memory,
        dict(
            memory=(memory, OWN),
            table=(table, DMA),
            wk=(cross_key, DMA),
            wv=(cross_value, DMA),
            bv=(cross_value_bias, VM),
        ),
        dict(keys=memory_block, values=memory_block, keyed=memory_block, plain=memory_block),
        after=prepared.rows[:1],
        microseconds=7.0,
    )
    memory_keys, memory_values, keyed, plain = prj.keys, prj.values, prj.keyed, prj.plain

    vectors = [
        self_query_bias,
        self_value_bias,
        self_out_bias,
        norm_one_gain,
        norm_one_bias,
        cross_query_bias,
        cross_out_bias,
        norm_two_gain,
        norm_two_bias,
        project_bias,
        norm_three_gain,
        norm_three_bias,
    ]
    BQ, BV, BO, G1, B1, BCQ, BCO, G2, B2, BP, G3, B3 = range(12)

    def vector(r, place):
        return r.vectors[place][...].astype(F32).reshape(1, width)

    def staggered(tasks, first, second):
        for n in range(len(tasks) + 1):
            if n < len(tasks):
                first(n, *tasks[n])
            if n > 0:
                second(n - 1, *tasks[n - 1])

    def attend(queries, keys, values, kept, inverse, buffers, bias, results):
        parts = {}

        def first(n, i, g):
            cols = slice(g * wide, (g + 1) * wide)
            shift = jnp.concatenate([bias(i)] * (many // 128), axis=1)
            buffers[n % 2][...] = nt(keys(i, cols), spread_heads(queries(i)[:, cols], head)) + shift

        def second(n, i, g):
            cols = slice(g * wide, (g + 1) * wide)
            big = slice(g * many, (g + 1) * many)
            scores = buffers[n % 2][...]
            highest = jnp.max(scores, axis=0, keepdims=True)
            raised = jnp.exp(scores - highest)
            total = jnp.sum(raised, axis=0, keepdims=True)
            kept[i, :, big] = raised.astype(BF16)
            back = 1.0 / total
            inverse[i, :, big] = jnp.broadcast_to(back, (8, many))
            parts[g] = diagonal(tn(values(i, cols), kept[i, :, big]) * back, head, rows)
            if g == groups - 1:
                results[i * rows : (i + 1) * rows, :] = jnp.concatenate(
                    [parts[j] for j in range(groups)], axis=0
                ).T.astype(BF16)

        staggered([(i, g) for i in range(own) for g in range(groups)], first, second)

    def forward(r):
        x_buf, e_buf = r.x0, r.embed
        for k in range(group):
            piece = r.rows[k]
            for i in range(own):
                x_buf[i * rows + k * slot : i * rows + (k + 1) * slot, :] = piece[i]
                e_buf[i * rows + k * slot : i * rows + (k + 1) * slot, :] = piece[own].astype(F32)
        r.put(x0=None)
        a_in = (x_buf[...].astype(F32) + e_buf[...]).astype(BF16)
        r.put(a_in=a_in)
        queries = (nn(a_in, r.wq[...]) + vector(r, BQ)).astype(BF16)
        r.put(q1=(queries.astype(F32) * scale).astype(BF16))
        r.put(k1=nn(a_in, r.wk[...]).astype(BF16))
        r.put(v1=(nn(x_buf[...], r.wv[...]) + vector(r, BV)).astype(BF16))

        row = lax.broadcasted_iota(jnp.int32, (rows, 128), 0) % slot
        r.self_bias[...] = jnp.where(row < chunk, 0.0, -1e30)
        attend(
            lambda i: r.q1[i * rows : (i + 1) * rows, :],
            lambda i, cols: r.k1[i * rows : (i + 1) * rows, cols],
            lambda i, cols: r.v1[i * rows : (i + 1) * rows, cols],
            r.e1,
            r.inv1,
            (r.self_scores, r.self_scores_two),
            lambda i: r.self_bias[...],
            r.o1,
        )
        r.put(e1=None)
        r.put(inv1=None)
        r.put(o1=None)
        summed = x_buf[...].astype(F32) + nn(r.o1[...], r.wo[...]) + vector(r, BO)
        unit, spread, normed = norm_forward(summed, vector(r, G1), vector(r, B1))
        r.put(unit1=unit)
        r.put(spread1=spread)
        r.normed[...] = normed
        r.put(c_in=(normed + e_buf[...]).astype(BF16))
        queries = (nn(r.c_in[...], r.wcq[...]) + vector(r, BCQ)).astype(BF16)
        r.put(q2=(queries.astype(F32) * scale).astype(BF16))
        for i in range(own):
            length = r.lengths[lax.axis_index("pb") * own + i]
            row = lax.broadcasted_iota(jnp.int32, (part, 128), 0)
            for q in range(group):
                seen = (row + q * quarter < length) & (row < quarter)
                r.cross_bias[i, q * part : (q + 1) * part, :] = jnp.where(seen, 0.0, -1e30)
        attend(
            lambda i: r.q2[i * rows : (i + 1) * rows, :],
            lambda i, cols: r.keys[i, :, cols],
            lambda i, cols: r.values[i, :, cols],
            r.e2,
            r.inv2,
            (r.cross_scores, r.cross_scores_two),
            lambda i: r.cross_bias[i],
            r.o2,
        )
        r.put(e2=None)
        r.put(inv2=None)
        r.put(o2=None)
        summed = r.normed[...] + nn(r.o2[...], r.wco[...]) + vector(r, BCO)
        unit, spread, normed = norm_forward(summed, vector(r, G2), vector(r, B2))
        r.put(unit2=unit)
        r.put(spread2=spread)
        r.normed[...] = normed
        r.put(x2b=normed.astype(BF16))
        r.third[...] = normed + vector(r, BP)
        for j in range(HIDDEN_CHUNKS):
            cols = slice(j * step, (j + 1) * step)
            before = nn(r.x2b[...], r.we[:, cols]) + r.be[cols].astype(F32).reshape(1, step)
            share_below = 0.5 + 0.5 * lax.erf(before * (0.5**0.5))
            density = jnp.exp(-0.5 * before * before) * ((2.0 * math.pi) ** (-0.5))
            r.slope[:, cols] = share_below + before * density
            active = (before * share_below).astype(BF16)
            r.third[...] += nn(active, r.wp[cols, :])
            r.active_t[cols, :] = active.T
        index = lax.axis_index("pb")

        def ship(source, kept, sent):
            for y in range(group // 2):
                for c, target in ((0, kept), (1, sent)):
                    first = pl.multiple_of((index ^ (2 * y + c)) * share, 16)
                    target[y] = source[pl.ds(first, share), :]

        ship(r.active_t, r.act_keep, r.act_send)
        r.put(act_send=None, act_keep=None)
        unit, spread, normed = norm_forward(r.third[...], vector(r, G3), vector(r, B3))
        low = normed.astype(BF16)
        cot = r.cot
        for k in range(group):
            piece = r.rows[k]
            for i in range(own):
                here = slice(i * rows + k * slot, i * rows + (k + 1) * slot)
                (r.near[k] if k < 2 else r.far.at[k - 2])[i] = low[here, :]
                cot[here, :] = piece[own + 1 + i].astype(F32)
        r.put(near=0)
        r.put(near=1)
        r.put(far=None)
        sums = r.sums
        sums[...] = jnp.zeros(sums.shape, F32)
        sums[0:1, :] = column_sum(cot[...] * unit)
        sums[1:2, :] = column_sum(cot[...])
        third = norm_backward(cot[...], unit, spread, vector(r, G3))
        r.put(dr3=third)
        branch = third.astype(BF16)
        r.put(df=branch)
        sums[2:3, :] = column_sum(branch)
        r.put(sums=None)
        for j in range(HIDDEN_CHUNKS):
            cols = slice(j * step, (j + 1) * step)
            grad = (nt(r.df[...], r.wp[cols, :]) * r.slope[:, cols]).astype(BF16)
            r.dh[:, cols] = grad
            r.hidden_sum[:, cols] = column_sum(grad)
            r.active_t[cols, :] = grad.T
        ship(r.active_t, r.dh_keep, r.dh_send)
        r.put(dh_send=None, dh_keep=None, dh=None, hidden_sum=None)

    two = group // 2
    fw = run(
        forward,
        dict(
            lengths=(lengths, SM),
            rows=(row_parts, VM),
            vectors=(vectors, VM),
            be=(expand_bias, VM),
            wq=(self_query, DMA),
            wk=(self_key, DMA),
            wv=(self_value, DMA),
            wo=(self_out, DMA),
            wcq=(cross_query, DMA),
            keys=(memory_keys, DMA),
            values=(memory_values, DMA),
            wco=(cross_out, DMA),
            we=(expand_weight, DMA),
            wp=(project_weight, DMA),
        ),
        dict(

            x0=((all_rows, width), BF16, DMA),
            a_in=((all_rows, width), BF16, DMA),
            q1=((all_rows, width), BF16, DMA),
            k1=((all_rows, width), BF16, DMA),
            v1=((all_rows, width), BF16, DMA),
            e1=((own, rows, groups * many), BF16, DMA),
            inv1=((own, 8, groups * many), F32, DMA),
            o1=((all_rows, width), BF16, DMA),
            unit1=((all_rows, width), F32, DMA),
            spread1=((all_rows, 1), F32, DMA),
            c_in=((all_rows, width), BF16, DMA),
            q2=((all_rows, width), BF16, DMA),
            e2=((own, span, groups * many), BF16, DMA),
            inv2=((own, 8, groups * many), F32, DMA),
            o2=((all_rows, width), BF16, DMA),
            unit2=((all_rows, width), F32, DMA),
            spread2=((all_rows, 1), F32, DMA),
            x2b=((all_rows, width), BF16, DMA),
            act_keep=((two, share, all_rows), BF16, DMA),
            act_send=((two, share, all_rows), BF16, DMA),
            dr3=((all_rows, width), F32, DMA),
            df=((all_rows, width), BF16, DMA),
            dh=((all_rows, hidden), BF16, DMA),
            dh_keep=((two, share, all_rows), BF16, DMA),
            dh_send=((two, share, all_rows), BF16, DMA),
            sums=((8, width), F32, DMA),
            hidden_sum=((1, hidden), F32, DMA),
        near=([(own, slot, width)] * 2, BF16, DMA),
            far=((2, own, slot, width), BF16, DMA),
        ),
        dict(
            embed=((all_rows, width), F32),
            self_scores=((rows, many), F32),
            self_scores_two=((rows, many), F32),
            self_bias=((rows, 128), F32),
            cross_scores=((span, many), F32),
            cross_scores_two=((span, many), F32),
            cross_bias=((own, span, 128), F32),
            normed=((all_rows, width), F32),
            third=((all_rows, width), F32),
            cot=((all_rows, width), F32),
            slope=((all_rows, hidden), F32),
            active_t=((hidden, all_rows), BF16),
        ),
        microseconds=18.0,
    )

    project_order = list(ba_bits)
    expand_order = [ba_bits[1], ba_bits[0]] + list(ba_bits[2:])
    half = width // 2

    def row_place(steps, relative, y):
        place_of = 0
        for axis, bit in steps:
            place_of = 2 * place_of + (y if axis == "pb" else relative // bit % 2)
        return place_of

    def pack(r, grad, region, offset):
        base, steps, size = region
        index, here = lax.axis_index("pb"), lax.axis_index("ba")
        for relative in range(ba_size):
            for y in range(two):
                first = base + row_place(steps, relative, y) * size + offset
                for c, target in ((0, r.keep), (1, r.send)):
                    source = pl.multiple_of((here ^ relative) * block, 8)
                    column = pl.multiple_of((index ^ (2 * y + c)) * lanes, 128)
                    target[first : first + block, :] = grad[pl.ds(source, block), pl.ds(column, lanes)].astype(BF16)

    later = [("pb", 2)] + [("ba", bit) for bit in ba_bits[2:]]
    copies = ba_size * two
    cross_size = 4 * block
    self_size = 4 * block + slot
    self_region = (0, [("ba", ba_bits[0]), ("ba", ba_bits[1])] + later, self_size)
    cross_region = (copies * self_size, [("ba", ba_bits[1]), ("ba", ba_bits[0])] + later, cross_size)
    vector_count = 13 * width + hidden
    extra = padded_to(vector_count // 128, 16)
    big_rows = own * part + part * 5 // 128 * 16
    packed = (copies * (self_size + cross_size) + extra, lanes)

    def attend_back(queries, grads, keys, values, kept, inverse, scores, logits, results, grad_keys, grad_values, finished=None):
        parts = {}
        spreads = {}

        def first(n, i, g):
            cols = slice(g * wide, (g + 1) * wide)
            back = inverse[i, 0:1, g * many : (g + 1) * many]
            upright = jnp.broadcast_to(back, (128, many)).T
            lane = lax.broadcasted_iota(jnp.int32, (1, wide), 1) // head
            piece = grads(i)[:, cols].astype(F32)
            spreads[n] = jnp.concatenate(
                [
                    (piece * upright[h * rows : (h + 1) * rows, 0:1]).astype(BF16)
                    * (lane == h).astype(F32).astype(BF16)
                    for h in range(GROUP_HEADS)
                ],
                axis=0,
            )
            scores[n % 2][...] = nt(values(i, cols), spreads[n])

        def second(n, i, g):
            cols = slice(g * wide, (g + 1) * wide)
            big = slice(g * many, (g + 1) * many)
            score, logit = scores[n % 2], logits[n % 2]
            back = inverse[i, 0:1, big]
            inner = jnp.sum(kept[i, :, big].astype(F32) * score[...], axis=0, keepdims=True)
            logit[...] = (kept[i, :, big].astype(F32) * (score[...] - inner * back)).astype(BF16)
            grad_values(i, cols, nn(kept[i, :, big], spreads[n]))
            grad_keys(i, cols, nn(logit[...], spread_heads(queries(i)[:, cols], head)))
            parts[g] = diagonal(tn(keys(i, cols), logit[...]), head, rows)
            if g == groups - 1:
                whole = jnp.concatenate([parts[j] for j in range(groups)], axis=0)
                results[i * rows : (i + 1) * rows, :] = (whole.T * scale).astype(BF16)
                if finished:
                    finished(i)

        staggered([(i, g) for i in range(own) for g in range(groups)], first, second)

    def cross_back(r):
        grad = r.dr3[...] + nt(r.dh[...], r.we[...])
        sums = r.sums
        sums[...] = jnp.zeros(sums.shape, F32)
        unit = r.unit2[...]
        sums[0:1, :] = column_sum(grad * unit)
        sums[1:2, :] = column_sum(grad)
        dr2 = norm_backward(grad, unit, r.spread2[...], vector(r, G2))
        r.put(dr2=dr2)
        branch = dr2.astype(BF16)
        sums[2:3, :] = column_sum(branch)
        r.put(ds2=branch)
        r.do2[...] = nt(branch, r.wco[...]).astype(BF16)
        def grad_keys(i, cols, value):
            r.dk[i, :, cols] = value.astype(BF16)

        def grad_values(i, cols, value):
            r.dv[i, :, cols] = value.astype(BF16)

        index = lax.axis_index("pb")
        cut = big_rows - own * part

        def memory_back(i):
            r.put_part(i, dk=None, dv=None)
            for k in range(group - 1, -1, -1):
                edge = pl.ds(pl.multiple_of((index ^ k) * part, 16), part)
                value = (nt(r.dk[i, edge, :], r.wck[...]) + nt(r.dv[i, edge, :], r.wcv[...])).astype(BF16)
                if k < 2:
                    r.near[k][i] = value
                elif k == 2:
                    r.far_big[i * part : (i + 1) * part, :] = value
                elif i == 0:
                    r.far_big[own * part : own * part + cut, :] = value[:cut]
                    r.far_small[0 : part - cut, :] = value[cut:]
                else:
                    r.far_small[i * part - cut : (i + 1) * part - cut, :] = value

        attend_back(
            lambda i: r.q2[i * rows : (i + 1) * rows, :],
            lambda i: r.do2[i * rows : (i + 1) * rows, :],
            lambda i, cols: r.keys[i, :, cols],
            lambda i, cols: r.values[i, :, cols],
            r.e2,
            r.inv2,
            (r.scores, r.scores_two),
            (r.logit, r.logit_two),
            r.dq,
            grad_keys,
            grad_values,
            memory_back,
        )
        r.put(far_big=None, far_small=None)
        r.put(near=0)
        r.put(near=1)
        r.put(dq=None)
        sums[3:4, :] = column_sum(r.dq[...])
        total = jnp.zeros((1, width), F32)
        for i in range(own):
            total = total + column_sum(r.dv[i])
        sums[4:5, :] = total
        r.put(sums=None)
        r.put(dc=nt(r.dq[...], r.wcq[...]))

    act_got = swap(fw.act_send, "pb", 1)
    x2b_got = swap(fw.x2b, "pb", 1)
    df_got = swap(fw.df, "pb", 1)
    dh_got = swap(fw.dh_send, "pb", 1)
    back = run(
        cross_back,
        dict(
            vectors=(vectors, VM),
            dh=(fw.dh, DMA),
            we=(expand_weight, DMA),
            dr3=(fw.dr3, DMA),
            unit2=(fw.unit2, DMA),
            spread2=(fw.spread2, DMA),
            wco=(cross_out, DMA),
            values=(memory_values, DMA),
            inv2=(fw.inv2, DMA),
            e2=(fw.e2, DMA),
            q2=(fw.q2, DMA),
            keys=(memory_keys, DMA),
            wck=(cross_key, DMA),
            wcv=(cross_value, DMA),
            wcq=(cross_query, DMA),
        ),
        dict(
            near=([(own, part, width)] * 2, BF16, DMA),
            far_big=((big_rows, width), BF16, DMA),
            far_small=((2 * own * part - big_rows, width), BF16, DMA),
            dq=((all_rows, width), BF16, DMA),
            dc=((all_rows, width), F32, DMA),
            dk=((own, span, width), BF16, DMA),
            dv=((own, span, width), BF16, DMA),
            dr2=((all_rows, width), F32, DMA),
            ds2=((all_rows, width), BF16, DMA),
            sums=((8, width), F32, DMA),
        ),
        dict(do2=((all_rows, width), BF16), scores=((span, many), F32), scores_two=((span, many), F32), logit=((span, many), BF16), logit_two=((span, many), BF16)),
        microseconds=20.0,
    )


    def cross_weights(r):
        grad = r.grad
        grad[...] = tn(r.o2[...], r.ds2[...])
        pack(r, grad, cross_region, 3 * block)
        grad[...] = tn(r.c_in[...], r.cross_dq[...])
        pack(r, grad, cross_region, 0 * block)
        grad[...] = tn(r.plain[0], r.cross_dv[0])
        for i in range(1, own):
            grad[...] += tn(r.plain[i], r.cross_dv[i])
        pack(r, grad, cross_region, 2 * block)
        grad[...] = tn(r.keyed[0], r.cross_dk[0])
        for i in range(1, own):
            grad[...] += tn(r.keyed[i], r.cross_dk[i])
        pack(r, grad, cross_region, 1 * block)

    def rest_back(r):
        grad = r.dr2[...] + r.dc[...]
        sums = r.sums
        sums[...] = jnp.zeros(sums.shape, F32)
        unit = r.unit1[...]
        sums[0:1, :] = column_sum(grad * unit)
        sums[1:2, :] = column_sum(grad)
        first = r.first
        first[...] = norm_backward(grad, unit, r.spread1[...], vector(r, G1))
        branch = first[...].astype(BF16)
        sums[2:3, :] = column_sum(branch)
        whole = r.grad
        whole[...] = tn(r.o1[...], branch)
        pack(r, whole, self_region, 3 * block)
        r.do1[...] = nt(branch, r.wo[...]).astype(BF16)
        def grad_keys(i, cols, value):
            r.dk[i * rows : (i + 1) * rows, cols] = value.astype(BF16)

        def grad_values(i, cols, value):
            r.dv[i * rows : (i + 1) * rows, cols] = value.astype(BF16)

        attend_back(
            lambda i: r.q1[i * rows : (i + 1) * rows, :],
            lambda i: r.do1[i * rows : (i + 1) * rows, :],
            lambda i, cols: r.k1[i * rows : (i + 1) * rows, cols],
            lambda i, cols: r.v1[i * rows : (i + 1) * rows, cols],
            r.e1,
            r.inv1,
            (r.scores, r.scores_two),
            (r.logit, r.logit_two),
            r.dq,
            grad_keys,
            grad_values,
        )
        dq, dk, dv = r.dq[...], r.dk[...], r.dv[...]
        sums[3:4, :] = column_sum(dq)
        sums[4:5, :] = column_sum(dv)
        both = nt(dq, r.wq[...]) + nt(dk, r.wk[...])
        low = (first[...] + both + nt(dv, r.wv[...])).astype(BF16)
        for k in range(group):
            for i in range(own):
                (r.near[k] if k < 2 else r.far.at[k - 2])[i] = low[i * rows + k * slot : i * rows + (k + 1) * slot, :]
        for j in range(2):
            r.near[j][own:] = r.out_near[j][...]
            r.far[j, own:] = r.out_far[j]
        r.put(near=0)
        r.put(near=1)
        r.put(far=None)
        both = both + r.dc[...]
        embed = both[0:rows]
        for i in range(1, own):
            embed = embed + both[i * rows : (i + 1) * rows]
        embed = nn(embed.astype(BF16), permutation(project_order, width, ba_size)).astype(BF16)
        order_bits = project_order
        for position in range(ba_size):
            relative = sum(((position >> (len(order_bits) - 1 - b)) & 1) * bit for b, bit in enumerate(order_bits))
            for y in range(two):
                first = row_place(self_region[1], relative, y) * self_size + 4 * block
                for c, target in ((0, r.keep), (1, r.send)):
                    k = 2 * y + c
                    piece = embed[k * slot : (k + 1) * slot, position * block : (position + 1) * block]
                    filled = jnp.concatenate([piece, jnp.zeros((slot, lanes - block), BF16)], axis=1)
                    target[first : first + slot, :] = filled
        table_rows = r.rows
        table_rows[...] = jnp.zeros(table_rows.shape, F32)
        sources = [
            (sums, 3),
            (sums, 4),
            (sums, 2),
            (sums, 0),
            (sums, 1),
            (r.sums_s, 3),
            (r.sums_s, 4),
            (r.sums_s, 2),
            (r.sums_s, 0),
            (r.sums_s, 1),
            (r.sums_f, 2),
            (r.sums_f, 0),
            (r.sums_f, 1),
        ] + [(r.hidden_sum, None)]
        filled_rows = 0
        for source, place_of in sources:
            place_of = place_of or 0
            for j in range(source.shape[1] // 128):
                table_rows[filled_rows : filled_rows + 1, :] = source[place_of : place_of + 1, j * 128 : (j + 1) * 128]
                filled_rows += 1
        low_rows = table_rows[...].astype(BF16)
        r.keep[packed[0] - extra :, :] = low_rows
        r.send[packed[0] - extra :, :] = low_rows
        for matrix, left, right in ((0, r.a_in, dq), (1, r.a_in, dk), (2, r.x0, dv)):
            whole[...] = tn(left[...], right)
            pack(r, whole, self_region, matrix * block)
        cross_weights(r)
        r.put(send=None, keep=None)

    act_got, x2b_got, df_got, dh_got, hidden_start = meet(act_got, x2b_got, df_got, dh_got, back.ds2)

    def hidden_grads(r):
        r.perm[...] = permutation(project_order, width, ba_size)
        tile = width // 4

        def columns(rows, swapped):
            value = nn(rows, r.perm[...]).astype(BF16)
            tiles = [value[:, t * tile : (t + 1) * tile] for t in ((0, 2, 1, 3) if swapped else range(4))]
            return jnp.concatenate(tiles, axis=1)

        def one(swapped, keep, got, rows_own, rows_got, kept, sent):
            own_cols = columns(rows_own(), swapped)
            got_cols = columns(rows_got(), swapped)
            for y in range(two):
                total = nn(keep()[y], own_cols) + nn(got()[y], got_cols)
                kept[y] = total[:, :half].astype(BF16)
                sent[y] = total[:, half:].astype(BF16)

        one(
            False,
            lambda: r.act_keep,
            lambda: r.act_got,
            lambda: r.df[...],
            lambda: r.df_got[...],
            r.p_keep,
            r.p_send,
        )
        r.put(p_send=None, p_keep=None)
        one(
            True,
            lambda: r.dh_keep,
            lambda: r.dh_got,
            lambda: r.x2b[...],
            lambda: r.x2b_got[...],
            r.e_keep,
            r.e_send,
        )
        r.put(e_send=None, e_keep=None)

    piece = ((two, share, half), BF16, DMA)
    hid = run(
        hidden_grads,
        dict(
            df=(tie(fw.df, hidden_start), DMA),
            df_got=(df_got, DMA),
            act_keep=(fw.act_keep, DMA),
            act_got=(act_got, DMA),
            x2b=(fw.x2b, DMA),
            x2b_got=(x2b_got, DMA),
            dh_keep=(fw.dh_keep, DMA),
            dh_got=(dh_got, DMA),
        ),
        dict(p_keep=piece, p_send=piece, e_keep=piece, e_send=piece),
        dict(perm=((width, width), BF16)),
        microseconds=4.0,
    )

    p_send, e_send, far_big, mem_near = meet(hid.p_send, hid.e_send, back.far_big, back.near[1])

    p_got = swap(p_send, "ba", ba_bits[0])
    e_got = swap(e_send, "ba", ba_bits[1])
    big_got = swap(far_big, "pb", 2)
    mem_other = swap(mem_near, "pb", 1)
    slf = run(
        rest_back,
        dict(
            vectors=(vectors, VM),
            dr2=(tie(back.dr2, p_send, e_send), DMA),
            dc=(back.dc, DMA),
            unit1=(fw.unit1, DMA),
            spread1=(fw.spread1, DMA),
            o1=(fw.o1, DMA),
            wo=(self_out, DMA),
            inv1=(fw.inv1, DMA),
            e1=(fw.e1, DMA),
            q1=(fw.q1, DMA),
            k1=(fw.k1, DMA),
            v1=(fw.v1, DMA),
            wq=(self_query, DMA),
            wk=(self_key, DMA),
            wv=(self_value, DMA),
            a_in=(fw.a_in, DMA),
            x0=(fw.x0, DMA),
            out_near=(fw.near, DMA),
            out_far=(fw.far, DMA),
            o2=(fw.o2, DMA),
            ds2=(back.ds2, DMA),
            c_in=(fw.c_in, DMA),
            cross_dq=(back.dq, DMA),
            cross_dv=(back.dv, DMA),
            plain=(plain, DMA),
            cross_dk=(back.dk, DMA),
            keyed=(keyed, DMA),
            sums_s=(back.sums, DMA),
            sums_f=(fw.sums, DMA),
            hidden_sum=(fw.hidden_sum, DMA),
        ),
        dict(
            keep=(packed, BF16, DMA),
            send=(packed, BF16, DMA),
            near=([(2 * own, slot, width)] * 2, BF16, DMA),
            far=((2, 2 * own, slot, width), BF16, DMA),
        ),
        dict(
            sums=((8, width), F32),
            rows=((extra, 128), F32),
            first=((all_rows, width), F32),
            grad=((width, width), F32),
            do1=((all_rows, width), BF16),
            dq=((all_rows, width), BF16),
            dk=((all_rows, width), BF16),
            dv=((all_rows, width), BF16),
            scores=((rows, many), F32),
            scores_two=((rows, many), F32),
            logit=((rows, many), BF16),
            logit_two=((rows, many), BF16),
        ),
        microseconds=7.0,
    )
    p_got, e_got, big_got, mem_other, send, far_small = meet(
        p_got, e_got, big_got, mem_other, slf.send, back.far_small
    )

    p_keep, p_send = halves(pair_sum(hid.p_keep, p_got), -1)
    e_keep, e_send = halves(pair_sum(hid.e_keep, e_got), -1)
    p_got = swap(p_send, "ba", ba_bits[1])
    e_got = swap(e_send, "ba", ba_bits[0])
    got = swap(send, "pb", 1)
    small_got = swap(far_small, "pb", 2)
    last_first = swap(big_got[own * part :], "pb", 1)
    p_got, e_got, got, last_first, small_got = meet(p_got, e_got, got, last_first, small_got)

    edge = copies * self_size
    a_keep, a_send = sum_halves(slf.keep, got, 0, edge, extra)
    b_keep, b_send = sum_halves(slf.keep, got, edge, packed[0] - extra, 0)
    p_total, e_total = pair_sum(p_keep, p_got), pair_sum(e_keep, e_got)
    f_keep, f_send = (jnp.stack([p_total[y], e_total[y]]).astype(BF16) for y in range(two))
    a_got = swap(a_send, "ba", ba_bits[0])
    b_got = swap(b_send, "ba", ba_bits[1])
    f_got = swap(f_send, "pb", 2)
    last_second = swap(small_got, "pb", 1)
    a_got, b_got, f_got, last_second, home_near, home_far = meet(
        a_got, b_got, f_got, last_second, slf.near[1], slf.far
    )

    f_total = pair_sum(f_keep, f_got)
    f_half = f_total.shape[-1] // 2
    f_keep, f_send = (
        jnp.concatenate(
            [f_total[0, :, j * f_half : (j + 1) * f_half], f_total[1, :, j * f_half : (j + 1) * f_half]], axis=-1
        ).astype(BF16)
        for j in range(2)
    )
    a_keep, a_send = sum_halves(a_keep, a_got, 0, a_keep.shape[0] - extra, extra)
    b_keep, b_send = sum_halves(b_keep, b_got, 0, b_keep.shape[0], 0)
    a_got = swap(a_send, "ba", ba_bits[1])
    b_got = swap(b_send, "ba", ba_bits[0])
    home_other = swap(home_near, "pb", 1)
    home_across = swap(home_far, "pb", 2)

    def place_memory(r):
        index = lax.axis_index("pb")
        cut = big_rows - own * part
        for i in range(own):
            across = r.across[i * part : i * part + quarter, :]
            if i == 0:
                last = jnp.concatenate([r.last_first[...], r.last_second[0 : quarter - cut, :]], axis=0)
            else:
                last = r.last_second[i * part - cut : i * part - cut + quarter, :]
            for k, piece in enumerate((r.mine[i, 0:quarter, :], r.other[i, 0:quarter, :], across, last)):
                r.wide[:, (index ^ k) * own + i, :] = piece.astype(F32)
        r.put(whole=r.wide[...].astype(BF16))

    memory_grad = run(
        place_memory,
        dict(
            mine=(tie(back.near[0], f_send, a_send, b_send), DMA),
            other=(mem_other, DMA),
            across=(big_got, DMA),
            last_first=(last_first, DMA),
            last_second=(last_second, DMA),
        ),
        dict(whole=((quarter, items, width), BF16, DMA)),
        dict(wide=((quarter, items, width), F32)),
        microseconds=4.0,
        spare=4,
    ).whole
    f_send, a_got, b_got, home_other, home_across, memory_grad = meet(
        f_send, a_got, b_got, home_other, home_across, memory_grad
    )

    keep, send = row_halves(
        interleave(pair_sum(a_keep, a_got), pair_sum(b_keep, b_got), self_size, cross_size, extra), extra
    )
    got = swap(send, "pb", 2)
    f_got = swap(f_send, "ba", ba_bits[2])
    home_last = swap(home_across[1], "pb", 1)
    got, f_got, home_last = meet(got, f_got, home_last)

    keep, send = row_halves(pair_sum(keep, got), extra)
    got = swap(send, "ba", ba_bits[2])
    hidden_out = pair_sum(f_keep, f_got)
    project_out, expand_out = (
        finish(part_out, ba_bits[3:], lambda total: halves(total, -1))
        for part_out in (hidden_out[:, :f_half], hidden_out[:, f_half:])
    )
    expand_out = expand_out.T

    def place_rows(r):
        index = lax.axis_index("pb")
        for i in range(own):
            for k in range(group):
                source = (r.mine, r.other, r.across.at[0], r.last)[k]
                r.wide[:, (index ^ k) * own + i, :] = source[i, 0:chunk, :].astype(F32)
                r.wide_out[:, (index ^ k) * own + i, :] = source[own + i, 0:chunk, :].astype(F32)
        r.put(grad=r.wide[...].astype(BF16))
        r.put(out=r.wide_out[...].astype(BF16))

    wide_rows = (chunk, items, width)
    rows_home = run(
        place_rows,
        dict(
            mine=(tie(slf.near[0], send), DMA),
            other=(home_other, DMA),
            across=(home_across, DMA),
            last=(home_last, DMA),
        ),
        dict(grad=(wide_rows, BF16, DMA), out=(wide_rows, BF16, DMA)),
        dict(wide=(wide_rows, F32), wide_out=(wide_rows, F32)),
        microseconds=2.0,
        spare=4,
    )
    input_grad, layer_output = rows_home.grad, rows_home.out
    square_outs = finish(pair_sum(keep, got), ba_bits[3:], lambda total: row_halves(total, extra))
    input_grad, layer_output = input_grad.transpose(1, 0, 2), layer_output.transpose(1, 0, 2)
    memory_grad = memory_grad.transpose(1, 0, 2)
    self_outs = jnp.concatenate([square_outs[:self_size], square_outs[self_size + cross_size :]])
    cross_outs = square_outs[self_size : self_size + cross_size]

    summands = self_outs[self_outs.shape[0] - extra :].reshape(-1)[:vector_count]
    vecs = [summands[j * width : (j + 1) * width] for j in range(13)]
    expand_bias_out = summands[13 * width :]

    def square(outs, matrix):
        return outs[matrix * block : (matrix + 1) * block]

    return (
        layer_output,
        input_grad,
        memory_grad,
        self_outs[4 * block : 4 * block + chunk, :block],
        square(self_outs, 0),
        vecs[0],
        square(self_outs, 1),
        square(self_outs, 2),
        vecs[1],
        square(self_outs, 3),
        vecs[2],
        vecs[3],
        vecs[4],
        square(cross_outs, 0),
        vecs[5],
        square(cross_outs, 1),
        square(cross_outs, 2),
        vecs[6],
        square(cross_outs, 3),
        vecs[7],
        vecs[8],
        vecs[9],
        expand_out,
        expand_bias_out,
        project_out,
        vecs[10],
        vecs[11],
        vecs[12],
    )


def solution(mesh):
    rows = P("ba", "pb", None)
    copied = P()
    placed = (rows, P("ba", None, None), P("ba"), P("pb", None)) + (copied,) * 24 + (rows,)
    square = P("ba", "pb")
    return jax.shard_map(
        local,
        mesh=mesh,
        in_specs=placed,
        out_specs=(
            rows,
            rows,
            rows,
            P("pb", "ba"),
            square,
            copied,
            square,
            square,
            copied,
            square,
            copied,
            copied,
            copied,
            square,
            copied,
            square,
            square,
            copied,
            square,
            copied,
            copied,
            copied,
            square,
            copied,
            P("pb", "ba"),
            copied,
            copied,
            copied,
        ),
        check_vma=False,
    )
```

```python
import math

import jax
import jax.numpy as jnp
import numpy as np
from jax import lax
from jax.experimental import pallas as pl
from jax.experimental.pallas import tpu as pltpu
from jax.sharding import PartitionSpec as P

HEADS = 8
GROUP_HEADS = 4
F32 = jnp.float32
BF16 = jnp.bfloat16
HIDDEN_CHUNKS = 5
VMEM_BYTES = 58 * 2**20


def sinusoid(count, model_width):
    position = np.arange(count, dtype=np.float32)
    column = np.arange(model_width // 2, dtype=np.float32)
    frequency = np.exp(column * np.float32(-2.0 * math.log(10000.0) / model_width)).astype(np.float32)
    angles = (position[:, None] * frequency[None, :]).astype(np.float32)
    table = np.stack([np.sin(angles), np.cos(angles)], axis=-1)
    return table.reshape(count, model_width).astype(np.float32)


def padded_to(extent, multiple):
    return -(-extent // multiple) * multiple


def nn(left, right):
    return lax.dot_general(left, right, (((1,), (0,)), ((), ())), preferred_element_type=F32)


def nt(left, right):
    return lax.dot_general(left, right, (((1,), (1,)), ((), ())), preferred_element_type=F32)


def tn(left, right):
    return lax.dot_general(left, right, (((0,), (0,)), ((), ())), preferred_element_type=F32)


VM, SM, DMA, OWN = range(4)


class Named:
    def __init__(self, find):
        self.find = find

    def __getattr__(self, key):
        return self.find(key)


class Numbered:
    def __init__(self, find, key):
        self.find, self.key = find, key

    def __getitem__(self, place):
        return self.find((self.key, place))


def flat(entries):
    result = {}
    for key, (value, *rest) in entries.items():
        if isinstance(value, list):
            for place, member in enumerate(value):
                result[(key, place)] = (member, *rest)
        else:
            result[key] = (value, *rest)
    return result


def run(body, ins, outs, scratch=None, after=(), microseconds=5.0, spare=64, most=VMEM_BYTES):
    listed = {key for entries in (ins, outs) for key, entry in entries.items() if isinstance(entry[0], list)}
    ins, outs, scratch = flat(ins), flat(outs), scratch or {}
    in_dma = [key for key, entry in ins.items() if entry[1] in (DMA, OWN)]
    out_dma = [key for key, entry in outs.items() if entry[2] == DMA]

    def kernel(*refs):
        refs = list(refs)
        held = {key: refs.pop(0) for key in ins}
        del refs[: len(after)]
        results = {key: refs.pop(0) for key in outs}
        arrived = {key: refs.pop(0) for key in in_dma}
        leaving = {key: refs.pop(0) for key in out_dma}
        held.update(results)
        sources = {key: held[key] for key in in_dma}
        held.update(arrived)
        held.update(leaving)
        held.update({key: refs.pop(0) for key in scratch})
        in_sem, out_sem, part_sem = refs
        pending = {}
        for place, key in enumerate(in_dma):
            source = sources[key]
            if ins[key][1] == OWN:
                count = arrived[key].shape[0]
                source = source.at[pl.ds(lax.axis_index("pb") * count, count)]
            pending[key] = pltpu.make_async_copy(source, arrived[key], in_sem.at[place])
            pending[key].start()
        started = {}

        def find(key):
            if key in listed:
                return Numbered(find, key)
            if key in pending:
                pending.pop(key).wait()
            return held[key]

        def put(**values):
            for key, value in values.items():
                if key in listed:
                    key = (key, value)
                elif value is not None:
                    held[key][...] = value
                if key in leaving:
                    place = out_dma.index(key)
                    started[key] = pltpu.make_async_copy(leaving[key], results[key], out_sem.at[place])
                    started[key].start()

        def put_part(part, **values):
            for key in values:
                place = out_dma.index(key)
                copy = pltpu.make_async_copy(leaving[key].at[part], results[key].at[part], part_sem.at[place, part])
                copy.start()
                started[(key, part)] = copy
                started[key] = copy

        bag = Named(find)
        bag.put = put
        bag.put_part = put_part
        body(bag)
        for key in list(pending):
            pending.pop(key).wait()
        for key in out_dma:
            assert key in started, key
        for copy in {id(copy): copy for copy in started.values()}.values():
            copy.wait()

    spaces = [pltpu.VMEM, pltpu.SMEM, pl.ANY, pl.ANY]
    arrays = [entry[0] for entry in ins.values()]
    nbytes = sum(int(np.prod(array.shape)) * array.dtype.itemsize for array in arrays)
    held_bytes = sum(
        int(np.prod(shape)) * (4 if dtype == F32 else 2)
        for shape, dtype in [(entry[0].shape, entry[0].dtype) for entry in ins.values()]
        + [(entry[0], entry[1]) for entry in outs.values()]
        + list(scratch.values())
    )
    made = pl.pallas_call(
        kernel,
        out_shape=[jax.ShapeDtypeStruct(entry[0], entry[1]) for entry in outs.values()],
        in_specs=[pl.BlockSpec(memory_space=spaces[entry[1]]) for entry in ins.values()]
        + [pl.BlockSpec(memory_space=pl.ANY)] * len(after),
        out_specs=[pl.BlockSpec(memory_space=spaces[entry[2]]) for entry in outs.values()],
        scratch_shapes=[
            pltpu.VMEM(
                (ins[key][0].shape[0] // lax.axis_size("pb"), *ins[key][0].shape[1:])
                if ins[key][1] == OWN
                else ins[key][0].shape,
                ins[key][0].dtype,
            )
            for key in in_dma
        ]
        + [pltpu.VMEM(outs[key][0], outs[key][1]) for key in out_dma]
        + [pltpu.VMEM(shape, dtype) for shape, dtype in scratch.values()]
        + [pltpu.SemaphoreType.DMA((max(1, len(in_dma)),)), pltpu.SemaphoreType.DMA((max(1, len(out_dma)),)), pltpu.SemaphoreType.DMA((max(1, len(out_dma)), 2))],
        compiler_params=pltpu.CompilerParams(vmem_limit_bytes=min(most, held_bytes + spare * 2**20)),
        cost_estimate=pl.CostEstimate(
            flops=int(microseconds * 1e3), bytes_accessed=1024, transcendentals=0
        ),
        name=body.__name__,
    )(*arrays, *after)
    by_key = dict(zip(outs, made))

    def result(key):
        if key in listed:
            return [value for name, value in by_key.items() if isinstance(name, tuple) and name[0] == key]
        return by_key[key]

    return Named(result)


def norm_forward(values, gain, shift):
    average = jnp.mean(values, axis=-1, keepdims=True)
    centred = values - average
    spread = jnp.mean(centred * centred, axis=-1, keepdims=True)
    scale = lax.rsqrt(spread + 1e-05)
    unit = centred * scale
    return unit, scale, unit * gain + shift


def norm_backward(grad, unit, scale, gain):
    lifted = grad * gain
    first = jnp.mean(lifted, axis=-1, keepdims=True)
    second = jnp.mean(lifted * unit, axis=-1, keepdims=True)
    return scale * (lifted - first - unit * second)


def column_sum(values):
    return jnp.sum(values.astype(F32), axis=0, keepdims=True)


def spread_heads(rows, width):
    count, columns = rows.shape
    lane = lax.broadcasted_iota(jnp.int32, (1, columns), 1) // width
    return jnp.concatenate(
        [rows * (lane == h).astype(F32).astype(BF16) for h in range(columns // width)], axis=0
    )


def diagonal(blocks, width, count):
    heads = blocks.shape[0] // width
    return jnp.concatenate(
        [blocks[h * width : (h + 1) * width, h * count : (h + 1) * count] for h in range(heads)], axis=0
    )


def swap(values, axis, bit):
    size = lax.axis_size(axis)
    return lax.ppermute(values, axis, [(i, i ^ bit) for i in range(size)])


def bits_of(size):
    return [1 << b for b in range(size.bit_length() - 1)]


def exchange(values, axis):
    size = lax.axis_size(axis)
    return [values[0]] + [swap(values[k], axis, k) for k in range(1, size)]


def pair_sum(kept, got):
    return kept.astype(F32) + got.astype(F32)


def meet(*arrays):
    return lax.optimization_barrier(arrays)


def tie(values, *before):
    return lax.optimization_barrier((values, *before))[0]


def halves(values, dim):
    dim = dim % values.ndim
    if values.shape[dim] == 2:
        parts = [lax.index_in_dim(values, j, dim, keepdims=False) for j in range(2)]
    else:
        half = values.shape[dim] // 2
        parts = [lax.slice_in_dim(values, j * half, (j + 1) * half, axis=dim) for j in range(2)]
    return parts[0].astype(BF16), parts[1].astype(BF16)


def row_halves(total, extra):
    body = total.shape[0] - extra
    parts = [total[: body // 2], total[body // 2 : body]]
    if extra:
        parts = [jnp.concatenate([part, total[body:]]) for part in parts]
    return parts[0].astype(BF16), parts[1].astype(BF16)


def sum_halves(kept, got, low, high, extra):
    def piece(first, last):
        return pair_sum(kept[first:last], got[first:last]).astype(BF16)

    middle = (low + high) // 2
    tail = [piece(kept.shape[0] - extra, kept.shape[0])] if extra else []
    return tuple(
        jnp.concatenate([piece(*edge)] + tail) if tail else piece(*edge) for edge in ((low, middle), (middle, high))
    )


def finish(total, bits, split):
    for bit in bits:
        kept, sent = split(total)
        total = pair_sum(kept, swap(sent, "ba", bit))
    return total


def interleave(first, second, first_size, second_size, extra):
    count = second.shape[0] // second_size
    body = jnp.concatenate(
        [
            first[: count * first_size].reshape(count, first_size, -1),
            second.reshape(count, second_size, -1),
        ],
        axis=1,
    )
    return jnp.concatenate([body.reshape(count * (first_size + second_size), -1), first[count * first_size :]])


def permutation(order, model_width, ba_size):
    mine = lax.axis_index("ba")
    width = model_width // ba_size
    column = lax.broadcasted_iota(jnp.int32, (1, model_width), 1)
    position = column // width
    relative = jnp.zeros_like(column)
    for step, bit in enumerate(order):
        digit = (position >> (len(order) - 1 - step)) & 1
        relative = relative + digit * bit
    source = (relative ^ mine) * width + column % width
    row = lax.broadcasted_iota(jnp.int32, (model_width, model_width), 0)
    return (row == source).astype(BF16)


def local(
    decoder_input,
    memory,
    lengths,
    query_embed,
    self_query,
    self_query_bias,
    self_key,
    self_value,
    self_value_bias,
    self_out,
    self_out_bias,
    norm_one_gain,
    norm_one_bias,
    cross_query,
    cross_query_bias,
    cross_key,
    cross_value,
    cross_value_bias,
    cross_out,
    cross_out_bias,
    norm_two_gain,
    norm_two_bias,
    expand_weight,
    expand_bias,
    project_weight,
    project_bias,
    norm_three_gain,
    norm_three_bias,
    out_cotangent,
):
    items, chunk, width = decoder_input.shape
    tokens = memory.shape[1]
    hidden = expand_weight.shape[1]
    group = lax.axis_size("pb")
    ba_size = lax.axis_size("ba")
    place = lax.axis_index("pb")
    mine = lax.axis_index("ba")
    own = items // group
    quarter = tokens // group
    slot = padded_to(chunk, 32)
    rows = group * slot
    all_rows = own * rows
    part = padded_to(quarter, 16)
    span = group * part
    head = width // HEADS
    scale = head ** (-0.5)
    share = hidden // group
    step = hidden // HIDDEN_CHUNKS
    wide = GROUP_HEADS * head
    many = GROUP_HEADS * rows
    groups = HEADS // GROUP_HEADS
    ba_bits = bits_of(ba_size)
    block = width // ba_size
    lanes = width // group


    def prepare(r):
        index = lax.axis_index("pb")
        r.wide_x[...] = r.x[...].astype(F32)
        r.wide_g[...] = r.g[...].astype(F32)
        for k in range(group):
            source = (index ^ k) * own
            piece = r.rows[k]
            piece[...] = jnp.zeros(piece.shape, BF16)
            for i in range(own):
                piece[i, 0:chunk, :] = r.wide_x[:, source + i, :].astype(BF16)
                piece[own + 1 + i, 0:chunk, :] = r.wide_g[:, source + i, :].astype(BF16)
            piece[own, 0:chunk, :] = r.e[...]

    prepared = run(
        prepare,
        dict(
            x=(decoder_input.transpose(1, 0, 2), VM),
            e=(query_embed, VM),
            g=(out_cotangent.transpose(1, 0, 2), VM),
        ),
        dict(rows=([(2 * own + 1, slot, width)] * group, BF16, VM)),
        dict(wide_x=((chunk, items, width), F32), wide_g=((chunk, items, width), F32)),
        microseconds=1.0,
    )
    row_parts = exchange(prepared.rows, "pb")

    table = np.zeros((group, part, width), np.float32)
    table[:, :quarter] = sinusoid(tokens, width).reshape(group, quarter, width)
    table = jnp.asarray(table.reshape(span, width))

    def project_memory(r):
        for i in range(own):
            source = r.memory[i]
            for q in range(group):
                r.plain[i, q * part : q * part + quarter, :] = source[q * quarter : (q + 1) * quarter, :]
                if part > quarter:
                    r.plain[i, q * part + quarter : (q + 1) * part, :] = jnp.zeros((part - quarter, width), BF16)
            r.keyed[i] = (r.plain[i].astype(F32) + r.table[...]).astype(BF16)
            r.keys[i] = nn(r.keyed[i], r.wk[...]).astype(BF16)
            r.put_part(i, keys=None, keyed=None)
            r.values[i] = (nn(r.plain[i], r.wv[...]) + r.bv[...].astype(F32).reshape(1, width)).astype(BF16)
            r.put_part(i, values=None, plain=None)

    memory_block = ((own, span, width), BF16, DMA)
    prj = run(
        project_memory,
        dict(
            memory=(memory, OWN),
            table=(table, DMA),
            wk=(cross_key, DMA),
            wv=(cross_value, DMA),
            bv=(cross_value_bias, VM),
        ),
        dict(keys=memory_block, values=memory_block, keyed=memory_block, plain=memory_block),
        after=prepared.rows[:1],
        microseconds=7.0,
    )
    memory_keys, memory_values, keyed, plain = prj.keys, prj.values, prj.keyed, prj.plain

    vectors = [
        self_query_bias,
        self_value_bias,
        self_out_bias,
        norm_one_gain,
        norm_one_bias,
        cross_query_bias,
        cross_out_bias,
        norm_two_gain,
        norm_two_bias,
        project_bias,
        norm_three_gain,
        norm_three_bias,
    ]
    BQ, BV, BO, G1, B1, BCQ, BCO, G2, B2, BP, G3, B3 = range(12)

    def vector(r, place):
        return r.vectors[place][...].astype(F32).reshape(1, width)

    def staggered(tasks, first, second):
        for n in range(len(tasks) + 1):
            if n < len(tasks):
                first(n, *tasks[n])
            if n > 0:
                second(n - 1, *tasks[n - 1])

    def attend(queries, keys, values, kept, inverse, buffers, bias, results):
        parts = {}

        def first(n, i, g):
            cols = slice(g * wide, (g + 1) * wide)
            shift = jnp.concatenate([bias(i)] * (many // 128), axis=1)
            buffers[n % 2][...] = nt(keys(i, cols), spread_heads(queries(i)[:, cols], head)) + shift

        def second(n, i, g):
            cols = slice(g * wide, (g + 1) * wide)
            big = slice(g * many, (g + 1) * many)
            scores = buffers[n % 2][...]
            highest = jnp.max(scores, axis=0, keepdims=True)
            raised = jnp.exp(scores - highest)
            total = jnp.sum(raised, axis=0, keepdims=True)
            kept[i, :, big] = raised.astype(BF16)
            back = 1.0 / total
            inverse[i, :, big] = jnp.broadcast_to(back, (8, many))
            parts[g] = diagonal(tn(values(i, cols), kept[i, :, big]) * back, head, rows)
            if g == groups - 1:
                results[i * rows : (i + 1) * rows, :] = jnp.concatenate(
                    [parts[j] for j in range(groups)], axis=0
                ).T.astype(BF16)

        staggered([(i, g) for i in range(own) for g in range(groups)], first, second)

    def forward(r):
        x_buf, e_buf = r.x0, r.embed
        for k in range(group):
            piece = r.rows[k]
            for i in range(own):
                x_buf[i * rows + k * slot : i * rows + (k + 1) * slot, :] = piece[i]
                e_buf[i * rows + k * slot : i * rows + (k + 1) * slot, :] = piece[own].astype(F32)
        r.put(x0=None)
        a_in = (x_buf[...].astype(F32) + e_buf[...]).astype(BF16)
        r.put(a_in=a_in)
        queries = (nn(a_in, r.wq[...]) + vector(r, BQ)).astype(BF16)
        r.put(q1=(queries.astype(F32) * scale).astype(BF16))
        r.put(k1=nn(a_in, r.wk[...]).astype(BF16))
        r.put(v1=(nn(x_buf[...], r.wv[...]) + vector(r, BV)).astype(BF16))

        row = lax.broadcasted_iota(jnp.int32, (rows, 128), 0) % slot
        r.self_bias[...] = jnp.where(row < chunk, 0.0, -1e30)
        attend(
            lambda i: r.q1[i * rows : (i + 1) * rows, :],
            lambda i, cols: r.k1[i * rows : (i + 1) * rows, cols],
            lambda i, cols: r.v1[i * rows : (i + 1) * rows, cols],
            r.e1,
            r.inv1,
            (r.self_scores, r.self_scores_two),
            lambda i: r.self_bias[...],
            r.o1,
        )
        r.put(e1=None)
        r.put(inv1=None)
        r.put(o1=None)
        summed = x_buf[...].astype(F32) + nn(r.o1[...], r.wo[...]) + vector(r, BO)
        unit, spread, normed = norm_forward(summed, vector(r, G1), vector(r, B1))
        r.put(unit1=unit)
        r.put(spread1=spread)
        r.normed[...] = normed
        r.put(c_in=(normed + e_buf[...]).astype(BF16))
        queries = (nn(r.c_in[...], r.wcq[...]) + vector(r, BCQ)).astype(BF16)
        r.put(q2=(queries.astype(F32) * scale).astype(BF16))
        for i in range(own):
            length = r.lengths[lax.axis_index("pb") * own + i]
            row = lax.broadcasted_iota(jnp.int32, (part, 128), 0)
            for q in range(group):
                seen = (row + q * quarter < length) & (row < quarter)
                r.cross_bias[i, q * part : (q + 1) * part, :] = jnp.where(seen, 0.0, -1e30)
        attend(
            lambda i: r.q2[i * rows : (i + 1) * rows, :],
            lambda i, cols: r.keys[i, :, cols],
            lambda i, cols: r.values[i, :, cols],
            r.e2,
            r.inv2,
            (r.cross_scores, r.cross_scores_two),
            lambda i: r.cross_bias[i],
            r.o2,
        )
        r.put(e2=None)
        r.put(inv2=None)
        r.put(o2=None)
        summed = r.normed[...] + nn(r.o2[...], r.wco[...]) + vector(r, BCO)
        unit, spread, normed = norm_forward(summed, vector(r, G2), vector(r, B2))
        r.put(unit2=unit)
        r.put(spread2=spread)
        r.normed[...] = normed
        r.put(x2b=normed.astype(BF16))
        r.third[...] = normed + vector(r, BP)
        for j in range(HIDDEN_CHUNKS):
            cols = slice(j * step, (j + 1) * step)
            before = nn(r.x2b[...], r.we[:, cols]) + r.be[cols].astype(F32).reshape(1, step)
            share_below = 0.5 + 0.5 * lax.erf(before * (0.5**0.5))
            density = jnp.exp(-0.5 * before * before) * ((2.0 * math.pi) ** (-0.5))
            r.slope[:, cols] = share_below + before * density
            active = (before * share_below).astype(BF16)
            r.third[...] += nn(active, r.wp[cols, :])
            r.active_t[cols, :] = active.T
        index = lax.axis_index("pb")

        def ship(source, kept, sent):
            for y in range(group // 2):
                for c, target in ((0, kept), (1, sent)):
                    first = pl.multiple_of((index ^ (2 * y + c)) * share, 16)
                    target[y] = source[pl.ds(first, share), :]

        ship(r.active_t, r.act_keep, r.act_send)
        r.put(act_send=None, act_keep=None)
        unit, spread, normed = norm_forward(r.third[...], vector(r, G3), vector(r, B3))
        low = normed.astype(BF16)
        cot = r.cot
        for k in range(group):
            piece = r.rows[k]
            for i in range(own):
                here = slice(i * rows + k * slot, i * rows + (k + 1) * slot)
                (r.near[k] if k < 2 else r.far.at[k - 2])[i] = low[here, :]
                cot[here, :] = piece[own + 1 + i].astype(F32)
        r.put(near=0)
        r.put(near=1)
        r.put(far=None)
        sums = r.sums
        sums[...] = jnp.zeros(sums.shape, F32)
        sums[0:1, :] = column_sum(cot[...] * unit)
        sums[1:2, :] = column_sum(cot[...])
        third = norm_backward(cot[...], unit, spread, vector(r, G3))
        r.put(dr3=third)
        branch = third.astype(BF16)
        r.put(df=branch)
        sums[2:3, :] = column_sum(branch)
        r.put(sums=None)
        for j in range(HIDDEN_CHUNKS):
            cols = slice(j * step, (j + 1) * step)
            grad = (nt(r.df[...], r.wp[cols, :]) * r.slope[:, cols]).astype(BF16)
            r.dh[:, cols] = grad
            r.hidden_sum[:, cols] = column_sum(grad)
            r.active_t[cols, :] = grad.T
        ship(r.active_t, r.dh_keep, r.dh_send)
        r.put(dh_send=None, dh_keep=None, dh=None, hidden_sum=None)

    two = group // 2
    fw = run(
        forward,
        dict(
            lengths=(lengths, SM),
            rows=(row_parts, VM),
            vectors=(vectors, VM),
            be=(expand_bias, VM),
            wq=(self_query, DMA),
            wk=(self_key, DMA),
            wv=(self_value, DMA),
            wo=(self_out, DMA),
            wcq=(cross_query, DMA),
            keys=(memory_keys, DMA),
            values=(memory_values, DMA),
            wco=(cross_out, DMA),
            we=(expand_weight, DMA),
            wp=(project_weight, DMA),
        ),
        dict(

            x0=((all_rows, width), BF16, DMA),
            a_in=((all_rows, width), BF16, DMA),
            q1=((all_rows, width), BF16, DMA),
            k1=((all_rows, width), BF16, DMA),
            v1=((all_rows, width), BF16, DMA),
            e1=((own, rows, groups * many), BF16, DMA),
            inv1=((own, 8, groups * many), F32, DMA),
            o1=((all_rows, width), BF16, DMA),
            unit1=((all_rows, width), F32, DMA),
            spread1=((all_rows, 1), F32, DMA),
            c_in=((all_rows, width), BF16, DMA),
            q2=((all_rows, width), BF16, DMA),
            e2=((own, span, groups * many), BF16, DMA),
            inv2=((own, 8, groups * many), F32, DMA),
            o2=((all_rows, width), BF16, DMA),
            unit2=((all_rows, width), F32, DMA),
            spread2=((all_rows, 1), F32, DMA),
            x2b=((all_rows, width), BF16, DMA),
            act_keep=((two, share, all_rows), BF16, DMA),
            act_send=((two, share, all_rows), BF16, DMA),
            dr3=((all_rows, width), F32, DMA),
            df=((all_rows, width), BF16, DMA),
            dh=((all_rows, hidden), BF16, DMA),
            dh_keep=((two, share, all_rows), BF16, DMA),
            dh_send=((two, share, all_rows), BF16, DMA),
            sums=((8, width), F32, DMA),
            hidden_sum=((1, hidden), F32, DMA),
        near=([(own, slot, width)] * 2, BF16, DMA),
            far=((2, own, slot, width), BF16, DMA),
        ),
        dict(
            embed=((all_rows, width), F32),
            self_scores=((rows, many), F32),
            self_scores_two=((rows, many), F32),
            self_bias=((rows, 128), F32),
            cross_scores=((span, many), F32),
            cross_scores_two=((span, many), F32),
            cross_bias=((own, span, 128), F32),
            normed=((all_rows, width), F32),
            third=((all_rows, width), F32),
            cot=((all_rows, width), F32),
            slope=((all_rows, hidden), F32),
            active_t=((hidden, all_rows), BF16),
        ),
        microseconds=18.0,
    )

    project_order = list(ba_bits)
    expand_order = [ba_bits[1], ba_bits[0]] + list(ba_bits[2:])
    half = width // 2

    def row_place(steps, relative, y):
        place_of = 0
        for axis, bit in steps:
            place_of = 2 * place_of + (y if axis == "pb" else relative // bit % 2)
        return place_of

    def pack(r, grad, region, offset):
        base, steps, size = region
        index, here = lax.axis_index("pb"), lax.axis_index("ba")
        for relative in range(ba_size):
            for y in range(two):
                first = base + row_place(steps, relative, y) * size + offset
                for c, target in ((0, r.keep), (1, r.send)):
                    source = pl.multiple_of((here ^ relative) * block, 8)
                    column = pl.multiple_of((index ^ (2 * y + c)) * lanes, 128)
                    target[first : first + block, :] = grad[pl.ds(source, block), pl.ds(column, lanes)].astype(BF16)

    later = [("pb", 2)] + [("ba", bit) for bit in ba_bits[2:]]
    copies = ba_size * two
    cross_size = 4 * block
    embed_rows = slot // 2
    self_size = 4 * block + embed_rows
    self_region = (0, [("ba", ba_bits[0]), ("ba", ba_bits[1])] + later, self_size)
    cross_region = (copies * self_size, [("ba", ba_bits[1]), ("ba", ba_bits[0])] + later, cross_size)
    vector_count = 13 * width + hidden
    extra = padded_to(vector_count // 128, 16)
    cut = part // 48 * 16
    packed = (copies * (self_size + cross_size) + extra, lanes)

    def attend_back(queries, grads, keys, values, kept, inverse, scores, logits, results, grad_keys, grad_values, finished=None):
        parts = {}
        spreads = {}

        def first(n, i, g):
            cols = slice(g * wide, (g + 1) * wide)
            back = inverse[i, 0:1, g * many : (g + 1) * many]
            upright = jnp.broadcast_to(back, (128, many)).T
            lane = lax.broadcasted_iota(jnp.int32, (1, wide), 1) // head
            piece = grads(i)[:, cols].astype(F32)
            spreads[n] = jnp.concatenate(
                [
                    (piece * upright[h * rows : (h + 1) * rows, 0:1]).astype(BF16)
                    * (lane == h).astype(F32).astype(BF16)
                    for h in range(GROUP_HEADS)
                ],
                axis=0,
            )
            scores[n % 2][...] = nt(values(i, cols), spreads[n])

        def second(n, i, g):
            cols = slice(g * wide, (g + 1) * wide)
            big = slice(g * many, (g + 1) * many)
            score, logit = scores[n % 2], logits[n % 2]
            back = inverse[i, 0:1, big]
            inner = jnp.sum(kept[i, :, big].astype(F32) * score[...], axis=0, keepdims=True)
            logit[...] = (kept[i, :, big].astype(F32) * (score[...] - inner * back)).astype(BF16)
            grad_values(i, cols, nn(kept[i, :, big], spreads[n]))
            grad_keys(i, cols, nn(logit[...], spread_heads(queries(i)[:, cols], head)))
            parts[g] = diagonal(tn(keys(i, cols), logit[...]), head, rows)
            if g == groups - 1:
                whole = jnp.concatenate([parts[j] for j in range(groups)], axis=0)
                results[i * rows : (i + 1) * rows, :] = (whole.T * scale).astype(BF16)
                if finished:
                    finished(i)

        staggered([(i, g) for i in range(own) for g in range(groups)], first, second)

    def cross_back(r):
        grad = r.dr3[...] + nt(r.dh[...], r.we[...])
        sums = r.sums
        sums[...] = jnp.zeros(sums.shape, F32)
        unit = r.unit2[...]
        sums[0:1, :] = column_sum(grad * unit)
        sums[1:2, :] = column_sum(grad)
        dr2 = norm_backward(grad, unit, r.spread2[...], vector(r, G2))
        r.put(dr2=dr2)
        branch = dr2.astype(BF16)
        sums[2:3, :] = column_sum(branch)
        r.put(ds2=branch)
        r.do2[...] = nt(branch, r.wco[...]).astype(BF16)
        def grad_keys(i, cols, value):
            r.dk[i, :, cols] = value.astype(BF16)

        def grad_values(i, cols, value):
            r.dv[i, :, cols] = value.astype(BF16)

        index = lax.axis_index("pb")
        def memory_back(i):
            r.put_part(i, dk=None, dv=None)
            for k in range(group - 1, -1, -1):
                edge = pl.ds(pl.multiple_of((index ^ k) * part, 16), part)
                value = (nt(r.dk[i, edge, :], r.wck[...]) + nt(r.dv[i, edge, :], r.wcv[...])).astype(BF16)
                if k < 2:
                    r.near[k][i] = value
                elif k == 3:
                    r.far_big[i * part : (i + 1) * part, :] = value
                elif i < own - 1:
                    r.far_small[i * part : (i + 1) * part, :] = value
                else:
                    r.far_small[i * part : i * part + cut, :] = value[:cut]
                    r.far_third[...] = value[cut:]

        attend_back(
            lambda i: r.q2[i * rows : (i + 1) * rows, :],
            lambda i: r.do2[i * rows : (i + 1) * rows, :],
            lambda i, cols: r.keys[i, :, cols],
            lambda i, cols: r.values[i, :, cols],
            r.e2,
            r.inv2,
            (r.scores, r.scores_two),
            (r.logit, r.logit_two),
            r.dq,
            grad_keys,
            grad_values,
            memory_back,
        )
        r.put(far_big=None, far_small=None, far_third=None)
        r.put(near=0)
        r.put(near=1)
        r.put(dq=None)
        sums[3:4, :] = column_sum(r.dq[...])
        total = jnp.zeros((1, width), F32)
        for i in range(own):
            total = total + column_sum(r.dv[i])
        sums[4:5, :] = total
        r.put(sums=None)
        r.put(dc=nt(r.dq[...], r.wcq[...]))

    act_got = swap(fw.act_send, "pb", 1)
    x2b_got = swap(fw.x2b, "pb", 1)
    df_got = swap(fw.df, "pb", 1)
    dh_got = swap(fw.dh_send, "pb", 1)
    back = run(
        cross_back,
        dict(
            vectors=(vectors, VM),
            dh=(fw.dh, DMA),
            we=(expand_weight, DMA),
            dr3=(fw.dr3, DMA),
            unit2=(fw.unit2, DMA),
            spread2=(fw.spread2, DMA),
            wco=(cross_out, DMA),
            values=(memory_values, DMA),
            inv2=(fw.inv2, DMA),
            e2=(fw.e2, DMA),
            q2=(fw.q2, DMA),
            keys=(memory_keys, DMA),
            wck=(cross_key, DMA),
            wcv=(cross_value, DMA),
            wcq=(cross_query, DMA),
        ),
        dict(
            near=([(own, part, width)] * 2, BF16, DMA),
            far_big=((own * part, width), BF16, DMA),
            far_small=(((own - 1) * part + cut, width), BF16, DMA),
            far_third=((part - cut, width), BF16, DMA),
            dq=((all_rows, width), BF16, DMA),
            dc=((all_rows, width), F32, DMA),
            dk=((own, span, width), BF16, DMA),
            dv=((own, span, width), BF16, DMA),
            dr2=((all_rows, width), F32, DMA),
            ds2=((all_rows, width), BF16, DMA),
            sums=((8, width), F32, DMA),
        ),
        dict(do2=((all_rows, width), BF16), scores=((span, many), F32), scores_two=((span, many), F32), logit=((span, many), BF16), logit_two=((span, many), BF16)),
        microseconds=20.0,
        most=63 * 2**20 + 2**19,
    )


    def cross_weights(r):
        grad = r.grad
        grad[...] = tn(r.o2[...], r.ds2[...])
        pack(r, grad, cross_region, 3 * block)
        grad[...] = tn(r.c_in[...], r.cross_dq[...])
        pack(r, grad, cross_region, 0 * block)
        grad[...] = tn(r.plain[0], r.cross_dv[0])
        for i in range(1, own):
            grad[...] += tn(r.plain[i], r.cross_dv[i])
        pack(r, grad, cross_region, 2 * block)
        grad[...] = tn(r.keyed[0], r.cross_dk[0])
        for i in range(1, own):
            grad[...] += tn(r.keyed[i], r.cross_dk[i])
        pack(r, grad, cross_region, 1 * block)

    def rest_back(r):
        grad = r.dr2[...] + r.dc[...]
        sums = r.sums
        sums[...] = jnp.zeros(sums.shape, F32)
        unit = r.unit1[...]
        sums[0:1, :] = column_sum(grad * unit)
        sums[1:2, :] = column_sum(grad)
        first = r.first
        first[...] = norm_backward(grad, unit, r.spread1[...], vector(r, G1))
        branch = first[...].astype(BF16)
        sums[2:3, :] = column_sum(branch)
        whole = r.grad
        whole[...] = tn(r.o1[...], branch)
        pack(r, whole, self_region, 3 * block)
        r.do1[...] = nt(branch, r.wo[...]).astype(BF16)
        def grad_keys(i, cols, value):
            r.dk[i * rows : (i + 1) * rows, cols] = value.astype(BF16)

        def grad_values(i, cols, value):
            r.dv[i * rows : (i + 1) * rows, cols] = value.astype(BF16)

        attend_back(
            lambda i: r.q1[i * rows : (i + 1) * rows, :],
            lambda i: r.do1[i * rows : (i + 1) * rows, :],
            lambda i, cols: r.k1[i * rows : (i + 1) * rows, cols],
            lambda i, cols: r.v1[i * rows : (i + 1) * rows, cols],
            r.e1,
            r.inv1,
            (r.scores, r.scores_two),
            (r.logit, r.logit_two),
            r.dq,
            grad_keys,
            grad_values,
        )
        dq, dk, dv = r.dq[...], r.dk[...], r.dv[...]
        sums[3:4, :] = column_sum(dq)
        sums[4:5, :] = column_sum(dv)
        both = nt(dq, r.wq[...]) + nt(dk, r.wk[...])
        low = (first[...] + both + nt(dv, r.wv[...])).astype(BF16)
        for k in range(group):
            for i in range(own):
                (r.near[k] if k < 2 else r.far.at[k - 2])[i] = low[i * rows + k * slot : i * rows + (k + 1) * slot, :]
        for j in range(2):
            r.near[j][own:] = r.out_near[j][...]
            r.far[j, own:] = r.out_far[j]
        r.put(near=0)
        r.put(near=1)
        r.put(far=None)
        both = both + r.dc[...]
        embed = both[0:rows]
        for i in range(1, own):
            embed = embed + both[i * rows : (i + 1) * rows]
        embed = nn(embed.astype(BF16), permutation(project_order, width, ba_size)).astype(BF16)
        order_bits = project_order
        for position in range(ba_size):
            relative = sum(((position >> (len(order_bits) - 1 - b)) & 1) * bit for b, bit in enumerate(order_bits))
            for y in range(two):
                first = row_place(self_region[1], relative, y) * self_size + 4 * block
                for c, target in ((0, r.keep), (1, r.send)):
                    k = 2 * y + c
                    piece = embed[k * slot : (k + 1) * slot, position * block : (position + 1) * block]
                    gap = [jnp.zeros((embed_rows, lanes // 2 - block), BF16)] if block < lanes // 2 else []
                    filled = jnp.concatenate([piece[:embed_rows]] + gap + [piece[embed_rows:]] + gap, axis=1)
                    target[first : first + embed_rows, :] = filled
        table_rows = r.rows
        table_rows[...] = jnp.zeros(table_rows.shape, F32)
        sources = [
            (sums, 3),
            (sums, 4),
            (sums, 2),
            (sums, 0),
            (sums, 1),
            (r.sums_s, 3),
            (r.sums_s, 4),
            (r.sums_s, 2),
            (r.sums_s, 0),
            (r.sums_s, 1),
            (r.sums_f, 2),
            (r.sums_f, 0),
            (r.sums_f, 1),
        ] + [(r.hidden_sum, None)]
        filled_rows = 0
        for source, place_of in sources:
            place_of = place_of or 0
            for j in range(source.shape[1] // 128):
                table_rows[filled_rows : filled_rows + 1, :] = source[place_of : place_of + 1, j * 128 : (j + 1) * 128]
                filled_rows += 1
        low_rows = table_rows[...].astype(BF16)
        r.keep[packed[0] - extra :, :] = low_rows
        r.send[packed[0] - extra :, :] = low_rows
        for matrix, left, right in ((0, r.a_in, dq), (1, r.a_in, dk), (2, r.x0, dv)):
            whole[...] = tn(left[...], right)
            pack(r, whole, self_region, matrix * block)
        cross_weights(r)
        r.put(send=None, keep=None)

    act_got, x2b_got, df_got, dh_got, hidden_start = meet(act_got, x2b_got, df_got, dh_got, back.ds2)

    def hidden_grads(r):
        r.perm[...] = permutation(project_order, width, ba_size)
        tile = width // 4

        def columns(rows, swapped):
            value = nn(rows, r.perm[...]).astype(BF16)
            tiles = [value[:, t * tile : (t + 1) * tile] for t in ((0, 2, 1, 3) if swapped else range(4))]
            return jnp.concatenate(tiles, axis=1)

        def one(swapped, keep, got, rows_own, rows_got, kept, sent):
            own_cols = columns(rows_own(), swapped)
            got_cols = columns(rows_got(), swapped)
            for y in range(two):
                total = nn(keep()[y], own_cols) + nn(got()[y], got_cols)
                kept[y] = total[:, :half].astype(BF16)
                sent[y] = total[:, half:].astype(BF16)

        one(
            False,
            lambda: r.act_keep,
            lambda: r.act_got,
            lambda: r.df[...],
            lambda: r.df_got[...],
            r.p_keep,
            r.p_send,
        )
        r.put(p_send=None, p_keep=None)
        one(
            True,
            lambda: r.dh_keep,
            lambda: r.dh_got,
            lambda: r.x2b[...],
            lambda: r.x2b_got[...],
            r.e_keep,
            r.e_send,
        )
        r.put(e_send=None, e_keep=None)

    piece = ((two, share, half), BF16, DMA)
    hid = run(
        hidden_grads,
        dict(
            df=(tie(fw.df, hidden_start), DMA),
            df_got=(df_got, DMA),
            act_keep=(fw.act_keep, DMA),
            act_got=(act_got, DMA),
            x2b=(fw.x2b, DMA),
            x2b_got=(x2b_got, DMA),
            dh_keep=(fw.dh_keep, DMA),
            dh_got=(dh_got, DMA),
        ),
        dict(p_keep=piece, p_send=piece, e_keep=piece, e_send=piece),
        dict(perm=((width, width), BF16)),
        microseconds=4.0,
    )

    p_send, e_send, far_big, mem_near = meet(hid.p_send, hid.e_send, back.far_big, back.near[1])

    p_got = swap(p_send, "ba", ba_bits[0])
    e_got = swap(e_send, "ba", ba_bits[1])
    big_got = swap(far_big, "pb", 2)
    mem_other = swap(mem_near, "pb", 1)
    slf = run(
        rest_back,
        dict(
            vectors=(vectors, VM),
            dr2=(tie(back.dr2, p_send, e_send), DMA),
            dc=(back.dc, DMA),
            unit1=(fw.unit1, DMA),
            spread1=(fw.spread1, DMA),
            o1=(fw.o1, DMA),
            wo=(self_out, DMA),
            inv1=(fw.inv1, DMA),
            e1=(fw.e1, DMA),
            q1=(fw.q1, DMA),
            k1=(fw.k1, DMA),
            v1=(fw.v1, DMA),
            wq=(self_query, DMA),
            wk=(self_key, DMA),
            wv=(self_value, DMA),
            a_in=(fw.a_in, DMA),
            x0=(fw.x0, DMA),
            out_near=(fw.near, DMA),
            out_far=(fw.far, DMA),
            o2=(fw.o2, DMA),
            ds2=(back.ds2, DMA),
            c_in=(fw.c_in, DMA),
            cross_dq=(back.dq, DMA),
            cross_dv=(back.dv, DMA),
            plain=(plain, DMA),
            cross_dk=(back.dk, DMA),
            keyed=(keyed, DMA),
            sums_s=(back.sums, DMA),
            sums_f=(fw.sums, DMA),
            hidden_sum=(fw.hidden_sum, DMA),
        ),
        dict(
            keep=(packed, BF16, DMA),
            send=(packed, BF16, DMA),
            near=([(2 * own, slot, width)] * 2, BF16, DMA),
            far=((2, 2 * own, slot, width), BF16, DMA),
        ),
        dict(
            sums=((8, width), F32),
            rows=((extra, 128), F32),
            first=((all_rows, width), F32),
            grad=((width, width), F32),
            do1=((all_rows, width), BF16),
            dq=((all_rows, width), BF16),
            dk=((all_rows, width), BF16),
            dv=((all_rows, width), BF16),
            scores=((rows, many), F32),
            scores_two=((rows, many), F32),
            logit=((rows, many), BF16),
            logit_two=((rows, many), BF16),
        ),
        microseconds=7.0,
    )
    p_got, e_got, big_got, mem_other, send, far_small = meet(
        p_got, e_got, big_got, mem_other, slf.send, back.far_small
    )

    p_keep, p_send = halves(pair_sum(hid.p_keep, p_got), -1)
    e_keep, e_send = halves(pair_sum(hid.e_keep, e_got), -1)
    p_got = swap(p_send, "ba", ba_bits[1])
    e_got = swap(e_send, "ba", ba_bits[0])
    got = swap(send, "pb", 1)
    small_got = swap(far_small, "pb", 2)
    last = swap(big_got, "pb", 1)
    p_got, e_got, got, last, small_got, far_third = meet(p_got, e_got, got, last, small_got, back.far_third)

    edge = copies * self_size
    a_keep, a_send = sum_halves(slf.keep, got, 0, edge, extra)
    b_keep, b_send = sum_halves(slf.keep, got, edge, packed[0] - extra, 0)
    p_total, e_total = pair_sum(p_keep, p_got), pair_sum(e_keep, e_got)
    f_keep, f_send = (jnp.stack([p_total[y], e_total[y]]).astype(BF16) for y in range(two))
    a_got = swap(a_send, "ba", ba_bits[0])
    b_got = swap(b_send, "ba", ba_bits[1])
    f_got = swap(f_send, "pb", 2)
    third_got = swap(far_third, "pb", 2)
    a_got, b_got, f_got, third_got, home_near, home_far = meet(
        a_got, b_got, f_got, third_got, slf.near[1], slf.far
    )

    f_total = pair_sum(f_keep, f_got)
    f_half = f_total.shape[-1] // 2
    f_keep, f_send = (
        jnp.concatenate(
            [f_total[0, :, j * f_half : (j + 1) * f_half], f_total[1, :, j * f_half : (j + 1) * f_half]], axis=-1
        ).astype(BF16)
        for j in range(2)
    )
    a_keep, a_send = sum_halves(a_keep, a_got, 0, a_keep.shape[0] - extra, extra)
    b_keep, b_send = sum_halves(b_keep, b_got, 0, b_keep.shape[0], 0)
    a_got = swap(a_send, "ba", ba_bits[1])
    b_got = swap(b_send, "ba", ba_bits[0])
    home_other = swap(home_near, "pb", 1)
    home_across = swap(home_far, "pb", 2)

    def place_memory(r):
        index = lax.axis_index("pb")
        for i in range(own):
            last = r.last[i * part : i * part + quarter, :]
            if i < own - 1:
                across = r.across[i * part : i * part + quarter, :]
            else:
                across = jnp.concatenate(
                    [r.across[i * part : i * part + cut, :], r.third[0 : quarter - cut, :]], axis=0
                )
            for k, piece in enumerate((r.mine[i, 0:quarter, :], r.other[i, 0:quarter, :], across, last)):
                r.wide[:, (index ^ k) * own + i, :] = piece.astype(F32)
        r.put(whole=r.wide[...].astype(BF16))

    memory_grad = run(
        place_memory,
        dict(
            mine=(tie(back.near[0], f_send, a_send, b_send), DMA),
            other=(mem_other, DMA),
            across=(small_got, DMA),
            third=(third_got, DMA),
            last=(last, DMA),
        ),
        dict(whole=((quarter, items, width), BF16, DMA)),
        dict(wide=((quarter, items, width), F32)),
        microseconds=4.0,
        spare=4,
    ).whole
    f_send, a_got, b_got, home_other, home_across, memory_grad = meet(
        f_send, a_got, b_got, home_other, home_across, memory_grad
    )

    keep, send = row_halves(
        interleave(pair_sum(a_keep, a_got), pair_sum(b_keep, b_got), self_size, cross_size, extra), extra
    )
    got = swap(send, "pb", 2)
    f_got = swap(f_send, "ba", ba_bits[2])
    home_last = swap(home_across[1], "pb", 1)
    got, f_got, home_last = meet(got, f_got, home_last)

    keep, send = row_halves(pair_sum(keep, got), extra)
    got = swap(send, "ba", ba_bits[2])
    hidden_out = pair_sum(f_keep, f_got)
    project_out, expand_out = (
        finish(part_out, ba_bits[3:], lambda total: halves(total, -1))
        for part_out in (hidden_out[:, :f_half], hidden_out[:, f_half:])
    )
    expand_out = expand_out.T

    def place_rows(r):
        index = lax.axis_index("pb")
        for i in range(own):
            for k in range(group):
                source = (r.mine, r.other, r.across.at[0], r.last)[k]
                r.wide[:, (index ^ k) * own + i, :] = source[i, 0:chunk, :].astype(F32)
                r.wide_out[:, (index ^ k) * own + i, :] = source[own + i, 0:chunk, :].astype(F32)
        r.put(grad=r.wide[...].astype(BF16))
        r.put(out=r.wide_out[...].astype(BF16))

    wide_rows = (chunk, items, width)
    rows_home = run(
        place_rows,
        dict(
            mine=(tie(slf.near[0], send), DMA),
            other=(home_other, DMA),
            across=(home_across, DMA),
            last=(home_last, DMA),
        ),
        dict(grad=(wide_rows, BF16, DMA), out=(wide_rows, BF16, DMA)),
        dict(wide=(wide_rows, F32), wide_out=(wide_rows, F32)),
        microseconds=2.0,
        spare=4,
    )
    input_grad, layer_output = rows_home.grad, rows_home.out
    addends = [keep, got]
    if len(ba_bits) > 3:
        addends = [finish(pair_sum(keep, got), ba_bits[3:], lambda total: row_halves(total, extra))]
    places = [m * block for m in range(4)] + [self_size + m * block for m in range(4)]
    vector_rows = [width // 128] * 13 + [hidden // 128]

    def spread_out(r):
        total = r.addends[0][...].astype(F32)
        for j in range(1, len(addends)):
            total = total + r.addends[j][...].astype(F32)
        r.total[...] = total
        for m, first in enumerate(places):
            r.squares[m][...] = r.total[first : first + block, :]
        for j in range(2):
            count = min(embed_rows, chunk - j * embed_rows)
            left = j * lanes // 2
            r.embed[j * embed_rows : j * embed_rows + count, :] = r.total[
                4 * block : 4 * block + count, left : left + block
            ]
        first = addends[0].shape[0] - extra
        for j, count in enumerate(vector_rows):
            r.vectors[j][...] = r.total[first : first + count, :]
            first += count

    ends = run(
        spread_out,
        dict(addends=(addends, VM)),
        dict(
            squares=([(block, lanes)] * 8, F32, VM),
            embed=((chunk, block), F32, VM),
            vectors=([(count, 128) for count in vector_rows], F32, VM),
        ),
        dict(total=(addends[0].shape, F32)),
        microseconds=1.0,
        spare=4,
    )
    input_grad, layer_output = input_grad.transpose(1, 0, 2), layer_output.transpose(1, 0, 2)
    memory_grad = memory_grad.transpose(1, 0, 2)
    squares, vecs = ends.squares, [vector_out.reshape(-1) for vector_out in ends.vectors]

    return (
        layer_output,
        input_grad,
        memory_grad,
        ends.embed,
        squares[0],
        vecs[0],
        squares[1],
        squares[2],
        vecs[1],
        squares[3],
        vecs[2],
        vecs[3],
        vecs[4],
        squares[4],
        vecs[5],
        squares[5],
        squares[6],
        vecs[6],
        squares[7],
        vecs[7],
        vecs[8],
        vecs[9],
        expand_out,
        vecs[13],
        project_out,
        vecs[10],
        vecs[11],
        vecs[12],
    )


def solution(mesh):
    rows = P("ba", "pb", None)
    copied = P()
    placed = (rows, P("ba", None, None), P("ba"), P("pb", None)) + (copied,) * 24 + (rows,)
    square = P("ba", "pb")
    return jax.shard_map(
        local,
        mesh=mesh,
        in_specs=placed,
        out_specs=(
            rows,
            rows,
            rows,
            P("pb", "ba"),
            square,
            copied,
            square,
            square,
            copied,
            square,
            copied,
            copied,
            copied,
            square,
            copied,
            square,
            square,
            copied,
            square,
            copied,
            copied,
            copied,
            square,
            copied,
            P("pb", "ba"),
            copied,
            copied,
            copied,
        ),
        check_vma=False,
    )
```

```python
import math

import jax
import jax.numpy as jnp
import numpy as np
from jax import lax
from jax.experimental import pallas as pl
from jax.experimental.pallas import tpu as pltpu
from jax.sharding import PartitionSpec as P

HEADS = 8
GROUP_HEADS = 4
F32 = jnp.float32
BF16 = jnp.bfloat16
HIDDEN_CHUNKS = 5
VMEM_BYTES = 58 * 2**20


def sinusoid(count, model_width):
    position = np.arange(count, dtype=np.float32)
    column = np.arange(model_width // 2, dtype=np.float32)
    frequency = np.exp(column * np.float32(-2.0 * math.log(10000.0) / model_width)).astype(np.float32)
    angles = (position[:, None] * frequency[None, :]).astype(np.float32)
    table = np.stack([np.sin(angles), np.cos(angles)], axis=-1)
    return table.reshape(count, model_width).astype(np.float32)


def padded_to(extent, multiple):
    return -(-extent // multiple) * multiple


def nn(left, right):
    return lax.dot_general(left, right, (((1,), (0,)), ((), ())), preferred_element_type=F32)


def nt(left, right):
    return lax.dot_general(left, right, (((1,), (1,)), ((), ())), preferred_element_type=F32)


def tn(left, right):
    return lax.dot_general(left, right, (((0,), (0,)), ((), ())), preferred_element_type=F32)


VM, SM, DMA, OWN, RAW = range(5)


class Named:
    def __init__(self, find):
        self.find = find

    def __getattr__(self, key):
        return self.find(key)


class Numbered:
    def __init__(self, find, key):
        self.find, self.key = find, key

    def __getitem__(self, place):
        return self.find((self.key, place))


def flat(entries):
    result = {}
    for key, (value, *rest) in entries.items():
        if isinstance(value, list):
            for place, member in enumerate(value):
                result[(key, place)] = (member, *rest)
        else:
            result[key] = (value, *rest)
    return result


def run(body, ins, outs, scratch=None, after=(), microseconds=5.0, spare=64, most=VMEM_BYTES):
    listed = {key for entries in (ins, outs) for key, entry in entries.items() if isinstance(entry[0], list)}
    ins, outs, scratch = flat(ins), flat(outs), scratch or {}
    in_dma = [key for key, entry in ins.items() if entry[1] in (DMA, OWN)]
    out_dma = [key for key, entry in outs.items() if entry[2] == DMA]

    def kernel(*refs):
        refs = list(refs)
        held = {key: refs.pop(0) for key in ins}
        del refs[: len(after)]
        results = {key: refs.pop(0) for key in outs}
        arrived = {key: refs.pop(0) for key in in_dma}
        leaving = {key: refs.pop(0) for key in out_dma}
        held.update(results)
        sources = {key: held[key] for key in in_dma}
        held.update(arrived)
        held.update(leaving)
        held.update({key: refs.pop(0) for key in scratch})
        in_sem, out_sem, part_sem, row_sem = refs
        pending = {}
        for place, key in enumerate(in_dma):
            source = sources[key]
            if ins[key][1] == OWN:
                count = arrived[key].shape[0]
                source = source.at[pl.ds(lax.axis_index("pb") * count, count)]
            pending[key] = pltpu.make_async_copy(source, arrived[key], in_sem.at[place])
            pending[key].start()
        started = {}

        def find(key):
            if key in listed:
                return Numbered(find, key)
            if key in pending:
                pending.pop(key).wait()
            return held[key]

        def put(**values):
            for key, value in values.items():
                if key in listed:
                    key = (key, value)
                elif value is not None:
                    held[key][...] = value
                if key in leaving:
                    place = out_dma.index(key)
                    started[key] = pltpu.make_async_copy(leaving[key], results[key], out_sem.at[place])
                    started[key].start()

        def put_part(part, **values):
            for key in values:
                place = out_dma.index(key)
                copy = pltpu.make_async_copy(leaving[key].at[part], results[key].at[part], part_sem.at[place, part])
                copy.start()
                started[(key, part)] = copy
                started[key] = copy

        bag = Named(find)
        bag.put = put
        bag.put_part = put_part

        def push(key, source, target):
            copy = pltpu.make_async_copy(source, target(results[key]), row_sem.at[len(pushed)])
            copy.start()
            pushed.append(copy)
            started[key] = copy

        def put_rows(key, first, count):
            push(key, leaving[key].at[pl.ds(first, count)], lambda ref: ref.at[pl.ds(first, count)])

        pushed = []
        bag.push, bag.put_rows = push, put_rows
        body(bag)
        for key in list(pending):
            pending.pop(key).wait()
        for key in out_dma:
            assert key in started, key
        for copy in {id(copy): copy for copy in [*started.values(), *pushed]}.values():
            copy.wait()

    spaces = [pltpu.VMEM, pltpu.SMEM, pl.ANY, pl.ANY, pl.ANY]
    arrays = [entry[0] for entry in ins.values()]
    nbytes = sum(int(np.prod(array.shape)) * array.dtype.itemsize for array in arrays)
    held_bytes = sum(
        int(np.prod(shape)) * (4 if dtype == F32 else 2)
        for shape, dtype in [(entry[0].shape, entry[0].dtype) for entry in ins.values()]
        + [(entry[0], entry[1]) for entry in outs.values()]
        + list(scratch.values())
    )
    made = pl.pallas_call(
        kernel,
        out_shape=[jax.ShapeDtypeStruct(entry[0], entry[1]) for entry in outs.values()],
        in_specs=[pl.BlockSpec(memory_space=spaces[entry[1]]) for entry in ins.values()]
        + [pl.BlockSpec(memory_space=pl.ANY)] * len(after),
        out_specs=[pl.BlockSpec(memory_space=spaces[entry[2]]) for entry in outs.values()],
        scratch_shapes=[
            pltpu.VMEM(
                (ins[key][0].shape[0] // lax.axis_size("pb"), *ins[key][0].shape[1:])
                if ins[key][1] == OWN
                else ins[key][0].shape,
                ins[key][0].dtype,
            )
            for key in in_dma
        ]
        + [pltpu.VMEM(outs[key][0], outs[key][1]) for key in out_dma]
        + [pltpu.VMEM(shape, dtype) for shape, dtype in scratch.values()]
        + [pltpu.SemaphoreType.DMA((max(1, len(in_dma)),)), pltpu.SemaphoreType.DMA((max(1, len(out_dma)),)), pltpu.SemaphoreType.DMA((max(1, len(out_dma)), 2)), pltpu.SemaphoreType.DMA((8,))],
        compiler_params=pltpu.CompilerParams(vmem_limit_bytes=min(most, held_bytes + spare * 2**20)),
        cost_estimate=pl.CostEstimate(
            flops=int(microseconds * 1e3), bytes_accessed=1024, transcendentals=0
        ),
        name=body.__name__,
    )(*arrays, *after)
    by_key = dict(zip(outs, made))

    def result(key):
        if key in listed:
            return [value for name, value in by_key.items() if isinstance(name, tuple) and name[0] == key]
        return by_key[key]

    return Named(result)


def norm_forward(values, gain, shift):
    average = jnp.mean(values, axis=-1, keepdims=True)
    centred = values - average
    spread = jnp.mean(centred * centred, axis=-1, keepdims=True)
    scale = lax.rsqrt(spread + 1e-05)
    unit = centred * scale
    return unit, scale, unit * gain + shift


def norm_backward(grad, unit, scale, gain):
    lifted = grad * gain
    first = jnp.mean(lifted, axis=-1, keepdims=True)
    second = jnp.mean(lifted * unit, axis=-1, keepdims=True)
    return scale * (lifted - first - unit * second)


def column_sum(values):
    return jnp.sum(values.astype(F32), axis=0, keepdims=True)


def spread_heads(rows, width):
    count, columns = rows.shape
    lane = lax.broadcasted_iota(jnp.int32, (1, columns), 1) // width
    return jnp.concatenate(
        [rows * (lane == h).astype(F32).astype(BF16) for h in range(columns // width)], axis=0
    )


def diagonal(blocks, width, count):
    heads = blocks.shape[0] // width
    return jnp.concatenate(
        [blocks[h * width : (h + 1) * width, h * count : (h + 1) * count] for h in range(heads)], axis=0
    )


def swap(values, axis, bit):
    size = lax.axis_size(axis)
    return lax.ppermute(values, axis, [(i, i ^ bit) for i in range(size)])


def bits_of(size):
    return [1 << b for b in range(size.bit_length() - 1)]


def exchange(values, axis):
    size = lax.axis_size(axis)
    return [values[0]] + [swap(values[k], axis, k) for k in range(1, size)]


def pair_sum(kept, got):
    return kept.astype(F32) + got.astype(F32)


def meet(*arrays):
    return lax.optimization_barrier(arrays)


def tie(values, *before):
    return lax.optimization_barrier((values, *before))[0]


def halves(values, dim):
    dim = dim % values.ndim
    if values.shape[dim] == 2:
        parts = [lax.index_in_dim(values, j, dim, keepdims=False) for j in range(2)]
    else:
        half = values.shape[dim] // 2
        parts = [lax.slice_in_dim(values, j * half, (j + 1) * half, axis=dim) for j in range(2)]
    return parts[0].astype(BF16), parts[1].astype(BF16)


def row_halves(total, extra):
    body = total.shape[0] - extra
    parts = [total[: body // 2], total[body // 2 : body]]
    if extra:
        parts = [jnp.concatenate([part, total[body:]]) for part in parts]
    return parts[0].astype(BF16), parts[1].astype(BF16)


def sum_halves(kept, got, low, high, extra):
    def piece(first, last):
        return pair_sum(kept[first:last], got[first:last]).astype(BF16)

    middle = (low + high) // 2
    tail = [piece(kept.shape[0] - extra, kept.shape[0])] if extra else []
    return tuple(
        jnp.concatenate([piece(*edge)] + tail) if tail else piece(*edge) for edge in ((low, middle), (middle, high))
    )


def finish(total, bits, split):
    for bit in bits:
        kept, sent = split(total)
        total = pair_sum(kept, swap(sent, "ba", bit))
    return total


def interleave(first, second, first_size, second_size, extra):
    count = second.shape[0] // second_size
    body = jnp.concatenate(
        [
            first[: count * first_size].reshape(count, first_size, -1),
            second.reshape(count, second_size, -1),
        ],
        axis=1,
    )
    return jnp.concatenate([body.reshape(count * (first_size + second_size), -1), first[count * first_size :]])


def permutation(order, model_width, ba_size):
    mine = lax.axis_index("ba")
    width = model_width // ba_size
    column = lax.broadcasted_iota(jnp.int32, (1, model_width), 1)
    position = column // width
    relative = jnp.zeros_like(column)
    for step, bit in enumerate(order):
        digit = (position >> (len(order) - 1 - step)) & 1
        relative = relative + digit * bit
    source = (relative ^ mine) * width + column % width
    row = lax.broadcasted_iota(jnp.int32, (model_width, model_width), 0)
    return (row == source).astype(BF16)


def local(
    decoder_input,
    memory,
    lengths,
    query_embed,
    self_query,
    self_query_bias,
    self_key,
    self_value,
    self_value_bias,
    self_out,
    self_out_bias,
    norm_one_gain,
    norm_one_bias,
    cross_query,
    cross_query_bias,
    cross_key,
    cross_value,
    cross_value_bias,
    cross_out,
    cross_out_bias,
    norm_two_gain,
    norm_two_bias,
    expand_weight,
    expand_bias,
    project_weight,
    project_bias,
    norm_three_gain,
    norm_three_bias,
    out_cotangent,
):
    items, chunk, width = decoder_input.shape
    tokens = memory.shape[1]
    hidden = expand_weight.shape[1]
    group = lax.axis_size("pb")
    ba_size = lax.axis_size("ba")
    place = lax.axis_index("pb")
    mine = lax.axis_index("ba")
    own = items // group
    quarter = tokens // group
    slot = padded_to(chunk, 32)
    rows = group * slot
    all_rows = own * rows
    part = padded_to(quarter, 16)
    span = group * part
    head = width // HEADS
    scale = head ** (-0.5)
    share = hidden // group
    step = hidden // HIDDEN_CHUNKS
    wide = GROUP_HEADS * head
    many = GROUP_HEADS * rows
    groups = HEADS // GROUP_HEADS
    ba_bits = bits_of(ba_size)
    block = width // ba_size
    lanes = width // group


    def prepare(r):
        index = lax.axis_index("pb")
        r.wide_x[...] = r.x[...].astype(F32)
        r.wide_g[...] = r.g[...].astype(F32)
        for k in range(group):
            source = (index ^ k) * own
            piece = r.rows[k]
            piece[...] = jnp.zeros(piece.shape, BF16)
            for i in range(own):
                piece[i, 0:chunk, :] = r.wide_x[:, source + i, :].astype(BF16)
                piece[own + 1 + i, 0:chunk, :] = r.wide_g[:, source + i, :].astype(BF16)
            piece[own, 0:chunk, :] = r.e[...]

    prepared = run(
        prepare,
        dict(
            x=(decoder_input.transpose(1, 0, 2), VM),
            e=(query_embed, VM),
            g=(out_cotangent.transpose(1, 0, 2), VM),
        ),
        dict(rows=([(2 * own + 1, slot, width)] * group, BF16, VM)),
        dict(wide_x=((chunk, items, width), F32), wide_g=((chunk, items, width), F32)),
        microseconds=1.0,
    )
    row_parts = exchange(prepared.rows, "pb")

    table = np.zeros((group, part, width), np.float32)
    table[:, :quarter] = sinusoid(tokens, width).reshape(group, quarter, width)
    table = jnp.asarray(table.reshape(span, width))

    def project_memory(r):
        for i in range(own):
            source = r.memory[i]
            for q in range(group):
                r.plain[i, q * part : q * part + quarter, :] = source[q * quarter : (q + 1) * quarter, :]
                if part > quarter:
                    r.plain[i, q * part + quarter : (q + 1) * part, :] = jnp.zeros((part - quarter, width), BF16)
            r.keyed[i] = (r.plain[i].astype(F32) + r.table[...]).astype(BF16)
            r.keys[i] = nn(r.keyed[i], r.wk[...]).astype(BF16)
            r.put_part(i, keys=None, keyed=None)
            r.values[i] = (nn(r.plain[i], r.wv[...]) + r.bv[...].astype(F32).reshape(1, width)).astype(BF16)
            r.put_part(i, values=None, plain=None)

    memory_block = ((own, span, width), BF16, DMA)
    prj = run(
        project_memory,
        dict(
            memory=(memory, OWN),
            table=(table, DMA),
            wk=(cross_key, DMA),
            wv=(cross_value, DMA),
            bv=(cross_value_bias, VM),
        ),
        dict(keys=memory_block, values=memory_block, keyed=memory_block, plain=memory_block),
        after=prepared.rows[:1],
        microseconds=7.0,
    )
    memory_keys, memory_values, keyed, plain = prj.keys, prj.values, prj.keyed, prj.plain

    vectors = [
        self_query_bias,
        self_value_bias,
        self_out_bias,
        norm_one_gain,
        norm_one_bias,
        cross_query_bias,
        cross_out_bias,
        norm_two_gain,
        norm_two_bias,
        project_bias,
        norm_three_gain,
        norm_three_bias,
    ]
    BQ, BV, BO, G1, B1, BCQ, BCO, G2, B2, BP, G3, B3 = range(12)

    def vector(r, place):
        return r.vectors[place][...].astype(F32).reshape(1, width)

    def staggered(tasks, first, second):
        for n in range(len(tasks) + 1):
            if n < len(tasks):
                first(n, *tasks[n])
            if n > 0:
                second(n - 1, *tasks[n - 1])

    def attend(queries, keys, values, kept, inverse, buffers, bias, results):
        parts = {}

        def first(n, i, g):
            cols = slice(g * wide, (g + 1) * wide)
            shift = jnp.concatenate([bias(i)] * (many // 128), axis=1)
            buffers[n % 2][...] = nt(keys(i, cols), spread_heads(queries(i)[:, cols], head)) + shift

        def second(n, i, g):
            cols = slice(g * wide, (g + 1) * wide)
            big = slice(g * many, (g + 1) * many)
            scores = buffers[n % 2][...]
            highest = jnp.max(scores, axis=0, keepdims=True)
            raised = jnp.exp(scores - highest)
            total = jnp.sum(raised, axis=0, keepdims=True)
            kept[i, :, big] = raised.astype(BF16)
            back = 1.0 / total
            inverse[i, :, big] = jnp.broadcast_to(back, (8, many))
            parts[g] = diagonal(tn(values(i, cols), kept[i, :, big]) * back, head, rows)
            if g == groups - 1:
                results[i * rows : (i + 1) * rows, :] = jnp.concatenate(
                    [parts[j] for j in range(groups)], axis=0
                ).T.astype(BF16)

        staggered([(i, g) for i in range(own) for g in range(groups)], first, second)

    def forward(r):
        x_buf, e_buf = r.x0, r.embed
        for k in range(group):
            piece = r.rows[k]
            for i in range(own):
                x_buf[i * rows + k * slot : i * rows + (k + 1) * slot, :] = piece[i]
                e_buf[i * rows + k * slot : i * rows + (k + 1) * slot, :] = piece[own].astype(F32)
        r.put(x0=None)
        a_in = (x_buf[...].astype(F32) + e_buf[...]).astype(BF16)
        r.put(a_in=a_in)
        queries = (nn(a_in, r.wq[...]) + vector(r, BQ)).astype(BF16)
        r.put(q1=(queries.astype(F32) * scale).astype(BF16))
        r.put(k1=nn(a_in, r.wk[...]).astype(BF16))
        r.put(v1=(nn(x_buf[...], r.wv[...]) + vector(r, BV)).astype(BF16))

        row = lax.broadcasted_iota(jnp.int32, (rows, 128), 0) % slot
        r.self_bias[...] = jnp.where(row < chunk, 0.0, -1e30)
        attend(
            lambda i: r.q1[i * rows : (i + 1) * rows, :],
            lambda i, cols: r.k1[i * rows : (i + 1) * rows, cols],
            lambda i, cols: r.v1[i * rows : (i + 1) * rows, cols],
            r.e1,
            r.inv1,
            (r.self_scores, r.self_scores_two),
            lambda i: r.self_bias[...],
            r.o1,
        )
        r.put(e1=None)
        r.put(inv1=None)
        r.put(o1=None)
        summed = x_buf[...].astype(F32) + nn(r.o1[...], r.wo[...]) + vector(r, BO)
        unit, spread, normed = norm_forward(summed, vector(r, G1), vector(r, B1))
        r.put(unit1=unit)
        r.put(spread1=spread)
        r.normed[...] = normed
        r.put(c_in=(normed + e_buf[...]).astype(BF16))
        queries = (nn(r.c_in[...], r.wcq[...]) + vector(r, BCQ)).astype(BF16)
        r.put(q2=(queries.astype(F32) * scale).astype(BF16))
        for i in range(own):
            length = r.lengths[lax.axis_index("pb") * own + i]
            row = lax.broadcasted_iota(jnp.int32, (part, 128), 0)
            for q in range(group):
                seen = (row + q * quarter < length) & (row < quarter)
                r.cross_bias[i, q * part : (q + 1) * part, :] = jnp.where(seen, 0.0, -1e30)
        attend(
            lambda i: r.q2[i * rows : (i + 1) * rows, :],
            lambda i, cols: r.keys[i, :, cols],
            lambda i, cols: r.values[i, :, cols],
            r.e2,
            r.inv2,
            (r.cross_scores, r.cross_scores_two),
            lambda i: r.cross_bias[i],
            r.o2,
        )
        r.put(e2=None)
        r.put(inv2=None)
        r.put(o2=None)
        summed = r.normed[...] + nn(r.o2[...], r.wco[...]) + vector(r, BCO)
        unit, spread, normed = norm_forward(summed, vector(r, G2), vector(r, B2))
        r.put(unit2=unit)
        r.put(spread2=spread)
        r.normed[...] = normed
        r.put(x2b=normed.astype(BF16))
        r.third[...] = normed + vector(r, BP)
        for j in range(HIDDEN_CHUNKS):
            cols = slice(j * step, (j + 1) * step)
            before = nn(r.x2b[...], r.we[:, cols]) + r.be[cols].astype(F32).reshape(1, step)
            share_below = 0.5 + 0.5 * lax.erf(before * (0.5**0.5))
            density = jnp.exp(-0.5 * before * before) * ((2.0 * math.pi) ** (-0.5))
            r.slope[:, cols] = share_below + before * density
            active = (before * share_below).astype(BF16)
            r.third[...] += nn(active, r.wp[cols, :])
            r.active_t[cols, :] = active.T
        index = lax.axis_index("pb")

        def ship(source, out):
            for y in range(two):
                for c in (1, 0):
                    first = pl.multiple_of((index ^ (2 * y + c)) * share, 16)
                    r.push((out, c), source.at[pl.ds(first, share)], lambda ref: ref.at[y])

        ship(r.active_t, "act")
        unit, spread, normed = norm_forward(r.third[...], vector(r, G3), vector(r, B3))
        low = normed.astype(BF16)
        cot = r.cot
        for k in range(group):
            piece = r.rows[k]
            for i in range(own):
                here = slice(i * rows + k * slot, i * rows + (k + 1) * slot)
                (r.near[k] if k < 2 else r.far.at[k - 2])[i] = low[here, :]
                cot[here, :] = piece[own + 1 + i].astype(F32)
        r.put(near=0)
        r.put(near=1)
        r.put(far=None)
        sums = r.sums
        sums[...] = jnp.zeros(sums.shape, F32)
        sums[0:1, :] = column_sum(cot[...] * unit)
        sums[1:2, :] = column_sum(cot[...])
        third = norm_backward(cot[...], unit, spread, vector(r, G3))
        r.put(dr3=third)
        branch = third.astype(BF16)
        r.put(df=branch)
        sums[2:3, :] = column_sum(branch)
        r.put(sums=None)
        for j in range(HIDDEN_CHUNKS):
            cols = slice(j * step, (j + 1) * step)
            grad = (nt(r.df[...], r.wp[cols, :]) * r.slope[:, cols]).astype(BF16)
            r.dh[:, cols] = grad
            r.hidden_sum[:, cols] = column_sum(grad)
            r.grad_t[cols, :] = grad.T
        ship(r.grad_t, "dh_t")
        r.put(dh=None, hidden_sum=None)

    two = group // 2
    fw = run(
        forward,
        dict(
            lengths=(lengths, SM),
            rows=(row_parts, DMA),
            vectors=(vectors, VM),
            be=(expand_bias, VM),
            wq=(self_query, DMA),
            wk=(self_key, DMA),
            wv=(self_value, DMA),
            wo=(self_out, DMA),
            wcq=(cross_query, DMA),
            keys=(memory_keys, DMA),
            values=(memory_values, DMA),
            wco=(cross_out, DMA),
            we=(expand_weight, DMA),
            wp=(project_weight, DMA),
        ),
        dict(

            x0=((all_rows, width), BF16, DMA),
            a_in=((all_rows, width), BF16, DMA),
            q1=((all_rows, width), BF16, DMA),
            k1=((all_rows, width), BF16, DMA),
            v1=((all_rows, width), BF16, DMA),
            e1=((own, rows, groups * many), BF16, DMA),
            inv1=((own, 8, groups * many), F32, DMA),
            o1=((all_rows, width), BF16, DMA),
            unit1=((all_rows, width), F32, DMA),
            spread1=((all_rows, 1), F32, DMA),
            c_in=((all_rows, width), BF16, DMA),
            q2=((all_rows, width), BF16, DMA),
            e2=((own, span, groups * many), BF16, DMA),
            inv2=((own, 8, groups * many), F32, DMA),
            o2=((all_rows, width), BF16, DMA),
            unit2=((all_rows, width), F32, DMA),
            spread2=((all_rows, 1), F32, DMA),
            x2b=((all_rows, width), BF16, DMA),
            act=([(two, share, all_rows)] * 2, BF16, RAW),
            dr3=((all_rows, width), F32, DMA),
            df=((all_rows, width), BF16, DMA),
            dh=((all_rows, hidden), BF16, DMA),
            dh_t=([(two, share, all_rows)] * 2, BF16, RAW),
            sums=((8, width), F32, DMA),
            hidden_sum=((1, hidden), F32, DMA),
        near=([(own, slot, width)] * 2, BF16, DMA),
            far=((2, own, slot, width), BF16, DMA),
        ),
        dict(
            embed=((all_rows, width), F32),
            self_scores=((rows, many), F32),
            self_scores_two=((rows, many), F32),
            self_bias=((rows, 128), F32),
            cross_scores=((span, many), F32),
            cross_scores_two=((span, many), F32),
            cross_bias=((own, span, 128), F32),
            normed=((all_rows, width), F32),
            third=((all_rows, width), F32),
            cot=((all_rows, width), F32),
            slope=((all_rows, hidden), F32),
            active_t=((hidden, all_rows), BF16),
            grad_t=((hidden, all_rows), BF16),
        ),
        microseconds=18.0,
    )

    project_order = list(ba_bits)
    expand_order = [ba_bits[1], ba_bits[0]] + list(ba_bits[2:])
    half = width // 2

    def row_place(steps, relative, y):
        place_of = 0
        for axis, bit in steps:
            place_of = 2 * place_of + (y if axis == "pb" else relative // bit % 2)
        return place_of

    def pack(r, grad, region, offset):
        base, steps, size = region
        index, here = lax.axis_index("pb"), lax.axis_index("ba")
        for relative in range(ba_size):
            for y in range(two):
                first = base + row_place(steps, relative, y) * size + offset
                for c, target in ((0, r.keep), (1, r.send)):
                    source = pl.multiple_of((here ^ relative) * block, 8)
                    column = pl.multiple_of((index ^ (2 * y + c)) * lanes, 128)
                    target[first : first + block, :] = grad[pl.ds(source, block), pl.ds(column, lanes)].astype(BF16)

    later = [("pb", 2)] + [("ba", bit) for bit in ba_bits[2:]]
    copies = ba_size * two
    cross_size = 4 * block
    embed_rows = slot // 2
    self_size = 4 * block + embed_rows
    self_region = (0, [("ba", ba_bits[0]), ("ba", ba_bits[1])] + later, self_size)
    cross_region = (copies * self_size, [("ba", ba_bits[1]), ("ba", ba_bits[0])] + later, cross_size)
    vector_count = 13 * width + hidden
    extra = padded_to(vector_count // 128, 16)
    cut = part // 48 * 16
    packed = (copies * (self_size + cross_size) + extra, lanes)

    def attend_back(queries, grads, keys, values, kept, inverse, scores, logits, results, grad_keys, grad_values, finished=None):
        parts = {}
        spreads = {}

        def first(n, i, g):
            cols = slice(g * wide, (g + 1) * wide)
            back = inverse[i, 0:1, g * many : (g + 1) * many]
            upright = jnp.broadcast_to(back, (128, many)).T
            lane = lax.broadcasted_iota(jnp.int32, (1, wide), 1) // head
            piece = grads(i)[:, cols].astype(F32)
            spreads[n] = jnp.concatenate(
                [
                    (piece * upright[h * rows : (h + 1) * rows, 0:1]).astype(BF16)
                    * (lane == h).astype(F32).astype(BF16)
                    for h in range(GROUP_HEADS)
                ],
                axis=0,
            )
            scores[n % 2][...] = nt(values(i, cols), spreads[n])

        def second(n, i, g):
            cols = slice(g * wide, (g + 1) * wide)
            big = slice(g * many, (g + 1) * many)
            score, logit = scores[n % 2], logits[n % 2]
            back = inverse[i, 0:1, big]
            inner = jnp.sum(kept[i, :, big].astype(F32) * score[...], axis=0, keepdims=True)
            logit[...] = (kept[i, :, big].astype(F32) * (score[...] - inner * back)).astype(BF16)
            grad_values(i, cols, nn(kept[i, :, big], spreads[n]))
            grad_keys(i, cols, nn(logit[...], spread_heads(queries(i)[:, cols], head)))
            parts[g] = diagonal(tn(keys(i, cols), logit[...]), head, rows)
            if g == groups - 1:
                whole = jnp.concatenate([parts[j] for j in range(groups)], axis=0)
                results[i * rows : (i + 1) * rows, :] = (whole.T * scale).astype(BF16)
                if finished:
                    finished(i)

        staggered([(i, g) for i in range(own) for g in range(groups)], first, second)

    def cross_back(r):
        grad = r.dr3[...] + nt(r.dh[...], r.we[...])
        sums = r.sums
        sums[...] = jnp.zeros(sums.shape, F32)
        unit = r.unit2[...]
        sums[0:1, :] = column_sum(grad * unit)
        sums[1:2, :] = column_sum(grad)
        dr2 = norm_backward(grad, unit, r.spread2[...], vector(r, G2))
        r.put(dr2=dr2)
        branch = dr2.astype(BF16)
        sums[2:3, :] = column_sum(branch)
        r.put(ds2=branch)
        r.do2[...] = nt(branch, r.wco[...]).astype(BF16)
        def grad_keys(i, cols, value):
            r.dk[i, :, cols] = value.astype(BF16)

        def grad_values(i, cols, value):
            r.dv[i, :, cols] = value.astype(BF16)

        index = lax.axis_index("pb")
        def memory_back(i):
            r.put_part(i, dk=None, dv=None)
            for k in range(group - 1, -1, -1):
                edge = pl.ds(pl.multiple_of((index ^ k) * part, 16), part)
                value = (nt(r.dk[i, edge, :], r.wck[...]) + nt(r.dv[i, edge, :], r.wcv[...])).astype(BF16)
                if k < 2:
                    r.near[k][i] = value
                elif k == 3:
                    r.far_big[i * part : (i + 1) * part, :] = value
                elif i < own - 1:
                    r.far_small[i * part : (i + 1) * part, :] = value
                else:
                    r.far_small[i * part : i * part + cut, :] = value[:cut]
                    r.far_third[...] = value[cut:]
                if i == own - 1:
                    if k == 3:
                        r.put(far_big=None)
                    elif k == 2:
                        r.put(far_small=None, far_third=None)
                    else:
                        r.put(near=k)

        attend_back(
            lambda i: r.q2[i * rows : (i + 1) * rows, :],
            lambda i: r.do2[i * rows : (i + 1) * rows, :],
            lambda i, cols: r.keys[i, :, cols],
            lambda i, cols: r.values[i, :, cols],
            r.e2,
            r.inv2,
            (r.scores, r.scores_two),
            (r.logit, r.logit_two),
            r.dq,
            grad_keys,
            grad_values,
            memory_back,
        )
        r.put(dq=None)
        sums[3:4, :] = column_sum(r.dq[...])
        total = jnp.zeros((1, width), F32)
        for i in range(own):
            total = total + column_sum(r.dv[i])
        sums[4:5, :] = total
        r.put(sums=None)
        r.put(dc=nt(r.dq[...], r.wcq[...]))

    act_got = swap(fw.act[1], "pb", 1)
    x2b_got = swap(fw.x2b, "pb", 1)
    df_got = swap(fw.df, "pb", 1)
    dh_got = swap(fw.dh_t[1], "pb", 1)
    back = run(
        cross_back,
        dict(
            vectors=(vectors, VM),
            dh=(fw.dh, DMA),
            we=(expand_weight, DMA),
            dr3=(fw.dr3, DMA),
            unit2=(fw.unit2, DMA),
            spread2=(fw.spread2, DMA),
            wco=(cross_out, DMA),
            values=(memory_values, DMA),
            inv2=(fw.inv2, DMA),
            e2=(fw.e2, DMA),
            q2=(fw.q2, DMA),
            keys=(memory_keys, DMA),
            wck=(cross_key, DMA),
            wcv=(cross_value, DMA),
            wcq=(cross_query, DMA),
        ),
        dict(
            near=([(own, part, width)] * 2, BF16, DMA),
            far_big=((own * part, width), BF16, DMA),
            far_small=(((own - 1) * part + cut, width), BF16, DMA),
            far_third=((part - cut, width), BF16, DMA),
            dq=((all_rows, width), BF16, DMA),
            dc=((all_rows, width), F32, DMA),
            dk=((own, span, width), BF16, DMA),
            dv=((own, span, width), BF16, DMA),
            dr2=((all_rows, width), F32, DMA),
            ds2=((all_rows, width), BF16, DMA),
            sums=((8, width), F32, DMA),
        ),
        dict(do2=((all_rows, width), BF16), scores=((span, many), F32), scores_two=((span, many), F32), logit=((span, many), BF16), logit_two=((span, many), BF16)),
        microseconds=20.0,
        most=63 * 2**20 + 2**19,
    )


    def cross_weights(r):
        grad = r.grad
        grad[...] = tn(r.o2[...], r.ds2[...])
        pack(r, grad, cross_region, 3 * block)
        grad[...] = tn(r.c_in[...], r.cross_dq[...])
        pack(r, grad, cross_region, 0 * block)
        grad[...] = tn(r.plain[0], r.cross_dv[0])
        for i in range(1, own):
            grad[...] += tn(r.plain[i], r.cross_dv[i])
        pack(r, grad, cross_region, 2 * block)
        grad[...] = tn(r.keyed[0], r.cross_dk[0])
        for i in range(1, own):
            grad[...] += tn(r.keyed[i], r.cross_dk[i])
        pack(r, grad, cross_region, 1 * block)

    def rest_back(r):
        grad = r.dr2[...] + r.dc[...]
        sums = r.sums
        sums[...] = jnp.zeros(sums.shape, F32)
        unit = r.unit1[...]
        sums[0:1, :] = column_sum(grad * unit)
        sums[1:2, :] = column_sum(grad)
        first = r.first
        first[...] = norm_backward(grad, unit, r.spread1[...], vector(r, G1))
        branch = first[...].astype(BF16)
        sums[2:3, :] = column_sum(branch)
        whole = r.grad
        whole[...] = tn(r.o1[...], branch)
        pack(r, whole, self_region, 3 * block)
        r.do1[...] = nt(branch, r.wo[...]).astype(BF16)
        def grad_keys(i, cols, value):
            r.dk[i * rows : (i + 1) * rows, cols] = value.astype(BF16)

        def grad_values(i, cols, value):
            r.dv[i * rows : (i + 1) * rows, cols] = value.astype(BF16)

        attend_back(
            lambda i: r.q1[i * rows : (i + 1) * rows, :],
            lambda i: r.do1[i * rows : (i + 1) * rows, :],
            lambda i, cols: r.k1[i * rows : (i + 1) * rows, cols],
            lambda i, cols: r.v1[i * rows : (i + 1) * rows, cols],
            r.e1,
            r.inv1,
            (r.scores, r.scores_two),
            (r.logit, r.logit_two),
            r.dq,
            grad_keys,
            grad_values,
        )
        dq, dk, dv = r.dq[...], r.dk[...], r.dv[...]
        sums[3:4, :] = column_sum(dq)
        sums[4:5, :] = column_sum(dv)
        both = nt(dq, r.wq[...]) + nt(dk, r.wk[...])
        low = (first[...] + both + nt(dv, r.wv[...])).astype(BF16)
        for k in range(group):
            for i in range(own):
                (r.near[k] if k < 2 else r.far.at[k - 2])[i] = low[i * rows + k * slot : i * rows + (k + 1) * slot, :]
        for j in range(2):
            r.near[j][own:] = r.out_near[j][...]
            r.far[j, own:] = r.out_far[j]
        r.put(near=0)
        r.put(near=1)
        r.put(far=None)
        both = both + r.dc[...]
        embed = both[0:rows]
        for i in range(1, own):
            embed = embed + both[i * rows : (i + 1) * rows]
        embed = nn(embed.astype(BF16), permutation(project_order, width, ba_size)).astype(BF16)
        order_bits = project_order
        for position in range(ba_size):
            relative = sum(((position >> (len(order_bits) - 1 - b)) & 1) * bit for b, bit in enumerate(order_bits))
            for y in range(two):
                first = row_place(self_region[1], relative, y) * self_size + 4 * block
                for c, target in ((0, r.keep), (1, r.send)):
                    k = 2 * y + c
                    piece = embed[k * slot : (k + 1) * slot, position * block : (position + 1) * block]
                    gap = [jnp.zeros((embed_rows, lanes // 2 - block), BF16)] if block < lanes // 2 else []
                    filled = jnp.concatenate([piece[:embed_rows]] + gap + [piece[embed_rows:]] + gap, axis=1)
                    target[first : first + embed_rows, :] = filled
        table_rows = r.rows
        table_rows[...] = jnp.zeros(table_rows.shape, F32)
        sources = [
            (sums, 3),
            (sums, 4),
            (sums, 2),
            (sums, 0),
            (sums, 1),
            (r.sums_s, 3),
            (r.sums_s, 4),
            (r.sums_s, 2),
            (r.sums_s, 0),
            (r.sums_s, 1),
            (r.sums_f, 2),
            (r.sums_f, 0),
            (r.sums_f, 1),
        ] + [(r.hidden_sum, None)]
        filled_rows = 0
        for source, place_of in sources:
            place_of = place_of or 0
            for j in range(source.shape[1] // 128):
                table_rows[filled_rows : filled_rows + 1, :] = source[place_of : place_of + 1, j * 128 : (j + 1) * 128]
                filled_rows += 1
        low_rows = table_rows[...].astype(BF16)
        r.keep[packed[0] - extra :, :] = low_rows
        r.send[packed[0] - extra :, :] = low_rows
        for matrix, left, right in ((0, r.a_in, dq), (1, r.a_in, dk), (2, r.x0, dv)):
            whole[...] = tn(left[...], right)
            pack(r, whole, self_region, matrix * block)
        edge = copies * self_size
        tail = packed[0] - extra
        for rows_first, rows_count in ((0, edge), (tail, extra)):
            r.put_rows("send", rows_first, rows_count)
            r.put_rows("keep", rows_first, rows_count)
        cross_weights(r)
        r.put_rows("send", edge, tail - edge)
        r.put_rows("keep", edge, tail - edge)

    act_got, x2b_got, df_got, dh_got, hidden_start = meet(act_got, x2b_got, df_got, dh_got, back.ds2)

    def hidden_grads(r):
        r.perm[...] = permutation(project_order, width, ba_size)
        tile = width // 4

        def columns(rows, swapped):
            value = nn(rows, r.perm[...]).astype(BF16)
            tiles = [value[:, t * tile : (t + 1) * tile] for t in ((0, 2, 1, 3) if swapped else range(4))]
            return jnp.concatenate(tiles, axis=1)

        def one(swapped, keep, got, rows_own, rows_got, kept, sent):
            own_cols = columns(rows_own(), swapped)
            got_cols = columns(rows_got(), swapped)
            for y in range(two):
                total = nn(keep()[y], own_cols) + nn(got()[y], got_cols)
                kept[y] = total[:, :half].astype(BF16)
                sent[y] = total[:, half:].astype(BF16)

        one(
            False,
            lambda: r.act_keep,
            lambda: r.act_got,
            lambda: r.df[...],
            lambda: r.df_got[...],
            r.p_keep,
            r.p_send,
        )
        r.put(p_send=None, p_keep=None)
        one(
            True,
            lambda: r.dh_keep,
            lambda: r.dh_got,
            lambda: r.x2b[...],
            lambda: r.x2b_got[...],
            r.e_keep,
            r.e_send,
        )
        r.put(e_send=None, e_keep=None)

    piece = ((two, share, half), BF16, DMA)
    hid = run(
        hidden_grads,
        dict(
            df=(tie(fw.df, hidden_start), DMA),
            df_got=(df_got, DMA),
            act_keep=(fw.act[0], DMA),
            act_got=(act_got, DMA),
            x2b=(fw.x2b, DMA),
            x2b_got=(x2b_got, DMA),
            dh_keep=(fw.dh_t[0], DMA),
            dh_got=(dh_got, DMA),
        ),
        dict(p_keep=piece, p_send=piece, e_keep=piece, e_send=piece),
        dict(perm=((width, width), BF16)),
        microseconds=4.0,
    )

    p_send, e_send, far_big, mem_near = meet(hid.p_send, hid.e_send, back.far_big, back.near[1])

    p_got = swap(p_send, "ba", ba_bits[0])
    e_got = swap(e_send, "ba", ba_bits[1])
    big_got = swap(far_big, "pb", 2)
    mem_other = swap(mem_near, "pb", 1)
    slf = run(
        rest_back,
        dict(
            vectors=(vectors, VM),
            dr2=(tie(back.dr2, p_send, e_send), DMA),
            dc=(back.dc, DMA),
            unit1=(fw.unit1, DMA),
            spread1=(fw.spread1, DMA),
            o1=(fw.o1, DMA),
            wo=(self_out, DMA),
            inv1=(fw.inv1, DMA),
            e1=(fw.e1, DMA),
            q1=(fw.q1, DMA),
            k1=(fw.k1, DMA),
            v1=(fw.v1, DMA),
            wq=(self_query, DMA),
            wk=(self_key, DMA),
            wv=(self_value, DMA),
            a_in=(fw.a_in, DMA),
            x0=(fw.x0, DMA),
            out_near=(fw.near, DMA),
            out_far=(fw.far, DMA),
            o2=(fw.o2, DMA),
            ds2=(back.ds2, DMA),
            c_in=(fw.c_in, DMA),
            cross_dq=(back.dq, DMA),
            cross_dv=(back.dv, DMA),
            plain=(plain, DMA),
            cross_dk=(back.dk, DMA),
            keyed=(keyed, DMA),
            sums_s=(back.sums, DMA),
            sums_f=(fw.sums, DMA),
            hidden_sum=(fw.hidden_sum, DMA),
        ),
        dict(
            keep=(packed, BF16, DMA),
            send=(packed, BF16, DMA),
            near=([(2 * own, slot, width)] * 2, BF16, DMA),
            far=((2, 2 * own, slot, width), BF16, DMA),
        ),
        dict(
            sums=((8, width), F32),
            rows=((extra, 128), F32),
            first=((all_rows, width), F32),
            grad=((width, width), F32),
            do1=((all_rows, width), BF16),
            dq=((all_rows, width), BF16),
            dk=((all_rows, width), BF16),
            dv=((all_rows, width), BF16),
            scores=((rows, many), F32),
            scores_two=((rows, many), F32),
            logit=((rows, many), BF16),
            logit_two=((rows, many), BF16),
        ),
        microseconds=7.0,
    )
    p_got, e_got, big_got, mem_other, send, far_small = meet(
        p_got, e_got, big_got, mem_other, slf.send, back.far_small
    )

    p_keep, p_send = halves(pair_sum(hid.p_keep, p_got), -1)
    e_keep, e_send = halves(pair_sum(hid.e_keep, e_got), -1)
    p_got = swap(p_send, "ba", ba_bits[1])
    e_got = swap(e_send, "ba", ba_bits[0])
    got = swap(send, "pb", 1)
    small_got = swap(far_small, "pb", 2)
    last = swap(big_got, "pb", 1)
    p_got, e_got, got, last, small_got, far_third = meet(p_got, e_got, got, last, small_got, back.far_third)

    edge = copies * self_size
    a_keep, a_send = sum_halves(slf.keep, got, 0, edge, extra)
    b_keep, b_send = sum_halves(slf.keep, got, edge, packed[0] - extra, 0)
    p_total, e_total = pair_sum(p_keep, p_got), pair_sum(e_keep, e_got)
    f_keep, f_send = (jnp.stack([p_total[y], e_total[y]]).astype(BF16) for y in range(two))
    a_got = swap(a_send, "ba", ba_bits[0])
    b_got = swap(b_send, "ba", ba_bits[1])
    f_got = swap(f_send, "pb", 2)
    third_got = swap(far_third, "pb", 2)
    a_got, b_got, f_got, third_got, home_near, home_far = meet(
        a_got, b_got, f_got, third_got, slf.near[1], slf.far
    )

    f_total = pair_sum(f_keep, f_got)
    f_half = f_total.shape[-1] // 2
    f_keep, f_send = (
        jnp.concatenate(
            [f_total[0, :, j * f_half : (j + 1) * f_half], f_total[1, :, j * f_half : (j + 1) * f_half]], axis=-1
        ).astype(BF16)
        for j in range(2)
    )
    a_keep, a_send = sum_halves(a_keep, a_got, 0, a_keep.shape[0] - extra, extra)
    b_keep, b_send = sum_halves(b_keep, b_got, 0, b_keep.shape[0], 0)
    a_got = swap(a_send, "ba", ba_bits[1])
    b_got = swap(b_send, "ba", ba_bits[0])
    home_other = swap(home_near, "pb", 1)
    home_across = swap(home_far, "pb", 2)

    def place_memory(r):
        index = lax.axis_index("pb")
        for i in range(own):
            last = r.last[i * part : i * part + quarter, :]
            if i < own - 1:
                across = r.across[i * part : i * part + quarter, :]
            else:
                across = jnp.concatenate(
                    [r.across[i * part : i * part + cut, :], r.third[0 : quarter - cut, :]], axis=0
                )
            for k, piece in enumerate((r.mine[i, 0:quarter, :], r.other[i, 0:quarter, :], across, last)):
                r.wide[:, (index ^ k) * own + i, :] = piece.astype(F32)
        r.put(whole=r.wide[...].astype(BF16))

    memory_grad = run(
        place_memory,
        dict(
            mine=(tie(back.near[0], f_send, a_send, b_send), DMA),
            other=(mem_other, DMA),
            across=(small_got, DMA),
            third=(third_got, DMA),
            last=(last, DMA),
        ),
        dict(whole=((quarter, items, width), BF16, DMA)),
        dict(wide=((quarter, items, width), F32)),
        microseconds=4.0,
        spare=4,
    ).whole
    f_send, a_got, b_got, home_other, home_across, memory_grad = meet(
        f_send, a_got, b_got, home_other, home_across, memory_grad
    )

    keep, send = row_halves(
        interleave(pair_sum(a_keep, a_got), pair_sum(b_keep, b_got), self_size, cross_size, extra), extra
    )
    got = swap(send, "pb", 2)
    f_got = swap(f_send, "ba", ba_bits[2])
    home_last = swap(home_across[1], "pb", 1)
    got, f_got, home_last = meet(got, f_got, home_last)

    keep, send = row_halves(pair_sum(keep, got), extra)
    got = swap(send, "ba", ba_bits[2])
    hidden_out = pair_sum(f_keep, f_got)
    project_out, expand_out = (
        finish(part_out, ba_bits[3:], lambda total: halves(total, -1))
        for part_out in (hidden_out[:, :f_half], hidden_out[:, f_half:])
    )
    expand_out = expand_out.T

    def place_rows(r):
        index = lax.axis_index("pb")
        for i in range(own):
            for k in range(group):
                source = (r.mine, r.other, r.across.at[0], r.last)[k]
                r.wide[:, (index ^ k) * own + i, :] = source[i, 0:chunk, :].astype(F32)
                r.wide_out[:, (index ^ k) * own + i, :] = source[own + i, 0:chunk, :].astype(F32)
        r.put(grad=r.wide[...].astype(BF16))
        r.put(out=r.wide_out[...].astype(BF16))

    wide_rows = (chunk, items, width)
    rows_home = run(
        place_rows,
        dict(
            mine=(tie(slf.near[0], send), DMA),
            other=(home_other, DMA),
            across=(home_across, DMA),
            last=(home_last, DMA),
        ),
        dict(grad=(wide_rows, BF16, DMA), out=(wide_rows, BF16, DMA)),
        dict(wide=(wide_rows, F32), wide_out=(wide_rows, F32)),
        microseconds=2.0,
        spare=4,
    )
    input_grad, layer_output = rows_home.grad, rows_home.out
    addends = [keep, got]
    if len(ba_bits) > 3:
        addends = [finish(pair_sum(keep, got), ba_bits[3:], lambda total: row_halves(total, extra))]
    places = [m * block for m in range(4)] + [self_size + m * block for m in range(4)]
    vector_rows = [width // 128] * 13 + [hidden // 128]

    def spread_out(r):
        total = r.addends[0][...].astype(F32)
        for j in range(1, len(addends)):
            total = total + r.addends[j][...].astype(F32)
        r.total[...] = total
        for m, first in enumerate(places):
            r.squares[m][...] = r.total[first : first + block, :]
        for j in range(2):
            count = min(embed_rows, chunk - j * embed_rows)
            left = j * lanes // 2
            r.embed[j * embed_rows : j * embed_rows + count, :] = r.total[
                4 * block : 4 * block + count, left : left + block
            ]
        first = addends[0].shape[0] - extra
        for j, count in enumerate(vector_rows):
            r.vectors[j][...] = r.total[first : first + count, :]
            first += count

    ends = run(
        spread_out,
        dict(addends=(addends, VM)),
        dict(
            squares=([(block, lanes)] * 8, F32, VM),
            embed=((chunk, block), F32, VM),
            vectors=([(count, 128) for count in vector_rows], F32, VM),
        ),
        dict(total=(addends[0].shape, F32)),
        microseconds=1.0,
        spare=4,
    )
    input_grad, layer_output = input_grad.transpose(1, 0, 2), layer_output.transpose(1, 0, 2)
    memory_grad = memory_grad.transpose(1, 0, 2)
    squares, vecs = ends.squares, [vector_out.reshape(-1) for vector_out in ends.vectors]

    return (
        layer_output,
        input_grad,
        memory_grad,
        ends.embed,
        squares[0],
        vecs[0],
        squares[1],
        squares[2],
        vecs[1],
        squares[3],
        vecs[2],
        vecs[3],
        vecs[4],
        squares[4],
        vecs[5],
        squares[5],
        squares[6],
        vecs[6],
        squares[7],
        vecs[7],
        vecs[8],
        vecs[9],
        expand_out,
        vecs[13],
        project_out,
        vecs[10],
        vecs[11],
        vecs[12],
    )


def solution(mesh):
    rows = P("ba", "pb", None)
    copied = P()
    placed = (rows, P("ba", None, None), P("ba"), P("pb", None)) + (copied,) * 24 + (rows,)
    square = P("ba", "pb")
    return jax.shard_map(
        local,
        mesh=mesh,
        in_specs=placed,
        out_specs=(
            rows,
            rows,
            rows,
            P("pb", "ba"),
            square,
            copied,
            square,
            square,
            copied,
            square,
            copied,
            copied,
            copied,
            square,
            copied,
            square,
            square,
            copied,
            square,
            copied,
            copied,
            copied,
            square,
            copied,
            P("pb", "ba"),
            copied,
            copied,
            copied,
        ),
        check_vma=False,
    )
```

```python
import math

import jax
import jax.numpy as jnp
import numpy as np
from jax import lax
from jax.experimental import pallas as pl
from jax.experimental.pallas import tpu as pltpu
from jax.sharding import PartitionSpec as P

HEADS = 8
GROUP_HEADS = 4
F32 = jnp.float32
BF16 = jnp.bfloat16
HIDDEN_CHUNKS = 5
VMEM_BYTES = 58 * 2**20


def sinusoid(count, model_width):
    position = np.arange(count, dtype=np.float32)
    column = np.arange(model_width // 2, dtype=np.float32)
    frequency = np.exp(column * np.float32(-2.0 * math.log(10000.0) / model_width)).astype(np.float32)
    angles = (position[:, None] * frequency[None, :]).astype(np.float32)
    table = np.stack([np.sin(angles), np.cos(angles)], axis=-1)
    return table.reshape(count, model_width).astype(np.float32)


def padded_to(extent, multiple):
    return -(-extent // multiple) * multiple


def nn(left, right):
    return lax.dot_general(left, right, (((1,), (0,)), ((), ())), preferred_element_type=F32)


def nt(left, right):
    return lax.dot_general(left, right, (((1,), (1,)), ((), ())), preferred_element_type=F32)


def tn(left, right):
    return lax.dot_general(left, right, (((0,), (0,)), ((), ())), preferred_element_type=F32)


VM, SM, DMA, OWN, RAW = range(5)


class Named:
    def __init__(self, find):
        self.find = find

    def __getattr__(self, key):
        return self.find(key)


class Numbered:
    def __init__(self, find, key):
        self.find, self.key = find, key

    def __getitem__(self, place):
        return self.find((self.key, place))


def flat(entries):
    result = {}
    for key, (value, *rest) in entries.items():
        if isinstance(value, list):
            for place, member in enumerate(value):
                result[(key, place)] = (member, *rest)
        else:
            result[key] = (value, *rest)
    return result


def run(body, ins, outs, scratch=None, after=(), microseconds=5.0, spare=64, most=VMEM_BYTES):
    listed = {key for entries in (ins, outs) for key, entry in entries.items() if isinstance(entry[0], list)}
    ins, outs, scratch = flat(ins), flat(outs), scratch or {}
    in_dma = [key for key, entry in ins.items() if entry[1] in (DMA, OWN)]
    out_dma = [key for key, entry in outs.items() if entry[2] == DMA]

    def kernel(*refs):
        refs = list(refs)
        held = {key: refs.pop(0) for key in ins}
        del refs[: len(after)]
        results = {key: refs.pop(0) for key in outs}
        arrived = {key: refs.pop(0) for key in in_dma}
        leaving = {key: refs.pop(0) for key in out_dma}
        held.update(results)
        sources = {key: held[key] for key in in_dma}
        held.update(arrived)
        held.update(leaving)
        held.update({key: refs.pop(0) for key in scratch})
        in_sem, out_sem, part_sem, row_sem = refs
        pending = {}
        for place, key in enumerate(in_dma):
            source = sources[key]
            if ins[key][1] == OWN:
                count = arrived[key].shape[0]
                source = source.at[pl.ds(lax.axis_index("pb") * count, count)]
            pending[key] = pltpu.make_async_copy(source, arrived[key], in_sem.at[place])
            pending[key].start()
        started = {}

        def find(key):
            if key in listed:
                return Numbered(find, key)
            if key in pending:
                pending.pop(key).wait()
            return held[key]

        def put(**values):
            for key, value in values.items():
                if key in listed:
                    key = (key, value)
                elif value is not None:
                    held[key][...] = value
                if key in leaving:
                    place = out_dma.index(key)
                    started[key] = pltpu.make_async_copy(leaving[key], results[key], out_sem.at[place])
                    started[key].start()

        def put_part(part, **values):
            for key in values:
                place = out_dma.index(key)
                copy = pltpu.make_async_copy(leaving[key].at[part], results[key].at[part], part_sem.at[place, part])
                copy.start()
                started[(key, part)] = copy
                started[key] = copy

        bag = Named(find)
        bag.put = put
        bag.put_part = put_part

        def push(key, source, target):
            copy = pltpu.make_async_copy(source, target(results[key]), row_sem.at[len(pushed)])
            copy.start()
            pushed.append(copy)
            started[key] = copy

        def put_rows(key, first, count):
            push(key, leaving[key].at[pl.ds(first, count)], lambda ref: ref.at[pl.ds(first, count)])

        pushed = []
        bag.push, bag.put_rows = push, put_rows
        body(bag)
        for key in list(pending):
            pending.pop(key).wait()
        for key in out_dma:
            assert key in started, key
        for copy in {id(copy): copy for copy in [*started.values(), *pushed]}.values():
            copy.wait()

    spaces = [pltpu.VMEM, pltpu.SMEM, pl.ANY, pl.ANY, pl.ANY]
    arrays = [entry[0] for entry in ins.values()]
    nbytes = sum(int(np.prod(array.shape)) * array.dtype.itemsize for array in arrays)
    held_bytes = sum(
        int(np.prod(shape)) * (4 if dtype == F32 else 2)
        for shape, dtype in [(entry[0].shape, entry[0].dtype) for entry in ins.values()]
        + [(entry[0], entry[1]) for entry in outs.values()]
        + list(scratch.values())
    )
    made = pl.pallas_call(
        kernel,
        out_shape=[jax.ShapeDtypeStruct(entry[0], entry[1]) for entry in outs.values()],
        in_specs=[pl.BlockSpec(memory_space=spaces[entry[1]]) for entry in ins.values()]
        + [pl.BlockSpec(memory_space=pl.ANY)] * len(after),
        out_specs=[pl.BlockSpec(memory_space=spaces[entry[2]]) for entry in outs.values()],
        scratch_shapes=[
            pltpu.VMEM(
                (ins[key][0].shape[0] // lax.axis_size("pb"), *ins[key][0].shape[1:])
                if ins[key][1] == OWN
                else ins[key][0].shape,
                ins[key][0].dtype,
            )
            for key in in_dma
        ]
        + [pltpu.VMEM(outs[key][0], outs[key][1]) for key in out_dma]
        + [pltpu.VMEM(shape, dtype) for shape, dtype in scratch.values()]
        + [pltpu.SemaphoreType.DMA((max(1, len(in_dma)),)), pltpu.SemaphoreType.DMA((max(1, len(out_dma)),)), pltpu.SemaphoreType.DMA((max(1, len(out_dma)), 2)), pltpu.SemaphoreType.DMA((8,))],
        compiler_params=pltpu.CompilerParams(vmem_limit_bytes=min(most, held_bytes + spare * 2**20)),
        cost_estimate=pl.CostEstimate(
            flops=int(microseconds * 1e3), bytes_accessed=1024, transcendentals=0
        ),
        name=body.__name__,
    )(*arrays, *after)
    by_key = dict(zip(outs, made))

    def result(key):
        if key in listed:
            return [value for name, value in by_key.items() if isinstance(name, tuple) and name[0] == key]
        return by_key[key]

    return Named(result)


def norm_forward(values, gain, shift):
    average = jnp.mean(values, axis=-1, keepdims=True)
    centred = values - average
    spread = jnp.mean(centred * centred, axis=-1, keepdims=True)
    scale = lax.rsqrt(spread + 1e-05)
    unit = centred * scale
    return unit, scale, unit * gain + shift


def norm_backward(grad, unit, scale, gain):
    lifted = grad * gain
    first = jnp.mean(lifted, axis=-1, keepdims=True)
    second = jnp.mean(lifted * unit, axis=-1, keepdims=True)
    return scale * (lifted - first - unit * second)


def column_sum(values):
    return jnp.sum(values.astype(F32), axis=0, keepdims=True)


def spread_heads(rows, width):
    count, columns = rows.shape
    lane = lax.broadcasted_iota(jnp.int32, (1, columns), 1) // width
    return jnp.concatenate(
        [rows * (lane == h).astype(F32).astype(BF16) for h in range(columns // width)], axis=0
    )


def diagonal(blocks, width, count):
    heads = blocks.shape[0] // width
    return jnp.concatenate(
        [blocks[h * width : (h + 1) * width, h * count : (h + 1) * count] for h in range(heads)], axis=0
    )


def swap(values, axis, bit):
    size = lax.axis_size(axis)
    return lax.ppermute(values, axis, [(i, i ^ bit) for i in range(size)])


def bits_of(size):
    return [1 << b for b in range(size.bit_length() - 1)]


def exchange(values, axis):
    size = lax.axis_size(axis)
    return [values[0]] + [swap(values[k], axis, k) for k in range(1, size)]


def pair_sum(kept, got):
    return kept.astype(F32) + got.astype(F32)


def meet(*arrays):
    return lax.optimization_barrier(arrays)


def tie(values, *before):
    return lax.optimization_barrier((values, *before))[0]


def halves(values, dim):
    dim = dim % values.ndim
    if values.shape[dim] == 2:
        parts = [lax.index_in_dim(values, j, dim, keepdims=False) for j in range(2)]
    else:
        half = values.shape[dim] // 2
        parts = [lax.slice_in_dim(values, j * half, (j + 1) * half, axis=dim) for j in range(2)]
    return parts[0].astype(BF16), parts[1].astype(BF16)


def row_halves(total, extra):
    body = total.shape[0] - extra
    parts = [total[: body // 2], total[body // 2 : body]]
    if extra:
        parts = [jnp.concatenate([part, total[body:]]) for part in parts]
    return parts[0].astype(BF16), parts[1].astype(BF16)


def sum_halves(kept, got, low, high, extra):
    def piece(first, last):
        return pair_sum(kept[first:last], got[first:last]).astype(BF16)

    middle = (low + high) // 2
    tail = [piece(kept.shape[0] - extra, kept.shape[0])] if extra else []
    return tuple(
        jnp.concatenate([piece(*edge)] + tail) if tail else piece(*edge) for edge in ((low, middle), (middle, high))
    )


def finish(total, bits, split):
    for bit in bits:
        kept, sent = split(total)
        total = pair_sum(kept, swap(sent, "ba", bit))
    return total


def interleave(first, second, first_size, second_size, extra):
    count = second.shape[0] // second_size
    body = jnp.concatenate(
        [
            first[: count * first_size].reshape(count, first_size, -1),
            second.reshape(count, second_size, -1),
        ],
        axis=1,
    )
    return jnp.concatenate([body.reshape(count * (first_size + second_size), -1), first[count * first_size :]])


def permutation(order, model_width, ba_size):
    mine = lax.axis_index("ba")
    width = model_width // ba_size
    column = lax.broadcasted_iota(jnp.int32, (1, model_width), 1)
    position = column // width
    relative = jnp.zeros_like(column)
    for step, bit in enumerate(order):
        digit = (position >> (len(order) - 1 - step)) & 1
        relative = relative + digit * bit
    source = (relative ^ mine) * width + column % width
    row = lax.broadcasted_iota(jnp.int32, (model_width, model_width), 0)
    return (row == source).astype(BF16)


def local(
    decoder_input,
    memory,
    lengths,
    query_embed,
    self_query,
    self_query_bias,
    self_key,
    self_value,
    self_value_bias,
    self_out,
    self_out_bias,
    norm_one_gain,
    norm_one_bias,
    cross_query,
    cross_query_bias,
    cross_key,
    cross_value,
    cross_value_bias,
    cross_out,
    cross_out_bias,
    norm_two_gain,
    norm_two_bias,
    expand_weight,
    expand_bias,
    project_weight,
    project_bias,
    norm_three_gain,
    norm_three_bias,
    out_cotangent,
):
    items, chunk, width = decoder_input.shape
    tokens = memory.shape[1]
    hidden = expand_weight.shape[1]
    group = lax.axis_size("pb")
    ba_size = lax.axis_size("ba")
    place = lax.axis_index("pb")
    mine = lax.axis_index("ba")
    own = items // group
    quarter = tokens // group
    slot = padded_to(chunk, 32)
    rows = group * slot
    all_rows = own * rows
    part = padded_to(quarter, 16)
    span = group * part
    head = width // HEADS
    scale = head ** (-0.5)
    share = hidden // group
    step = hidden // HIDDEN_CHUNKS
    wide = GROUP_HEADS * head
    many = GROUP_HEADS * rows
    groups = HEADS // GROUP_HEADS
    ba_bits = bits_of(ba_size)
    block = width // ba_size
    lanes = width // group


    def prepare(r):
        index = lax.axis_index("pb")
        r.wide_x[...] = r.x[...].astype(F32)
        r.wide_g[...] = r.g[...].astype(F32)
        for k in range(group):
            source = (index ^ k) * own
            piece = r.rows[k]
            piece[...] = jnp.zeros(piece.shape, BF16)
            for i in range(own):
                piece[i, 0:chunk, :] = r.wide_x[:, source + i, :].astype(BF16)
                piece[own + 1 + i, 0:chunk, :] = r.wide_g[:, source + i, :].astype(BF16)
            piece[own, 0:chunk, :] = r.e[...]

    prepared = run(
        prepare,
        dict(
            x=(decoder_input.transpose(1, 0, 2), VM),
            e=(query_embed, VM),
            g=(out_cotangent.transpose(1, 0, 2), VM),
        ),
        dict(rows=([(2 * own + 1, slot, width)] * group, BF16, VM)),
        dict(wide_x=((chunk, items, width), F32), wide_g=((chunk, items, width), F32)),
        microseconds=1.0,
    )
    row_parts = exchange(prepared.rows, "pb")

    table = np.zeros((group, part, width), np.float32)
    table[:, :quarter] = sinusoid(tokens, width).reshape(group, quarter, width)
    table = jnp.asarray(table.reshape(span, width))

    def project_memory(r):
        for i in range(own):
            source = r.memory[i]
            for q in range(group):
                r.plain[i, q * part : q * part + quarter, :] = source[q * quarter : (q + 1) * quarter, :]
                if part > quarter:
                    r.plain[i, q * part + quarter : (q + 1) * part, :] = jnp.zeros((part - quarter, width), BF16)
            r.keyed[i] = (r.plain[i].astype(F32) + r.table[...]).astype(BF16)
            r.keys[i] = nn(r.keyed[i], r.wk[...]).astype(BF16)
            r.put_part(i, keys=None, keyed=None)
            r.values[i] = (nn(r.plain[i], r.wv[...]) + r.bv[...].astype(F32).reshape(1, width)).astype(BF16)
            r.put_part(i, values=None, plain=None)

    memory_block = ((own, span, width), BF16, DMA)
    prj = run(
        project_memory,
        dict(
            memory=(memory, OWN),
            table=(table, DMA),
            wk=(cross_key, DMA),
            wv=(cross_value, DMA),
            bv=(cross_value_bias, VM),
        ),
        dict(keys=memory_block, values=memory_block, keyed=memory_block, plain=memory_block),
        after=prepared.rows[:1],
        microseconds=7.0,
    )
    memory_keys, memory_values, keyed, plain = prj.keys, prj.values, prj.keyed, prj.plain

    vectors = [
        self_query_bias,
        self_value_bias,
        self_out_bias,
        norm_one_gain,
        norm_one_bias,
        cross_query_bias,
        cross_out_bias,
        norm_two_gain,
        norm_two_bias,
        project_bias,
        norm_three_gain,
        norm_three_bias,
    ]
    BQ, BV, BO, G1, B1, BCQ, BCO, G2, B2, BP, G3, B3 = range(12)

    def vector(r, place):
        return r.vectors[place][...].astype(F32).reshape(1, width)

    def staggered(tasks, first, second):
        for n in range(len(tasks) + 1):
            if n < len(tasks):
                first(n, *tasks[n])
            if n > 0:
                second(n - 1, *tasks[n - 1])

    def attend(queries, keys, values, kept, inverse, buffers, bias, results):
        parts = {}

        def first(n, i, g):
            cols = slice(g * wide, (g + 1) * wide)
            shift = jnp.concatenate([bias(i)] * (many // 128), axis=1)
            buffers[n % 2][...] = nt(keys(i, cols), spread_heads(queries(i)[:, cols], head)) + shift

        def second(n, i, g):
            cols = slice(g * wide, (g + 1) * wide)
            big = slice(g * many, (g + 1) * many)
            scores = buffers[n % 2][...]
            highest = jnp.max(scores, axis=0, keepdims=True)
            raised = jnp.exp(scores - highest)
            total = jnp.sum(raised, axis=0, keepdims=True)
            kept[i, :, big] = raised.astype(BF16)
            back = 1.0 / total
            inverse[i, :, big] = jnp.broadcast_to(back, (8, many))
            parts[g] = diagonal(tn(values(i, cols), kept[i, :, big]) * back, head, rows)
            if g == groups - 1:
                results[i * rows : (i + 1) * rows, :] = jnp.concatenate(
                    [parts[j] for j in range(groups)], axis=0
                ).T.astype(BF16)

        staggered([(i, g) for i in range(own) for g in range(groups)], first, second)

    def forward(r):
        x_buf, e_buf = r.x0, r.embed
        for k in range(group):
            piece = r.rows[k]
            for i in range(own):
                x_buf[i * rows + k * slot : i * rows + (k + 1) * slot, :] = piece[i]
                e_buf[i * rows + k * slot : i * rows + (k + 1) * slot, :] = piece[own].astype(F32)
        r.put(x0=None)
        a_in = (x_buf[...].astype(F32) + e_buf[...]).astype(BF16)
        r.put(a_in=a_in)
        queries = (nn(a_in, r.wq[...]) + vector(r, BQ)).astype(BF16)
        r.put(q1=(queries.astype(F32) * scale).astype(BF16))
        r.put(k1=nn(a_in, r.wk[...]).astype(BF16))
        r.put(v1=(nn(x_buf[...], r.wv[...]) + vector(r, BV)).astype(BF16))

        row = lax.broadcasted_iota(jnp.int32, (rows, 128), 0) % slot
        r.self_bias[...] = jnp.where(row < chunk, 0.0, -1e30)
        attend(
            lambda i: r.q1[i * rows : (i + 1) * rows, :],
            lambda i, cols: r.k1[i * rows : (i + 1) * rows, cols],
            lambda i, cols: r.v1[i * rows : (i + 1) * rows, cols],
            r.e1,
            r.inv1,
            (r.self_scores, r.self_scores_two),
            lambda i: r.self_bias[...],
            r.o1,
        )
        r.put(e1=None)
        r.put(inv1=None)
        r.put(o1=None)
        summed = x_buf[...].astype(F32) + nn(r.o1[...], r.wo[...]) + vector(r, BO)
        unit, spread, normed = norm_forward(summed, vector(r, G1), vector(r, B1))
        r.put(unit1=unit)
        r.put(spread1=spread)
        r.normed[...] = normed
        r.put(c_in=(normed + e_buf[...]).astype(BF16))
        queries = (nn(r.c_in[...], r.wcq[...]) + vector(r, BCQ)).astype(BF16)
        r.put(q2=(queries.astype(F32) * scale).astype(BF16))
        for i in range(own):
            length = r.lengths[lax.axis_index("pb") * own + i]
            row = lax.broadcasted_iota(jnp.int32, (part, 128), 0)
            for q in range(group):
                seen = (row + q * quarter < length) & (row < quarter)
                r.cross_bias[i, q * part : (q + 1) * part, :] = jnp.where(seen, 0.0, -1e30)
        attend(
            lambda i: r.q2[i * rows : (i + 1) * rows, :],
            lambda i, cols: r.keys[i, :, cols],
            lambda i, cols: r.values[i, :, cols],
            r.e2,
            r.inv2,
            (r.cross_scores, r.cross_scores_two),
            lambda i: r.cross_bias[i],
            r.o2,
        )
        r.put(e2=None)
        r.put(inv2=None)
        r.put(o2=None)
        summed = r.normed[...] + nn(r.o2[...], r.wco[...]) + vector(r, BCO)
        unit, spread, normed = norm_forward(summed, vector(r, G2), vector(r, B2))
        r.put(unit2=unit)
        r.put(spread2=spread)
        r.normed[...] = normed
        r.put(x2b=normed.astype(BF16))
        r.third[...] = normed + vector(r, BP)
        for j in range(HIDDEN_CHUNKS):
            cols = slice(j * step, (j + 1) * step)
            before = nn(r.x2b[...], r.we[:, cols]) + r.be[cols].astype(F32).reshape(1, step)
            share_below = 0.5 + 0.5 * lax.erf(before * (0.5**0.5))
            density = jnp.exp(-0.5 * before * before) * ((2.0 * math.pi) ** (-0.5))
            r.slope[:, cols] = share_below + before * density
            active = (before * share_below).astype(BF16)
            r.third[...] += nn(active, r.wp[cols, :])
            r.active_t[cols, :] = active.T
        index = lax.axis_index("pb")

        def ship(source, out):
            for y in range(two):
                for c in (1, 0):
                    first = pl.multiple_of((index ^ (2 * y + c)) * share, 16)
                    r.push((out, c), source.at[pl.ds(first, share)], lambda ref: ref.at[y])

        ship(r.active_t, "act")
        unit, spread, normed = norm_forward(r.third[...], vector(r, G3), vector(r, B3))
        low = normed.astype(BF16)
        cot = r.cot
        for k in range(group):
            piece = r.rows[k]
            for i in range(own):
                here = slice(i * rows + k * slot, i * rows + (k + 1) * slot)
                (r.near[k] if k < 2 else r.far.at[k - 2])[i] = low[here, :]
                cot[here, :] = piece[own + 1 + i].astype(F32)
        r.put(near=0)
        r.put(near=1)
        r.put(far=None)
        sums = r.sums
        sums[...] = jnp.zeros(sums.shape, F32)
        sums[0:1, :] = column_sum(cot[...] * unit)
        sums[1:2, :] = column_sum(cot[...])
        third = norm_backward(cot[...], unit, spread, vector(r, G3))
        r.put(dr3=third)
        branch = third.astype(BF16)
        r.put(df=branch)
        sums[2:3, :] = column_sum(branch)
        r.put(sums=None)
        for j in range(HIDDEN_CHUNKS):
            cols = slice(j * step, (j + 1) * step)
            grad = (nt(r.df[...], r.wp[cols, :]) * r.slope[:, cols]).astype(BF16)
            r.dh[:, cols] = grad
            r.hidden_sum[:, cols] = column_sum(grad)
            r.grad_t[cols, :] = grad.T
        ship(r.grad_t, "dh_t")
        r.put(dh=None, hidden_sum=None)

    two = group // 2
    fw = run(
        forward,
        dict(
            lengths=(lengths, SM),
            rows=(row_parts, DMA),
            vectors=(vectors, VM),
            be=(expand_bias, VM),
            wq=(self_query, DMA),
            wk=(self_key, DMA),
            wv=(self_value, DMA),
            wo=(self_out, DMA),
            wcq=(cross_query, DMA),
            keys=(memory_keys, DMA),
            values=(memory_values, DMA),
            wco=(cross_out, DMA),
            we=(expand_weight, DMA),
            wp=(project_weight, DMA),
        ),
        dict(

            x0=((all_rows, width), BF16, DMA),
            a_in=((all_rows, width), BF16, DMA),
            q1=((all_rows, width), BF16, DMA),
            k1=((all_rows, width), BF16, DMA),
            v1=((all_rows, width), BF16, DMA),
            e1=((own, rows, groups * many), BF16, DMA),
            inv1=((own, 8, groups * many), F32, DMA),
            o1=((all_rows, width), BF16, DMA),
            unit1=((all_rows, width), F32, DMA),
            spread1=((all_rows, 1), F32, DMA),
            c_in=((all_rows, width), BF16, DMA),
            q2=((all_rows, width), BF16, DMA),
            e2=((own, span, groups * many), BF16, DMA),
            inv2=((own, 8, groups * many), F32, DMA),
            o2=((all_rows, width), BF16, DMA),
            unit2=((all_rows, width), F32, DMA),
            spread2=((all_rows, 1), F32, DMA),
            x2b=((all_rows, width), BF16, DMA),
            act=([(two, share, all_rows)] * 2, BF16, RAW),
            dr3=((all_rows, width), F32, DMA),
            df=((all_rows, width), BF16, DMA),
            dh=((all_rows, hidden), BF16, DMA),
            dh_t=([(two, share, all_rows)] * 2, BF16, RAW),
            sums=((8, width), F32, DMA),
            hidden_sum=((1, hidden), F32, DMA),
        near=([(own, slot, width)] * 2, BF16, DMA),
            far=((2, own, slot, width), BF16, DMA),
        ),
        dict(
            embed=((all_rows, width), F32),
            self_scores=((rows, many), F32),
            self_scores_two=((rows, many), F32),
            self_bias=((rows, 128), F32),
            cross_scores=((span, many), F32),
            cross_scores_two=((span, many), F32),
            cross_bias=((own, span, 128), F32),
            normed=((all_rows, width), F32),
            third=((all_rows, width), F32),
            cot=((all_rows, width), F32),
            slope=((all_rows, hidden), F32),
            active_t=((hidden, all_rows), BF16),
            grad_t=((hidden, all_rows), BF16),
        ),
        microseconds=18.0,
    )

    project_order = list(ba_bits)
    expand_order = [ba_bits[1], ba_bits[0]] + list(ba_bits[2:])
    half = width // 2

    def row_place(steps, relative, y):
        place_of = 0
        for axis, bit in steps:
            place_of = 2 * place_of + (y if axis == "pb" else relative // bit % 2)
        return place_of

    def pack(r, grad, region, offset):
        base, steps, size = region
        index, here = lax.axis_index("pb"), lax.axis_index("ba")
        for relative in range(ba_size):
            for y in range(two):
                first = base + row_place(steps, relative, y) * size + offset
                for c, target in ((0, r.keep), (1, r.send)):
                    source = pl.multiple_of((here ^ relative) * block, 8)
                    column = pl.multiple_of((index ^ (2 * y + c)) * lanes, 128)
                    target[first : first + block, :] = grad[pl.ds(source, block), pl.ds(column, lanes)].astype(BF16)

    later = [("pb", 2)] + [("ba", bit) for bit in ba_bits[2:]]
    copies = ba_size * two
    cross_size = 4 * block
    embed_rows = slot // 2
    self_size = 4 * block + embed_rows
    self_region = (0, [("ba", ba_bits[0]), ("ba", ba_bits[1])] + later, self_size)
    cross_region = (copies * self_size, [("ba", ba_bits[1]), ("ba", ba_bits[0])] + later, cross_size)
    vector_count = 13 * width + hidden
    extra = padded_to(vector_count // 128, 16)
    cut = part // 48 * 16
    packed = (copies * (self_size + cross_size) + extra, lanes)

    def attend_back(queries, grads, keys, values, kept, inverse, scores, logits, results, grad_keys, grad_values, finished=None):
        parts = {}
        spreads = {}

        def first(n, i, g):
            cols = slice(g * wide, (g + 1) * wide)
            back = inverse[i, 0:1, g * many : (g + 1) * many]
            upright = jnp.broadcast_to(back, (128, many)).T
            lane = lax.broadcasted_iota(jnp.int32, (1, wide), 1) // head
            piece = grads(i)[:, cols].astype(F32)
            spreads[n] = jnp.concatenate(
                [
                    (piece * upright[h * rows : (h + 1) * rows, 0:1]).astype(BF16)
                    * (lane == h).astype(F32).astype(BF16)
                    for h in range(GROUP_HEADS)
                ],
                axis=0,
            )
            scores[n % 2][...] = nt(values(i, cols), spreads[n])

        def second(n, i, g):
            cols = slice(g * wide, (g + 1) * wide)
            big = slice(g * many, (g + 1) * many)
            score, logit = scores[n % 2], logits[n % 2]
            back = inverse[i, 0:1, big]
            inner = jnp.sum(kept[i, :, big].astype(F32) * score[...], axis=0, keepdims=True)
            logit[...] = (kept[i, :, big].astype(F32) * (score[...] - inner * back)).astype(BF16)
            grad_values(i, cols, nn(kept[i, :, big], spreads[n]))
            grad_keys(i, cols, nn(logit[...], spread_heads(queries(i)[:, cols], head)))
            parts[g] = diagonal(tn(keys(i, cols), logit[...]), head, rows)
            if g == groups - 1:
                whole = jnp.concatenate([parts[j] for j in range(groups)], axis=0)
                results[i * rows : (i + 1) * rows, :] = (whole.T * scale).astype(BF16)
                if finished:
                    finished(i)

        staggered([(i, g) for i in range(own) for g in range(groups)], first, second)

    def cross_back(r):
        grad = r.dr3[...] + nt(r.dh[...], r.we[...])
        sums = r.sums
        sums[...] = jnp.zeros(sums.shape, F32)
        unit = r.unit2[...]
        sums[0:1, :] = column_sum(grad * unit)
        sums[1:2, :] = column_sum(grad)
        dr2 = norm_backward(grad, unit, r.spread2[...], vector(r, G2))
        r.put(dr2=dr2)
        branch = dr2.astype(BF16)
        sums[2:3, :] = column_sum(branch)
        r.put(ds2=branch)
        r.do2[...] = nt(branch, r.wco[...]).astype(BF16)
        def grad_keys(i, cols, value):
            r.dk[i, :, cols] = value.astype(BF16)

        def grad_values(i, cols, value):
            r.dv[i, :, cols] = value.astype(BF16)

        index = lax.axis_index("pb")
        def memory_back(i):
            r.put_part(i, dk=None, dv=None)
            for k in range(group - 1, -1, -1):
                edge = pl.ds(pl.multiple_of((index ^ k) * part, 16), part)
                value = (nt(r.dk[i, edge, :], r.wck[...]) + nt(r.dv[i, edge, :], r.wcv[...])).astype(BF16)
                if k < 2:
                    r.near[k][i] = value
                elif k == 3:
                    r.far_big[i * part : (i + 1) * part, :] = value
                elif i < own - 1:
                    r.far_small[i * part : (i + 1) * part, :] = value
                else:
                    r.far_small[i * part : i * part + cut, :] = value[:cut]
                    r.far_third[...] = value[cut:]
                if i == own - 1:
                    if k == 3:
                        r.put(far_big=None)
                    elif k == 2:
                        r.put(far_small=None, far_third=None)
                    else:
                        r.put(near=k)

        attend_back(
            lambda i: r.q2[i * rows : (i + 1) * rows, :],
            lambda i: r.do2[i * rows : (i + 1) * rows, :],
            lambda i, cols: r.keys[i, :, cols],
            lambda i, cols: r.values[i, :, cols],
            r.e2,
            r.inv2,
            (r.scores, r.scores_two),
            (r.logit, r.logit_two),
            r.dq,
            grad_keys,
            grad_values,
            memory_back,
        )
        r.put(dq=None)
        sums[3:4, :] = column_sum(r.dq[...])
        total = jnp.zeros((1, width), F32)
        for i in range(own):
            total = total + column_sum(r.dv[i])
        sums[4:5, :] = total
        r.put(sums=None)
        r.put(dc=nt(r.dq[...], r.wcq[...]))

    act_got = swap(fw.act[1], "pb", 1)
    x2b_got = swap(fw.x2b, "pb", 1)
    df_got = swap(fw.df, "pb", 1)
    dh_got = swap(fw.dh_t[1], "pb", 1)
    back = run(
        cross_back,
        dict(
            vectors=(vectors, VM),
            dh=(fw.dh, DMA),
            we=(expand_weight, DMA),
            dr3=(fw.dr3, DMA),
            unit2=(fw.unit2, DMA),
            spread2=(fw.spread2, DMA),
            wco=(cross_out, DMA),
            values=(memory_values, DMA),
            inv2=(fw.inv2, DMA),
            e2=(fw.e2, DMA),
            q2=(fw.q2, DMA),
            keys=(memory_keys, DMA),
            wck=(cross_key, DMA),
            wcv=(cross_value, DMA),
            wcq=(cross_query, DMA),
        ),
        dict(
            near=([(own, part, width)] * 2, BF16, DMA),
            far_big=((own * part, width), BF16, DMA),
            far_small=(((own - 1) * part + cut, width), BF16, DMA),
            far_third=((part - cut, width), BF16, DMA),
            dq=((all_rows, width), BF16, DMA),
            dc=((all_rows, width), F32, DMA),
            dk=((own, span, width), BF16, DMA),
            dv=((own, span, width), BF16, DMA),
            dr2=((all_rows, width), F32, DMA),
            ds2=((all_rows, width), BF16, DMA),
            sums=((8, width), F32, DMA),
        ),
        dict(do2=((all_rows, width), BF16), scores=((span, many), F32), scores_two=((span, many), F32), logit=((span, many), BF16), logit_two=((span, many), BF16)),
        microseconds=20.0,
        most=63 * 2**20 + 2**19,
    )


    def cross_weights(r):
        grad = r.grad
        grad[...] = tn(r.o2[...], r.ds2[...])
        pack(r, grad, cross_region, 3 * block)
        grad[...] = tn(r.c_in[...], r.cross_dq[...])
        pack(r, grad, cross_region, 0 * block)
        grad[...] = tn(r.plain[0], r.cross_dv[0])
        for i in range(1, own):
            grad[...] += tn(r.plain[i], r.cross_dv[i])
        pack(r, grad, cross_region, 2 * block)
        grad[...] = tn(r.keyed[0], r.cross_dk[0])
        for i in range(1, own):
            grad[...] += tn(r.keyed[i], r.cross_dk[i])
        pack(r, grad, cross_region, 1 * block)

    def rest_back(r):
        grad = r.dr2[...] + r.dc[...]
        sums = r.sums
        sums[...] = jnp.zeros(sums.shape, F32)
        unit = r.unit1[...]
        sums[0:1, :] = column_sum(grad * unit)
        sums[1:2, :] = column_sum(grad)
        first = r.first
        first[...] = norm_backward(grad, unit, r.spread1[...], vector(r, G1))
        branch = first[...].astype(BF16)
        sums[2:3, :] = column_sum(branch)
        whole = r.grad
        whole[...] = tn(r.o1[...], branch)
        pack(r, whole, self_region, 3 * block)
        r.do1[...] = nt(branch, r.wo[...]).astype(BF16)
        def grad_keys(i, cols, value):
            r.dk[i * rows : (i + 1) * rows, cols] = value.astype(BF16)

        def grad_values(i, cols, value):
            r.dv[i * rows : (i + 1) * rows, cols] = value.astype(BF16)

        attend_back(
            lambda i: r.q1[i * rows : (i + 1) * rows, :],
            lambda i: r.do1[i * rows : (i + 1) * rows, :],
            lambda i, cols: r.k1[i * rows : (i + 1) * rows, cols],
            lambda i, cols: r.v1[i * rows : (i + 1) * rows, cols],
            r.e1,
            r.inv1,
            (r.scores, r.scores_two),
            (r.logit, r.logit_two),
            r.dq,
            grad_keys,
            grad_values,
        )
        dq, dk, dv = r.dq[...], r.dk[...], r.dv[...]
        sums[3:4, :] = column_sum(dq)
        sums[4:5, :] = column_sum(dv)
        both = nt(dq, r.wq[...]) + nt(dk, r.wk[...])
        low = (first[...] + both + nt(dv, r.wv[...])).astype(BF16)
        for k in range(group):
            for i in range(own):
                (r.near[k] if k < 2 else r.far.at[k - 2])[i] = low[i * rows + k * slot : i * rows + (k + 1) * slot, :]
        for j in range(2):
            r.near[j][own:] = r.out_near[j][...]
            r.far[j, own:] = r.out_far[j]
        r.put(near=0)
        r.put(near=1)
        r.put(far=None)
        both = both + r.dc[...]
        embed = both[0:rows]
        for i in range(1, own):
            embed = embed + both[i * rows : (i + 1) * rows]
        embed = nn(embed.astype(BF16), permutation(project_order, width, ba_size)).astype(BF16)
        order_bits = project_order
        for position in range(ba_size):
            relative = sum(((position >> (len(order_bits) - 1 - b)) & 1) * bit for b, bit in enumerate(order_bits))
            for y in range(two):
                first = row_place(self_region[1], relative, y) * self_size + 4 * block
                for c, target in ((0, r.keep), (1, r.send)):
                    k = 2 * y + c
                    piece = embed[k * slot : (k + 1) * slot, position * block : (position + 1) * block]
                    gap = [jnp.zeros((embed_rows, lanes // 2 - block), BF16)] if block < lanes // 2 else []
                    filled = jnp.concatenate([piece[:embed_rows]] + gap + [piece[embed_rows:]] + gap, axis=1)
                    target[first : first + embed_rows, :] = filled
        table_rows = r.rows
        table_rows[...] = jnp.zeros(table_rows.shape, F32)
        sources = [
            (sums, 3),
            (sums, 4),
            (sums, 2),
            (sums, 0),
            (sums, 1),
            (r.sums_s, 3),
            (r.sums_s, 4),
            (r.sums_s, 2),
            (r.sums_s, 0),
            (r.sums_s, 1),
            (r.sums_f, 2),
            (r.sums_f, 0),
            (r.sums_f, 1),
        ] + [(r.hidden_sum, None)]
        filled_rows = 0
        for source, place_of in sources:
            place_of = place_of or 0
            for j in range(source.shape[1] // 128):
                table_rows[filled_rows : filled_rows + 1, :] = source[place_of : place_of + 1, j * 128 : (j + 1) * 128]
                filled_rows += 1
        low_rows = table_rows[...].astype(BF16)
        r.keep[packed[0] - extra :, :] = low_rows
        r.send[packed[0] - extra :, :] = low_rows
        for matrix, left, right in ((0, r.a_in, dq), (1, r.a_in, dk), (2, r.x0, dv)):
            whole[...] = tn(left[...], right)
            pack(r, whole, self_region, matrix * block)
        edge = copies * self_size
        tail = packed[0] - extra
        for rows_first, rows_count in ((0, edge), (tail, extra)):
            r.put_rows("send", rows_first, rows_count)
            r.put_rows("keep", rows_first, rows_count)
        cross_weights(r)
        r.put_rows("send", edge, tail - edge)
        r.put_rows("keep", edge, tail - edge)

    act_got, x2b_got, df_got, dh_got, hidden_start = meet(act_got, x2b_got, df_got, dh_got, back.ds2)

    def hidden_grads(r):
        r.perm[...] = permutation(project_order, width, ba_size)
        tile = width // 4

        def columns(rows, swapped):
            value = nn(rows, r.perm[...]).astype(BF16)
            tiles = [value[:, t * tile : (t + 1) * tile] for t in ((0, 2, 1, 3) if swapped else range(4))]
            return jnp.concatenate(tiles, axis=1)

        def one(swapped, keep, got, rows_own, rows_got, kept, sent, done):
            own_cols = columns(rows_own(), swapped)
            got_cols = columns(rows_got(), swapped)
            for y in range(two):
                total = nn(keep()[y], own_cols) + nn(got()[y], got_cols)
                kept[y] = total[:, :half].astype(BF16)
                sent[y] = total[:, half:].astype(BF16)
                done(y)

        one(
            False,
            lambda: r.act_keep,
            lambda: r.act_got,
            lambda: r.df[...],
            lambda: r.df_got[...],
            r.p_keep,
            r.p_send,
            lambda y: r.put_part(y, p_send=None, p_keep=None),
        )
        one(
            True,
            lambda: r.dh_keep,
            lambda: r.dh_got,
            lambda: r.x2b[...],
            lambda: r.x2b_got[...],
            r.e_keep,
            r.e_send,
            lambda y: r.put_part(y, e_send=None, e_keep=None),
        )

    piece = ((two, share, half), BF16, DMA)
    hid = run(
        hidden_grads,
        dict(
            df=(tie(fw.df, hidden_start), DMA),
            df_got=(df_got, DMA),
            act_keep=(fw.act[0], DMA),
            act_got=(act_got, DMA),
            x2b=(fw.x2b, DMA),
            x2b_got=(x2b_got, DMA),
            dh_keep=(fw.dh_t[0], DMA),
            dh_got=(dh_got, DMA),
        ),
        dict(p_keep=piece, p_send=piece, e_keep=piece, e_send=piece),
        dict(perm=((width, width), BF16)),
        microseconds=4.0,
    )

    p_send, e_send, far_big, mem_near = meet(hid.p_send, hid.e_send, back.far_big, back.near[1])

    p_got = swap(p_send, "ba", ba_bits[0])
    e_got = swap(e_send, "ba", ba_bits[1])
    big_got = swap(far_big, "pb", 2)
    mem_other = swap(mem_near, "pb", 1)
    slf = run(
        rest_back,
        dict(
            vectors=(vectors, VM),
            dr2=(tie(back.dr2, p_send, e_send), DMA),
            dc=(back.dc, DMA),
            unit1=(fw.unit1, DMA),
            spread1=(fw.spread1, DMA),
            o1=(fw.o1, DMA),
            wo=(self_out, DMA),
            inv1=(fw.inv1, DMA),
            e1=(fw.e1, DMA),
            q1=(fw.q1, DMA),
            k1=(fw.k1, DMA),
            v1=(fw.v1, DMA),
            wq=(self_query, DMA),
            wk=(self_key, DMA),
            wv=(self_value, DMA),
            a_in=(fw.a_in, DMA),
            x0=(fw.x0, DMA),
            out_near=(fw.near, DMA),
            out_far=(fw.far, DMA),
            o2=(fw.o2, DMA),
            ds2=(back.ds2, DMA),
            c_in=(fw.c_in, DMA),
            cross_dq=(back.dq, DMA),
            cross_dv=(back.dv, DMA),
            plain=(plain, DMA),
            cross_dk=(back.dk, DMA),
            keyed=(keyed, DMA),
            sums_s=(back.sums, DMA),
            sums_f=(fw.sums, DMA),
            hidden_sum=(fw.hidden_sum, DMA),
        ),
        dict(
            keep=(packed, BF16, DMA),
            send=(packed, BF16, DMA),
            near=([(2 * own, slot, width)] * 2, BF16, DMA),
            far=((2, 2 * own, slot, width), BF16, DMA),
        ),
        dict(
            sums=((8, width), F32),
            rows=((extra, 128), F32),
            first=((all_rows, width), F32),
            grad=((width, width), F32),
            do1=((all_rows, width), BF16),
            dq=((all_rows, width), BF16),
            dk=((all_rows, width), BF16),
            dv=((all_rows, width), BF16),
            scores=((rows, many), F32),
            scores_two=((rows, many), F32),
            logit=((rows, many), BF16),
            logit_two=((rows, many), BF16),
        ),
        microseconds=7.0,
    )
    p_got, e_got, big_got, mem_other, send, far_small = meet(
        p_got, e_got, big_got, mem_other, slf.send, back.far_small
    )

    p_keep, p_send = halves(pair_sum(hid.p_keep, p_got), -1)
    e_keep, e_send = halves(pair_sum(hid.e_keep, e_got), -1)
    p_got = swap(p_send, "ba", ba_bits[1])
    e_got = swap(e_send, "ba", ba_bits[0])
    got = swap(send, "pb", 1)
    small_got = swap(far_small, "pb", 2)
    last = swap(big_got, "pb", 1)
    p_got, e_got, got, last, small_got, far_third = meet(p_got, e_got, got, last, small_got, back.far_third)

    edge = copies * self_size
    a_keep, a_send = sum_halves(slf.keep, got, 0, edge, extra)
    b_keep, b_send = sum_halves(slf.keep, got, edge, packed[0] - extra, 0)
    p_total, e_total = pair_sum(p_keep, p_got), pair_sum(e_keep, e_got)
    f_keep, f_send = (jnp.stack([p_total[y], e_total[y]]).astype(BF16) for y in range(two))
    a_got = swap(a_send, "ba", ba_bits[0])
    b_got = swap(b_send, "ba", ba_bits[1])
    f_got = swap(f_send, "pb", 2)
    third_got = swap(far_third, "pb", 2)
    a_got, b_got, f_got, third_got, home_near, home_far = meet(
        a_got, b_got, f_got, third_got, slf.near[1], slf.far
    )

    f_total = pair_sum(f_keep, f_got)
    f_half = f_total.shape[-1] // 2
    f_keep, f_send = (
        jnp.concatenate(
            [f_total[0, :, j * f_half : (j + 1) * f_half], f_total[1, :, j * f_half : (j + 1) * f_half]], axis=-1
        ).astype(BF16)
        for j in range(2)
    )
    a_keep, a_send = sum_halves(a_keep, a_got, 0, a_keep.shape[0] - extra, extra)
    b_keep, b_send = sum_halves(b_keep, b_got, 0, b_keep.shape[0], 0)
    a_got = swap(a_send, "ba", ba_bits[1])
    b_got = swap(b_send, "ba", ba_bits[0])
    home_other = swap(home_near, "pb", 1)
    home_across = swap(home_far, "pb", 2)

    def place_memory(r):
        index = lax.axis_index("pb")
        for i in range(own):
            last = r.last[i * part : i * part + quarter, :]
            if i < own - 1:
                across = r.across[i * part : i * part + quarter, :]
            else:
                across = jnp.concatenate(
                    [r.across[i * part : i * part + cut, :], r.third[0 : quarter - cut, :]], axis=0
                )
            for k, piece in enumerate((r.mine[i, 0:quarter, :], r.other[i, 0:quarter, :], across, last)):
                r.wide[:, (index ^ k) * own + i, :] = piece.astype(F32)
        r.put(whole=r.wide[...].astype(BF16))

    memory_grad = run(
        place_memory,
        dict(
            mine=(tie(back.near[0], f_send, a_send, b_send), DMA),
            other=(mem_other, DMA),
            across=(small_got, DMA),
            third=(third_got, DMA),
            last=(last, DMA),
        ),
        dict(whole=((quarter, items, width), BF16, DMA)),
        dict(wide=((quarter, items, width), F32)),
        microseconds=4.0,
        spare=4,
    ).whole
    f_send, a_got, b_got, home_other, home_across, memory_grad = meet(
        f_send, a_got, b_got, home_other, home_across, memory_grad
    )

    keep, send = row_halves(
        interleave(pair_sum(a_keep, a_got), pair_sum(b_keep, b_got), self_size, cross_size, extra), extra
    )
    got = swap(send, "pb", 2)
    f_got = swap(f_send, "ba", ba_bits[2])
    home_last = swap(home_across[1], "pb", 1)
    got, f_got, home_last = meet(got, f_got, home_last)

    keep, send = row_halves(pair_sum(keep, got), extra)
    got = swap(send, "ba", ba_bits[2])
    hidden_out = pair_sum(f_keep, f_got)
    project_out, expand_out = (
        finish(part_out, ba_bits[3:], lambda total: halves(total, -1))
        for part_out in (hidden_out[:, :f_half], hidden_out[:, f_half:])
    )
    expand_out = expand_out.T

    def place_rows(r):
        index = lax.axis_index("pb")
        for i in range(own):
            for k in range(group):
                source = (r.mine, r.other, r.across.at[0], r.last)[k]
                r.wide[:, (index ^ k) * own + i, :] = source[i, 0:chunk, :].astype(F32)
                r.wide_out[:, (index ^ k) * own + i, :] = source[own + i, 0:chunk, :].astype(F32)
        r.put(grad=r.wide[...].astype(BF16))
        r.put(out=r.wide_out[...].astype(BF16))

    wide_rows = (chunk, items, width)
    rows_home = run(
        place_rows,
        dict(
            mine=(tie(slf.near[0], send), DMA),
            other=(home_other, DMA),
            across=(home_across, DMA),
            last=(home_last, DMA),
        ),
        dict(grad=(wide_rows, BF16, DMA), out=(wide_rows, BF16, DMA)),
        dict(wide=(wide_rows, F32), wide_out=(wide_rows, F32)),
        microseconds=2.0,
        spare=4,
    )
    input_grad, layer_output = rows_home.grad, rows_home.out
    addends = [keep, got]
    if len(ba_bits) > 3:
        addends = [finish(pair_sum(keep, got), ba_bits[3:], lambda total: row_halves(total, extra))]
    places = [m * block for m in range(4)] + [self_size + m * block for m in range(4)]
    vector_rows = [width // 128] * 13 + [hidden // 128]

    def spread_out(r):
        total = r.addends[0][...].astype(F32)
        for j in range(1, len(addends)):
            total = total + r.addends[j][...].astype(F32)
        r.total[...] = total
        for m, first in enumerate(places):
            r.squares[m][...] = r.total[first : first + block, :]
        for j in range(2):
            count = min(embed_rows, chunk - j * embed_rows)
            left = j * lanes // 2
            r.embed[j * embed_rows : j * embed_rows + count, :] = r.total[
                4 * block : 4 * block + count, left : left + block
            ]
        first = addends[0].shape[0] - extra
        for j, count in enumerate(vector_rows):
            r.vectors[j][...] = r.total[first : first + count, :]
            first += count

    ends = run(
        spread_out,
        dict(addends=(addends, VM)),
        dict(
            squares=([(block, lanes)] * 8, F32, VM),
            embed=((chunk, block), F32, VM),
            vectors=([(count, 128) for count in vector_rows], F32, VM),
        ),
        dict(total=(addends[0].shape, F32)),
        microseconds=1.0,
        spare=4,
    )
    input_grad, layer_output = input_grad.transpose(1, 0, 2), layer_output.transpose(1, 0, 2)
    memory_grad = memory_grad.transpose(1, 0, 2)
    squares, vecs = ends.squares, [vector_out.reshape(-1) for vector_out in ends.vectors]

    return (
        layer_output,
        input_grad,
        memory_grad,
        ends.embed,
        squares[0],
        vecs[0],
        squares[1],
        squares[2],
        vecs[1],
        squares[3],
        vecs[2],
        vecs[3],
        vecs[4],
        squares[4],
        vecs[5],
        squares[5],
        squares[6],
        vecs[6],
        squares[7],
        vecs[7],
        vecs[8],
        vecs[9],
        expand_out,
        vecs[13],
        project_out,
        vecs[10],
        vecs[11],
        vecs[12],
    )


def solution(mesh):
    rows = P("ba", "pb", None)
    copied = P()
    placed = (rows, P("ba", None, None), P("ba"), P("pb", None)) + (copied,) * 24 + (rows,)
    square = P("ba", "pb")
    return jax.shard_map(
        local,
        mesh=mesh,
        in_specs=placed,
        out_specs=(
            rows,
            rows,
            rows,
            P("pb", "ba"),
            square,
            copied,
            square,
            square,
            copied,
            square,
            copied,
            copied,
            copied,
            square,
            copied,
            square,
            square,
            copied,
            square,
            copied,
            copied,
            copied,
            square,
            copied,
            P("pb", "ba"),
            copied,
            copied,
            copied,
        ),
        check_vma=False,
    )
```
